32 devices in a mesh: resp: 8 (over y, x, core), mp: 4 (over z).
Axes of the slice: x: 2, y: 2, z: 4, core: 2. Of those that a mesh axis runs over, the one named last changes fastest.
Arguments:
- queries: bfloat16 [8, 512, 4096], P('resp', None, 'mp'), may hold values from -160 to 160
- keys: bfloat16 [8, 512, 512], P('resp'), may hold values from -8 to 8
- values: bfloat16 [8, 512, 512], P('resp'), may hold values from -6 to 6
- out_weight: bfloat16 [4096, 8192], P(None, 'mp'), may hold values from -1.5 to 1.5
- order_bias: float32 [2, 32], replicated, may hold values from -2 to 2
- partners: int32 [8, 6], P('resp'), may hold values from -1 to 7, as said below
- count: int32 [8], P('resp'), may hold values from 1 to 6, as said below
- order: int32 [8, 6], P('resp'), may hold values 0 or 1
Outputs:
- judged: bfloat16 [8, 512, 8192], P('resp', None, 'mp')
The draws below stay inside these ranges and needn't reach their ends.
Inputs may be any that keep to these rules, and one draw needn't show every extreme that they name: `partners`: slot s of response r is used iff s < count[r]; unused slots hold -1; a used entry names a response other than r at cyclic distance at most 3; the used entries of a row are distinct. `count`: some response has 6 partners and some other has 1.
All inputs are finite; a program needn't handle non-finite values. No bound on the sum of `order` on one device may be relied on, other than what follows from the above.
Results may differ from the reference program's by a relative error of at most 0.0057.
Values may be sent and summed in bfloat16 or wider, within the bound.
No kernel may reach another device: no remote copies, remote signals or barrier semaphores. Data moves between devices by JAX's collectives and lax.ppermute only.
A program may use at most 128 MiB of HBM per device.

```python
import math
import jax
import jax.numpy as jnp
from jax import lax

D = 8192
HQ = 32
KVH = 4
HD = 128
LEN = 512
REACH = 3
SLOTS = 6
RESPONSES = 8


def links(key):
    base_key = jax.random.fold_in(key, 7)
    key_count, key_full, key_sparse, key_perm = jax.random.split(base_key, 4)
    counts = jax.random.randint(key_count, (RESPONSES,), 1, SLOTS + 1)
    fullest = jax.random.randint(key_full, (), 0, RESPONSES)
    sparsest = (fullest + 1 + jax.random.randint(key_sparse, (), 0, RESPONSES - 1)) % RESPONSES
    counts = counts.at[fullest].set(SLOTS).at[sparsest].set(1)
    offsets = jnp.concatenate([jnp.arange(1, REACH + 1), -jnp.arange(1, REACH + 1)]).astype(jnp.int32)
    row_keys = jax.random.split(key_perm, RESPONSES)
    shuffled = jax.vmap(lambda row_key: jax.random.permutation(row_key, offsets))(row_keys)
    row_ids = jnp.arange(RESPONSES, dtype=jnp.int32)[:, None]
    targets = (row_ids + shuffled) % RESPONSES
    in_use = jnp.arange(SLOTS, dtype=jnp.int32)[None, :] < counts[:, None]
    partner_ids = jnp.where(in_use, targets, -1)
    return (partner_ids.astype(jnp.int32), counts.astype(jnp.int32))


def draw_partners(key, part):
    return links(key)[0]


def draw_count(key, part):
    return links(key)[1]


def features(key):
    base_key = jax.random.fold_in(key, 3)
    key_query, key_key = jax.random.split(base_key)
    query_rows = jnp.clip(jax.random.normal(key_query, (RESPONSES, LEN, HQ * HD), jnp.float32), -6.0, 6.0)
    key_rows = jnp.clip(jax.random.normal(key_key, (RESPONSES, LEN, KVH * HD), jnp.float32), -6.0, 6.0)
    return (query_rows, key_rows)


def draw_queries(key, part):
    return features(key)[0].astype(jnp.bfloat16)


def draw_keys(key, part):
    return features(key)[1].astype(jnp.bfloat16)


def set_ends(result, own_key, low, top_value):
    place = [jax.random.randint(jax.random.fold_in(own_key, axis), (), 0, length) for axis, length in enumerate(result.shape)]
    longest = result.shape.index(max(result.shape))
    beside = place[:longest] + [(place[longest] + 1) % result.shape[longest]] + place[longest + 1:]
    return result.at[tuple(place)].set(low).at[tuple(beside)].set(top_value)


def level_of(own_key, dims, cuts, least, largest):
    gain, own = 1.0, jax.random.fold_in(own_key, 6)
    for dim, blocks in cuts:
        heights = jnp.exp(jax.random.uniform(jax.random.fold_in(own, dim), (blocks,), jnp.float32, least / len(cuts), largest / len(cuts)))
        gain = gain * jnp.repeat(heights, dims[dim] // blocks).reshape([-1 if axis == dim else 1 for axis in range(len(dims))])
    return gain


def gaussian(rng, shape, deviation, reach, cuts=(), kind=jnp.bfloat16):
    values = deviation * jax.random.normal(rng, shape, jnp.float32)
    if cuts:
        values = values * level_of(rng, shape, cuts, -0.22, 0.18)
    return jnp.clip(values, -reach, reach).astype(kind)


def setup_inputs(seed: int = 0) -> dict:
    seeds = jax.random.split(jax.random.key(seed), 9)
    queries = draw_queries(jax.random.fold_in(seeds[8], 71), 0)
    keys = draw_keys(jax.random.fold_in(seeds[8], 71), 0)
    values = gaussian(seeds[2], (RESPONSES, LEN, KVH * HD), 1.0, 6.0, ((0, 8),))
    out_weight = gaussian(seeds[3], (HQ * HD, D), (HD // 8) ** -0.5, 1.5, ((1, 4),))
    order_bias = jnp.clip(jax.random.uniform(seeds[4], (2, HQ), jnp.float32, -2.0, 2.0), -2.0, 2.0)
    partners = draw_partners(jax.random.fold_in(seeds[8], 71), 0)
    count = draw_count(jax.random.fold_in(seeds[8], 71), 0)
    order = set_ends((jax.random.randint(seeds[7], (RESPONSES, SLOTS), 0, 2) < 1).astype(jnp.int32), jax.random.fold_in(seeds[7], 1), 0, 1)
    return {"queries": queries, "keys": keys, "values": values, "out_weight": out_weight, "order_bias": order_bias, "partners": partners, "count": count, "order": order}


def reference(queries, keys, values, out_weight, order_bias, partners, count, order):
    group_size = HQ // KVH
    score_scale = 1.0 / math.sqrt(HD)
    slot_ids = jnp.arange(SLOTS, dtype=jnp.int32)
    causal = jnp.arange(LEN)[:, None] >= jnp.arange(LEN)[None, :]

    def one_response(resp_id):
        query_rows = queries[resp_id].reshape(LEN, HQ, HD).astype(jnp.float32)
        picked = jnp.maximum(partners[resp_id], 0).astype(jnp.int32)
        in_use = slot_ids < count[resp_id]
        key_rows = jnp.concatenate([keys[resp_id][None], keys[picked]], 0).reshape(SLOTS + 1, LEN, KVH, HD)
        value_rows = jnp.concatenate([values[resp_id][None], values[picked]], 0).reshape(SLOTS + 1, LEN, KVH, HD)
        key_rows = jnp.repeat(key_rows, group_size, axis=2).astype(jnp.float32)
        value_rows = jnp.repeat(value_rows, group_size, axis=2).astype(jnp.float32)
        scores = jnp.einsum('ihd,sjhd->hisj', query_rows, key_rows) * score_scale
        slot_bias = order_bias[order[resp_id]]
        bias_all = jnp.concatenate([jnp.zeros((1, HQ), jnp.float32), slot_bias], 0).T
        scores = scores + bias_all[:, None, :, None]
        partner_seen = jnp.broadcast_to(in_use[None, :, None], (LEN, SLOTS, LEN))
        visible = jnp.concatenate([causal[:, None, :], partner_seen], 1)
        scores = jnp.where(visible[None], scores, -jnp.inf)
        highest = lax.optimization_barrier(jnp.max(scores, axis=(2, 3), keepdims=True))
        expo = jnp.exp(scores - highest)
        weights = (expo / lax.optimization_barrier(jnp.sum(expo, axis=(2, 3), keepdims=True))).astype(jnp.bfloat16)
        attended = jnp.einsum('hisj,sjhd->ihd', weights.astype(jnp.float32), value_rows).astype(jnp.bfloat16)
        attended = attended.reshape(LEN, HQ * HD)
        return jnp.dot(attended, out_weight, preferred_element_type=jnp.float32).astype(jnp.bfloat16)
    return lax.map(one_response, jnp.arange(RESPONSES, dtype=jnp.int32))
```

```python
import functools
import math

import jax
import jax.numpy as jnp
from jax import lax
from jax.experimental import pallas as pl
from jax.experimental.pallas import tpu as pltpu
from jax.sharding import PartitionSpec as P

HQ = 32
KVH = 4
HD = 128
REACH = 3
SLOTS = 6
OFFSETS = tuple(range(1, REACH + 1)) + tuple(-hop for hop in range(1, REACH + 1))
BLOCKS = 1 + len(OFFSETS)
LOG2E = math.log2(math.e)


def shifted(value, axis, steps):
    count = lax.axis_size(axis)
    pairs = [(source, (source + steps) % count) for source in range(count)]
    return lax.ppermute(value, axis, pairs)


def attention_kernel(
    head_base, resp_total, where_ref, partners_ref, count_ref, order_ref, bias_ref, q_ref, *rest
):
    kv_refs = rest[:BLOCKS]
    out_ref = rest[BLOCKS]
    scores_ref, ones_ref = rest[BLOCKS + 1 :]
    rows = q_ref.shape[1]
    seq_len = kv_refs[0].shape[1]
    head_step, row_step = pl.program_id(0), pl.program_id(1)
    resp_self = where_ref[0]
    head = where_ref[1] + head_base + head_step
    scale = LOG2E / math.sqrt(HD)

    @pl.when((head_step == 0) & (row_step == 0))
    def _():
        ones_ref[...] = jnp.ones_like(ones_ref)

    offsets_bias = [jnp.float32(0.0)]
    for offset in OFFSETS:
        target = lax.rem(resp_self + offset + resp_total, resp_total)
        found = jnp.float32(-jnp.inf)
        for slot in range(SLOTS):
            hit = (slot < count_ref[0]) & (partners_ref[0, slot] == target)
            found = jnp.where(hit, bias_ref[order_ref[0, slot], head] * LOG2E, found)
        offsets_bias.append(found)

    query = q_ref[0]
    highest = None
    for block in range(BLOCKS):
        scores = lax.dot_general(
            query, kv_refs[block][0], (((1,), (1,)), ((), ())), preferred_element_type=jnp.float32
        )
        if block == 0:
            row_ids = lax.broadcasted_iota(jnp.int32, scores.shape, 0) + row_step * rows
            col_ids = lax.broadcasted_iota(jnp.int32, scores.shape, 1)
            scores = jnp.where(row_ids >= col_ids, scores, -jnp.inf)
        scores_ref[:, block * seq_len : (block + 1) * seq_len] = scores
        part = scores[:, :HD]
        for lane in range(HD, seq_len, HD):
            part = jnp.maximum(part, scores[:, lane : lane + HD])
        part = part * scale + offsets_bias[block]
        highest = part if highest is None else jnp.maximum(highest, part)
    highest = jnp.max(highest, axis=1, keepdims=True)
    total = jnp.zeros((rows, 2 * HD), jnp.float32)
    for block in range(BLOCKS):
        scores = scores_ref[:, block * seq_len : (block + 1) * seq_len]
        expo = jnp.exp2(scores * scale + (offsets_bias[block] - highest)).astype(jnp.bfloat16)
        wide = jnp.concatenate([kv_refs[block][1], ones_ref[...]], axis=1)
        total = total + jnp.dot(expo, wide, preferred_element_type=jnp.float32)
    out_ref[...] = (total[:, :HD] / total[:, HD:]).astype(out_ref.dtype)


def attention(where, partners, count, order, order_bias, queries, kv_blocks, head_base, heads, resp_total):
    seq_len = queries.shape[1]
    rows = min(seq_len, 256)
    smem = pl.BlockSpec(memory_space=pltpu.SMEM)
    whole = pl.BlockSpec(kv_blocks[0].shape, lambda head, row: (0, 0, 0))
    keys_all = BLOCKS * seq_len
    return pl.pallas_call(
        functools.partial(attention_kernel, head_base, resp_total),
        grid=(heads, seq_len // rows),
        in_specs=[smem] * 5
        + [pl.BlockSpec((1, rows, HD), lambda head, row: (0, row, head_base + head))]
        + [whole] * BLOCKS,
        out_specs=pl.BlockSpec((rows, HD), lambda head, row: (row, head)),
        out_shape=jax.ShapeDtypeStruct((seq_len, heads * HD), jnp.bfloat16),
        scratch_shapes=[
            pltpu.VMEM((rows, keys_all), jnp.float32),
            pltpu.VMEM((seq_len, HD), jnp.bfloat16),
        ],
        compiler_params=pltpu.CompilerParams(vmem_limit_bytes=40 * 1024 * 1024),
        cost_estimate=pl.CostEstimate(
            flops=heads * seq_len * keys_all * HD * 6,
            bytes_accessed=2 * seq_len * HD * (2 * heads + 2 * BLOCKS),
            transcendentals=heads * seq_len * keys_all,
        ),
        name="attend",
    )(where, partners, count, order, order_bias, queries, *kv_blocks)


def project_kernel(chunks, start, final, *refs):
    part_refs = refs[:chunks]
    weight_ref = refs[chunks]
    out_ref = refs[-1]
    total = None if start else refs[chunks + 1][...]
    for source in range(part_refs[0].shape[0]):
        for chunk in range(chunks):
            term = jnp.dot(
                part_refs[chunk][source], weight_ref[source, chunk], preferred_element_type=jnp.float32
            )
            total = term if total is None else total + term
    out_ref[...] = total.astype(out_ref.dtype)[None] if final else total


def project(total, parts, first_chunk, weight, final):
    sources, seq_len, width = parts[0].shape
    chunks = len(parts)
    out_width = weight.shape[3]
    step = min(out_width, 512)
    specs = [pl.BlockSpec((sources, seq_len, width), lambda col: (0, 0, 0))] * chunks
    specs.append(
        pl.BlockSpec((sources, chunks, width, step), lambda col: (0, first_chunk // chunks, 0, col))
    )
    operands = list(parts) + [weight]
    tile = pl.BlockSpec((seq_len, step), lambda col: (0, col))
    if total is not None:
        specs.append(tile)
        operands.append(total)
    if final:
        out_spec = pl.BlockSpec((1, seq_len, step), lambda col: (0, 0, col))
        out_shape = jax.ShapeDtypeStruct((1, seq_len, out_width), jnp.bfloat16)
    else:
        out_spec = tile
        out_shape = jax.ShapeDtypeStruct((seq_len, out_width), jnp.float32)
    return pl.pallas_call(
        functools.partial(project_kernel, chunks, total is None, final),
        grid=(out_width // step,),
        in_specs=specs,
        out_specs=out_spec,
        out_shape=out_shape,
        compiler_params=pltpu.CompilerParams(vmem_limit_bytes=40 * 1024 * 1024),
        cost_estimate=pl.CostEstimate(
            flops=2 * sources * seq_len * width * chunks * out_width,
            bytes_accessed=2 * sources * chunks * width * (seq_len + out_width) + 4 * seq_len * out_width,
            transcendentals=0,
        ),
        name="project",
    )(*operands)


def on_device(queries, keys, values, out_weight, order_bias, partners, count, order):
    heads_dev = queries.shape[2] // HD
    group_size = HQ // KVH
    resp_total = lax.axis_size("resp")
    mp_total = lax.axis_size("mp")
    first_head = lax.axis_index("mp") * heads_dev
    kv_head = first_head // group_size
    own_keys = lax.dynamic_slice_in_dim(keys[0], kv_head * HD, HD, 1)
    own_values = lax.dynamic_slice_in_dim(values[0], kv_head * HD, HD, 1)
    packed = jnp.stack([own_keys, own_values])
    kv_blocks = [packed] + [shifted(packed, "resp", -offset) for offset in OFFSETS]
    where = jnp.stack([lax.axis_index("resp"), first_head]).astype(jnp.int32)
    chunk_heads = max(1, heads_dev // 4)
    chunks = heads_dev // chunk_heads
    weight = out_weight.reshape(mp_total, chunks, chunk_heads * HD, out_weight.shape[1])
    total = None
    for chunk in range(chunks):
        attended = attention(
            where, partners, count, order, order_bias, queries, kv_blocks,
            chunk * chunk_heads, chunk_heads, resp_total,
        )
        gathered = lax.all_gather(attended, "mp", axis=0, tiled=False)
        total = project(total, [gathered], chunk, weight, chunk == chunks - 1)
    return total


def solution(mesh):
    in_specs = (
        P("resp", None, "mp"),
        P("resp", None, None),
        P("resp", None, None),
        P(None, "mp"),
        P(),
        P("resp", None),
        P("resp"),
        P("resp", None),
    )
    out_specs = P("resp", None, "mp")
    return jax.shard_map(
        on_device, mesh=mesh, in_specs=in_specs, out_specs=out_specs, check_vma=False
    )
```

```python
import functools
import math

import jax
import jax.numpy as jnp
from jax import lax
from jax.experimental import pallas as pl
from jax.experimental.pallas import tpu as pltpu
from jax.sharding import PartitionSpec as P

HQ = 32
KVH = 4
HD = 128
REACH = 3
SLOTS = 6
OFFSETS = tuple(range(1, REACH + 1)) + tuple(-hop for hop in range(1, REACH + 1))
FLIPS = (1, 2, 3, 5, 6, 7)
BLOCKS = 1 + len(OFFSETS)
LOG2E = math.log2(math.e)
VMEM_BYTES = 60 * 1024 * 1024


def flipped(value, bits):
    count = lax.axis_size("resp")
    return lax.ppermute(value, "resp", [(source, source ^ bits) for source in range(count)])


def shifted(value, axis, steps):
    count = lax.axis_size(axis)
    pairs = [(source, (source + steps) % count) for source in range(count)]
    return lax.ppermute(value, axis, pairs)


def pack_kernel(head_ref, keys_ref, values_ref, out_ref):
    del head_ref
    for tile in range(keys_ref.shape[1] // HD):
        rows = slice(tile * HD, (tile + 1) * HD)
        out_ref[0, rows, :] = keys_ref[0, rows, :].T
    out_ref[1] = values_ref[0]


def pack(kv_head, keys, values):
    seq_len = keys.shape[1]
    spec = pl.BlockSpec((1, seq_len, HD), lambda step, head: (0, 0, head[0]))
    return pl.pallas_call(
        pack_kernel,
        grid_spec=pltpu.PrefetchScalarGridSpec(
            num_scalar_prefetch=1,
            grid=(1,),
            in_specs=[spec, spec],
            out_specs=pl.BlockSpec((2, seq_len, HD), lambda step, head: (0, 0, 0)),
        ),
        out_shape=jax.ShapeDtypeStruct((2, seq_len, HD), keys.dtype),
        compiler_params=pltpu.CompilerParams(vmem_limit_bytes=VMEM_BYTES),
        cost_estimate=pl.CostEstimate(flops=0, bytes_accessed=8 * seq_len * HD, transcendentals=0),
        name="pack",
    )(kv_head, keys, values)


def gather_blocks(packed):
    if lax.axis_size("resp") != 8:
        return [packed] + [shifted(packed, "resp", -offset) for offset in OFFSETS]
    far = flipped(packed, 6)
    along_x = flipped(packed, 2)
    along_y = flipped(packed, 4)
    twin = flipped(packed, 1)
    return [
        packed, twin, along_x, flipped(along_x, 1), flipped(along_y, 1), far, flipped(far, 1)
    ]


def target_of(resp_self, resp_total, block):
    if resp_total == 8:
        return resp_self ^ FLIPS[block - 1]
    return lax.rem(resp_self + OFFSETS[block - 1] + resp_total, resp_total)


def attention_kernel(
    head_base, resp_total, where_ref, partners_ref, count_ref, order_ref, bias_ref, q_ref, *rest
):
    kv_refs = rest[:BLOCKS]
    out_ref = rest[BLOCKS]
    scores_ref, expo_ref, peak_ref, total_ref = rest[BLOCKS + 1 :]
    unit, rows = scores_ref.shape[:2]
    seq_len = kv_refs[0].shape[1]
    scale = LOG2E / math.sqrt(HD)
    first_head = where_ref[1] + head_base + pl.program_id(0) * unit

    hits = []
    for block in range(1, BLOCKS):
        target = target_of(where_ref[0], resp_total, block)
        hits.append(
            [(slot < count_ref[0]) & (partners_ref[0, slot] == target) for slot in range(SLOTS)]
        )

    def bias_of(member, block):
        if block == 0:
            return jnp.float32(0.0)
        found = jnp.float32(-jnp.inf)
        for slot in range(SLOTS):
            offset = bias_ref[order_ref[0, slot], first_head + member] * LOG2E
            found = jnp.where(hits[block - 1][slot], offset, found)
        return found

    bias = [[bias_of(member, block) for block in range(BLOCKS)] for member in range(unit)]
    ones = jnp.ones((seq_len, HD), jnp.bfloat16)

    def cols(block):
        return slice(block * seq_len, (block + 1) * seq_len)

    def score(member, block):
        keys = jnp.concatenate(
            [kv_refs[block][0, tile : tile + HD, :] for tile in range(0, seq_len, HD)], axis=1
        )
        scores = jnp.dot(
            q_ref[0, :, member * HD : (member + 1) * HD], keys, preferred_element_type=jnp.float32
        )
        if block == 0:
            row_ids = lax.broadcasted_iota(jnp.int32, scores.shape, 0)
            col_ids = lax.broadcasted_iota(jnp.int32, scores.shape, 1)
            scores = jnp.where(row_ids >= col_ids, scores, -jnp.inf)
        scores_ref[member, :, cols(block)] = scores
        part = scores[:, :HD]
        for lane in range(HD, seq_len, HD):
            part = jnp.maximum(part, scores[:, lane : lane + HD])
        part = part * scale + bias[member][block]
        peak_ref[member] = part if block == 0 else jnp.maximum(peak_ref[member], part)

    def settle(member):
        peak = jnp.max(peak_ref[member], axis=1, keepdims=True)
        peak_ref[member] = jnp.broadcast_to(peak, (rows, HD))

    def expo(member, block):
        offset = bias[member][block] - peak_ref[member]
        scores = scores_ref[member, :, cols(block)]
        shift = jnp.concatenate([offset] * (seq_len // HD), axis=1)
        expo_ref[member, :, cols(block)] = jnp.exp2(scores * scale + shift).astype(jnp.bfloat16)

    def attend(member, block):
        if block % 2 == 1 or block == BLOCKS - 1:
            low = block - block % 2
            wide = jnp.concatenate(
                [
                    jnp.concatenate([kv_refs[held][1], ones], axis=1)
                    for held in range(low, block + 1)
                ],
                axis=0,
            )
            term = jnp.dot(
                expo_ref[member, :, low * seq_len : (block + 1) * seq_len],
                wide,
                preferred_element_type=jnp.float32,
            )
            total_ref[member] = term if low == 0 else total_ref[member] + term

    def finish(member):
        total = total_ref[member]
        out_ref[:, member * HD : (member + 1) * HD] = (total[:, :HD] / total[:, HD:]).astype(
            out_ref.dtype
        )

    for stage in range(unit + 2):
        for block in range(BLOCKS):
            if 0 <= stage - 2 < unit:
                attend(stage - 2, block)
            if 0 <= stage - 1 < unit:
                expo(stage - 1, block)
            if stage < unit:
                score(stage, block)
        if stage < unit:
            settle(stage)
        if 0 <= stage - 2 < unit:
            finish(stage - 2)


def attention(where, partners, count, order, order_bias, queries, kv_blocks, head_base, heads, resp_total):
    seq_len = queries.shape[1]
    unit = 2 if heads % 2 == 0 else 1
    smem = pl.BlockSpec(memory_space=pltpu.SMEM)
    whole = pl.BlockSpec(kv_blocks[0].shape, lambda step: (0, 0, 0))
    keys_all = BLOCKS * seq_len
    return pl.pallas_call(
        functools.partial(attention_kernel, head_base, resp_total),
        grid=(heads // unit,),
        in_specs=[smem] * 5
        + [pl.BlockSpec((1, seq_len, unit * HD), lambda step: (0, 0, head_base // unit + step))]
        + [whole] * BLOCKS,
        out_specs=pl.BlockSpec((seq_len, unit * HD), lambda step: (0, step)),
        out_shape=jax.ShapeDtypeStruct((seq_len, heads * HD), jnp.bfloat16),
        scratch_shapes=[
            pltpu.VMEM((unit, seq_len, keys_all), jnp.float32),
            pltpu.VMEM((unit, seq_len, keys_all), jnp.bfloat16),
            pltpu.VMEM((unit, seq_len, HD), jnp.float32),
            pltpu.VMEM((unit, seq_len, 2 * HD), jnp.float32),
        ],
        compiler_params=pltpu.CompilerParams(vmem_limit_bytes=VMEM_BYTES),
        cost_estimate=pl.CostEstimate(
            flops=heads * seq_len * keys_all * HD * 6,
            bytes_accessed=2 * seq_len * HD * (2 * heads + 2 * BLOCKS),
            transcendentals=heads * seq_len * keys_all,
        ),
        name="attend",
    )(where, partners, count, order, order_bias, queries, *kv_blocks)


def project_kernel(terms, start, final, place_ref, *refs):
    total = None if start else refs[-2][...]
    taken = 0
    for choices in terms:
        held = refs[taken][...]
        for other in range(1, len(choices)):
            held = jnp.where(place_ref[0] == choices[other], refs[taken + other][...], held)
        taken += len(choices)
        term = jnp.dot(held, refs[taken][0], preferred_element_type=jnp.float32)
        taken += 1
        total = term if total is None else total + term
    refs[-1][...] = total.astype(refs[-1].dtype)[None] if final else total


def project(place, total, terms, weight, final):
    seq_len, width = terms[0][0][0][1].shape
    out_width = weight.shape[2]
    step = min(out_width, 512)
    specs, operands, kinds = [], [], []
    for buffers, row_of in terms:
        kinds.append(tuple(at for at, _ in buffers))
        for _, buffer in buffers:
            specs.append(pl.BlockSpec((seq_len, width), lambda col, place: (0, 0)))
            operands.append(buffer)
        specs.append(
            pl.BlockSpec((1, width, step), lambda col, place, row_of=row_of: (row_of(place), 0, col))
        )
        operands.append(weight)
    tile = pl.BlockSpec((seq_len, step), lambda col, place: (0, col))
    if total is not None:
        specs.append(tile)
        operands.append(total)
    if final:
        out_spec = pl.BlockSpec((1, seq_len, step), lambda col, place: (0, 0, col))
        out_shape = jax.ShapeDtypeStruct((1, seq_len, out_width), jnp.bfloat16)
    else:
        out_spec = tile
        out_shape = jax.ShapeDtypeStruct((seq_len, out_width), jnp.float32)
    return pl.pallas_call(
        functools.partial(project_kernel, tuple(kinds), total is None, final),
        grid_spec=pltpu.PrefetchScalarGridSpec(
            num_scalar_prefetch=1,
            grid=(out_width // step,),
            in_specs=specs,
            out_specs=out_spec,
        ),
        out_shape=out_shape,
        compiler_params=pltpu.CompilerParams(vmem_limit_bytes=VMEM_BYTES),
        cost_estimate=pl.CostEstimate(
            flops=2 * seq_len * width * len(terms) * out_width,
            bytes_accessed=2 * width * len(terms) * (seq_len + out_width) + 8 * seq_len * out_width,
            transcendentals=0,
        ),
        name="project",
    )(place, *operands)


def along_line(value, pairs):
    return lax.ppermute(value, "mp", pairs)


def on_device(queries, keys, values, out_weight, order_bias, partners, count, order):
    heads_dev = queries.shape[2] // HD
    group_size = HQ // KVH
    resp_total = lax.axis_size("resp")
    mp_total = lax.axis_size("mp")
    line = lax.axis_index("mp")
    first_head = line * heads_dev
    kv_head = (first_head // group_size).astype(jnp.int32)
    packed = pack(kv_head.reshape(1), keys, values)
    kv_blocks = gather_blocks(packed)
    where = jnp.stack([lax.axis_index("resp"), first_head]).astype(jnp.int32)
    place = line.astype(jnp.int32).reshape(1)

    def attended_of(head_base, heads):
        return attention(
            where, partners, count, order, order_bias, queries, kv_blocks, head_base, heads, resp_total
        )

    if mp_total != 4:
        gathered = lax.all_gather(attended_of(0, heads_dev), "mp", axis=0, tiled=False)
        weight = out_weight.reshape(mp_total, heads_dev * HD, out_weight.shape[1])
        terms = [
            ([(0, gathered[source])], lambda place, source=source: source)
            for source in range(mp_total)
        ]
        return project(place, None, terms, weight, True)

    chunks = 4
    chunk_heads = heads_dev // chunks
    weight = out_weight.reshape(mp_total * chunks, chunk_heads * HD, out_weight.shape[1])
    total = None
    for chunk in range(chunks):
        own = attended_of(chunk * chunk_heads, chunk_heads)
        down = along_line(own, [(1, 0), (2, 1), (3, 2)])
        up = along_line(own, [(0, 1), (1, 2), (2, 3)])
        down_next = along_line(down, [(1, 0), (2, 1)])
        up_next = along_line(up, [(1, 2), (2, 3)])
        far = along_line(jnp.where(line == 1, down_next, up_next), [(1, 0), (2, 3)])

        def row(source, chunk=chunk):
            return lambda place: lax.rem(source(place[0]), 4) * chunks + chunk

        terms = [
            ([(0, own)], row(lambda at: at)),
            ([(0, up), (0, far)], row(lambda at: at + 3)),
            ([(0, down), (3, far)], row(lambda at: at + 1)),
            ([(0, down_next), (2, up_next), (3, up_next)], row(lambda at: at + 2)),
        ]
        total = project(place, total, terms, weight, chunk == chunks - 1)
    return total


def solution(mesh):
    in_specs = (
        P("resp", None, "mp"),
        P("resp", None, None),
        P("resp", None, None),
        P(None, "mp"),
        P(),
        P("resp", None),
        P("resp"),
        P("resp", None),
    )
    out_specs = P("resp", None, "mp")
    return jax.shard_map(
        on_device, mesh=mesh, in_specs=in_specs, out_specs=out_specs, check_vma=False
    )
```

```python
import functools
import math

import jax
import jax.numpy as jnp
from jax import lax
from jax.experimental import pallas as pl
from jax.experimental.pallas import tpu as pltpu
from jax.sharding import PartitionSpec as P

HQ = 32
KVH = 4
HD = 128
REACH = 3
SLOTS = 6
OFFSETS = tuple(range(1, REACH + 1)) + tuple(-hop for hop in range(1, REACH + 1))
FLIPS = (1, 2, 3, 5, 6, 7)
BLOCKS = 1 + len(OFFSETS)
LOG2E = math.log2(math.e)
VMEM_BYTES = 60 * 1024 * 1024


def flipped(value, bits):
    count = lax.axis_size("resp")
    return lax.ppermute(value, "resp", [(source, source ^ bits) for source in range(count)])


def shifted(value, axis, steps):
    count = lax.axis_size(axis)
    pairs = [(source, (source + steps) % count) for source in range(count)]
    return lax.ppermute(value, axis, pairs)


def pack_kernel(head_ref, keys_ref, values_ref, out_ref):
    del head_ref
    for tile in range(keys_ref.shape[1] // HD):
        rows = slice(tile * HD, (tile + 1) * HD)
        out_ref[0, rows, :] = keys_ref[0, rows, :].T
    out_ref[1] = values_ref[0]


def pack(kv_head, keys, values):
    seq_len = keys.shape[1]
    spec = pl.BlockSpec((1, seq_len, HD), lambda step, head: (0, 0, head[0]))
    return pl.pallas_call(
        pack_kernel,
        grid_spec=pltpu.PrefetchScalarGridSpec(
            num_scalar_prefetch=1,
            grid=(1,),
            in_specs=[spec, spec],
            out_specs=pl.BlockSpec((2, seq_len, HD), lambda step, head: (0, 0, 0)),
        ),
        out_shape=jax.ShapeDtypeStruct((2, seq_len, HD), keys.dtype),
        compiler_params=pltpu.CompilerParams(vmem_limit_bytes=VMEM_BYTES),
        cost_estimate=pl.CostEstimate(flops=0, bytes_accessed=8 * seq_len * HD, transcendentals=0),
        name="pack",
    )(kv_head, keys, values)


def gather_blocks(packed):
    if lax.axis_size("resp") != 8:
        return [packed] + [shifted(packed, "resp", -offset) for offset in OFFSETS]
    far = flipped(packed, 6)
    along_x = flipped(packed, 2)
    along_y = flipped(packed, 4)
    twin = flipped(packed, 1)
    return [
        packed, twin, along_x, flipped(along_x, 1), flipped(along_y, 1), far, flipped(far, 1)
    ]


def target_of(resp_self, resp_total, block):
    if resp_total == 8:
        return resp_self ^ FLIPS[block - 1]
    return lax.rem(resp_self + OFFSETS[block - 1] + resp_total, resp_total)


def attention_kernel(
    head_base, resp_total, where_ref, partners_ref, count_ref, order_ref, bias_ref, q_ref, *rest
):
    kv_refs = rest[:BLOCKS]
    out_ref, scores_ref, expo_ref, peak_ref, total_ref = rest[-5:]
    unit, rows = scores_ref.shape[:2]
    seq_len = kv_refs[0].shape[1]
    scale = LOG2E / math.sqrt(HD)
    first_head = where_ref[1] + head_base + pl.program_id(0) * unit

    hits = []
    for block in range(1, BLOCKS):
        target = target_of(where_ref[0], resp_total, block)
        hits.append(
            [(slot < count_ref[0]) & (partners_ref[0, slot] == target) for slot in range(SLOTS)]
        )

    def bias_of(member, block):
        if block == 0:
            return jnp.float32(0.0)
        found = jnp.float32(-jnp.inf)
        for slot in range(SLOTS):
            offset = bias_ref[order_ref[0, slot], first_head + member] * LOG2E
            found = jnp.where(hits[block - 1][slot], offset, found)
        return found

    bias = [[bias_of(member, block) for block in range(BLOCKS)] for member in range(unit)]
    ones = jnp.ones((seq_len, HD), jnp.bfloat16)

    def cols(block):
        return slice(block * seq_len, (block + 1) * seq_len)

    def score(member, block):
        keys = jnp.concatenate(
            [kv_refs[block][0, tile : tile + HD, :] for tile in range(0, seq_len, HD)], axis=1
        )
        scores = jnp.dot(
            q_ref[0, :, member * HD : (member + 1) * HD], keys, preferred_element_type=jnp.float32
        )
        if block == 0:
            row_ids = lax.broadcasted_iota(jnp.int32, scores.shape, 0)
            col_ids = lax.broadcasted_iota(jnp.int32, scores.shape, 1)
            scores = jnp.where(row_ids >= col_ids, scores, -jnp.inf)
        scores_ref[member, :, cols(block)] = scores
        part = scores[:, :HD]
        for lane in range(HD, seq_len, HD):
            part = jnp.maximum(part, scores[:, lane : lane + HD])
        part = part * scale + bias[member][block]
        peak_ref[member] = part if block == 0 else jnp.maximum(peak_ref[member], part)

    def settle(member):
        peak = jnp.max(peak_ref[member], axis=1, keepdims=True)
        peak_ref[member] = jnp.broadcast_to(peak, (rows, HD))

    def expo(member, block):
        offset = bias[member][block] - peak_ref[member]
        scores = scores_ref[member, :, cols(block)]
        shift = jnp.concatenate([offset] * (seq_len // HD), axis=1)
        expo_ref[member, :, cols(block)] = jnp.exp2(scores * scale + shift).astype(jnp.bfloat16)

    def attend(member, block):
        if block % 2 == 1 or block == BLOCKS - 1:
            low = block - block % 2
            wide = jnp.concatenate(
                [
                    jnp.concatenate([kv_refs[held][1], ones], axis=1)
                    for held in range(low, block + 1)
                ],
                axis=0,
            )
            term = jnp.dot(
                expo_ref[member, :, low * seq_len : (block + 1) * seq_len],
                wide,
                preferred_element_type=jnp.float32,
            )
            total_ref[member] = term if low == 0 else total_ref[member] + term

    def finish(member):
        total = total_ref[member]
        out_ref[:, member * HD : (member + 1) * HD] = (total[:, :HD] / total[:, HD:]).astype(
            out_ref.dtype
        )

    for stage in range(unit + 2):
        for block in range(BLOCKS):
            if 0 <= stage - 2 < unit:
                attend(stage - 2, block)
            if 0 <= stage - 1 < unit:
                expo(stage - 1, block)
            if stage < unit:
                score(stage, block)
        if stage < unit:
            settle(stage)
        if 0 <= stage - 2 < unit:
            finish(stage - 2)


def attention(where, partners, count, order, order_bias, queries, kv_blocks, head_base, heads, resp_total, after=()):
    seq_len = queries.shape[1]
    unit = 2 if heads % 2 == 0 else 1
    smem = pl.BlockSpec(memory_space=pltpu.SMEM)
    whole = pl.BlockSpec(kv_blocks[0].shape, lambda step: (0, 0, 0))
    keys_all = BLOCKS * seq_len
    return pl.pallas_call(
        functools.partial(attention_kernel, head_base, resp_total),
        grid=(heads // unit,),
        in_specs=[smem] * 5
        + [pl.BlockSpec((1, seq_len, unit * HD), lambda step: (0, 0, head_base // unit + step))]
        + [whole] * BLOCKS
        + [pl.BlockSpec(memory_space=pl.ANY)] * len(after),
        out_specs=pl.BlockSpec((seq_len, unit * HD), lambda step: (0, step)),
        out_shape=jax.ShapeDtypeStruct((seq_len, heads * HD), jnp.bfloat16),
        scratch_shapes=[
            pltpu.VMEM((unit, seq_len, keys_all), jnp.float32),
            pltpu.VMEM((unit, seq_len, keys_all), jnp.bfloat16),
            pltpu.VMEM((unit, seq_len, HD), jnp.float32),
            pltpu.VMEM((unit, seq_len, 2 * HD), jnp.float32),
        ],
        compiler_params=pltpu.CompilerParams(vmem_limit_bytes=VMEM_BYTES),
        cost_estimate=pl.CostEstimate(
            flops=heads * seq_len * keys_all * HD * 6,
            bytes_accessed=2 * seq_len * HD * (2 * heads + 2 * BLOCKS),
            transcendentals=heads * seq_len * keys_all,
        ),
        name="attend",
    )(where, partners, count, order, order_bias, queries, *kv_blocks, *after)


def project_kernel(parts, start, final, waits, place_ref, *refs):
    inputs = refs[: sum(len(kinds) + rows for kinds, rows in parts)]
    out_at = len(inputs) + waits + (0 if start else 1)
    out_ref, held_refs = refs[out_at], refs[out_at + 1 :]
    left, right = [], []
    taken = chosen = 0
    for kinds, rows in parts:
        if len(kinds) == 1:
            left.append(inputs[taken][...])
        else:
            held_ref = held_refs[chosen]
            chosen += 1
            for other, places in enumerate(kinds):
                wanted = functools.reduce(jnp.logical_or, [place_ref[0] == at for at in places])

                @pl.when((pl.program_id(0) == 0) & wanted)
                def _(source_ref=inputs[taken + other]):
                    held_ref[...] = source_ref[...]

            left.append(held_ref[...])
        taken += len(kinds)
        for _ in range(rows):
            right.append(inputs[taken][0])
            taken += 1
    total = jnp.dot(
        jnp.concatenate(left, axis=1),
        jnp.concatenate(right, axis=0),
        preferred_element_type=jnp.float32,
    )
    if not start:
        total = total + refs[len(inputs)][...]
    out_ref[...] = total.astype(out_ref.dtype)[None] if final else total


def project(place, total, parts, weight, final, after=()):
    seq_len = parts[0][0][0][0].shape[0]
    width, out_width = weight.shape[1:]
    step = min(out_width, 512)
    specs, operands, kinds, held = [], [], [], []
    depth = 0
    for buffers, rows in parts:
        kinds.append((tuple(tuple(places) for _, places in buffers), len(rows)))
        for buffer, _ in buffers:
            specs.append(pl.BlockSpec(buffer.shape, lambda col, place: (0, 0)))
            operands.append(buffer)
        if len(buffers) > 1:
            held.append(pltpu.VMEM(buffers[0][0].shape, jnp.bfloat16))
        for row in rows:
            specs.append(
                pl.BlockSpec((1, width, step), lambda col, place, row=row: (row(place[0]), 0, col))
            )
            operands.append(weight)
        depth += width * len(rows)
    tile = pl.BlockSpec((seq_len, step), lambda col, place: (0, col))
    if total is not None:
        specs.append(tile)
        operands.append(total)
    specs += [pl.BlockSpec(memory_space=pl.ANY)] * len(after)
    operands += list(after)
    if final:
        out_spec = pl.BlockSpec((1, seq_len, step), lambda col, place: (0, 0, col))
        out_shape = jax.ShapeDtypeStruct((1, seq_len, out_width), jnp.bfloat16)
    else:
        out_spec = tile
        out_shape = jax.ShapeDtypeStruct((seq_len, out_width), jnp.float32)
    return pl.pallas_call(
        functools.partial(project_kernel, tuple(kinds), total is None, final, len(after)),
        grid_spec=pltpu.PrefetchScalarGridSpec(
            num_scalar_prefetch=1,
            grid=(out_width // step,),
            in_specs=specs,
            out_specs=out_spec,
            scratch_shapes=held,
        ),
        out_shape=out_shape,
        compiler_params=pltpu.CompilerParams(vmem_limit_bytes=24 * 1024 * 1024),
        cost_estimate=pl.CostEstimate(
            flops=2 * seq_len * depth * out_width,
            bytes_accessed=2 * depth * (seq_len + out_width) + 8 * seq_len * out_width,
            transcendentals=0,
        ),
        name="project",
    )(place, *operands)


def join_kernel(left_ref, right_ref, *refs):
    out_ref = refs[-1]
    width = left_ref.shape[1]
    out_ref[:, :width] = left_ref[...]
    out_ref[:, width:] = right_ref[...]


def join(left, right, after):
    rows, width = left.shape
    spec = pl.BlockSpec((rows, width), lambda step: (0, 0))
    return pl.pallas_call(
        join_kernel,
        grid=(1,),
        in_specs=[spec, spec] + [pl.BlockSpec(memory_space=pl.ANY)] * len(after),
        out_specs=pl.BlockSpec((rows, 2 * width), lambda step: (0, 0)),
        out_shape=jax.ShapeDtypeStruct((rows, 2 * width), left.dtype),
        compiler_params=pltpu.CompilerParams(vmem_limit_bytes=8 * 1024 * 1024),
        cost_estimate=pl.CostEstimate(flops=0, bytes_accessed=8 * rows * width, transcendentals=0),
        name="join",
    )(left, right, *after)


def along_line(value, pairs):
    return lax.ppermute(value, "mp", pairs)


def on_device(queries, keys, values, out_weight, order_bias, partners, count, order):
    heads_dev = queries.shape[2] // HD
    group_size = HQ // KVH
    resp_total = lax.axis_size("resp")
    mp_total = lax.axis_size("mp")
    line = lax.axis_index("mp")
    first_head = line * heads_dev
    kv_head = (first_head // group_size).astype(jnp.int32)
    packed = pack(kv_head.reshape(1), keys, values)
    kv_blocks = gather_blocks(packed)
    where = jnp.stack([lax.axis_index("resp"), first_head]).astype(jnp.int32)
    place = line.astype(jnp.int32).reshape(1)

    def attended_of(head_base, heads, after=()):
        return attention(
            where, partners, count, order, order_bias, queries, kv_blocks, head_base, heads, resp_total, after
        )

    if mp_total != 4:
        gathered = lax.all_gather(attended_of(0, heads_dev), "mp", axis=0, tiled=False)
        weight = out_weight.reshape(mp_total, heads_dev * HD, out_weight.shape[1])
        parts = [
            ([(gathered[source], ())], [lambda at, source=source: source]) for source in range(mp_total)
        ]
        return project(place, None, parts, weight, True)

    chunks = 4
    chunk_heads = heads_dev // chunks
    weight = out_weight.reshape(mp_total * chunks, chunk_heads * HD, out_weight.shape[1])
    inner, outer = (1, 2), (0, 3)
    own, pair, joined, crossed, forwarded = [], [], [], [], []

    def cross(chunk, after):
        joined.append(join(own[chunk], pair[chunk], after))
        crossed.append(along_line(joined[chunk], [(1, 2), (2, 1)]))

    def forward(chunk):
        forwarded.append(along_line(crossed[chunk], [(1, 0), (2, 3)]))

    def own_part(chunk):
        return ([(own[chunk], ())], [lambda at: at * chunks + chunk])

    def pair_part(chunk):
        return ([(pair[chunk], ())], [lambda at: (at ^ 1) * chunks + chunk])

    def far_part(chunk):
        rows = [
            lambda at: jnp.where(at < 2, 2, 1) * chunks + chunk,
            lambda at: jnp.where(at < 2, 3, 0) * chunks + chunk,
        ]
        return ([(crossed[chunk], inner), (forwarded[chunk], outer)], rows)

    for chunk in range(chunks):
        after = tuple(joined[chunk - 2 : chunk - 1]) + tuple(crossed[chunk - 3 : chunk - 2])
        own.append(attended_of(chunk * chunk_heads, chunk_heads, after if chunk >= 2 else ()))
        pair.append(along_line(own[chunk], [(0, 1), (1, 0), (2, 3), (3, 2)]))
        if chunk >= 1:
            cross(chunk - 1, (own[chunk],))
        if chunk >= 2:
            forward(chunk - 2)
    parts = [own_part(chunk) for chunk in range(4)] + [pair_part(chunk) for chunk in range(3)]
    total = project(place, None, parts, weight, False, (joined[2], crossed[1]))
    cross(3, (total,))
    forward(2)
    total = project(
        place, total, [pair_part(3), far_part(0), far_part(1)], weight, False, (joined[3], crossed[2])
    )
    forward(3)
    total = project(place, total, [far_part(2)], weight, False, (crossed[3],))
    return project(place, total, [far_part(3)], weight, True)


def solution(mesh):
    in_specs = (
        P("resp", None, "mp"),
        P("resp", None, None),
        P("resp", None, None),
        P(None, "mp"),
        P(),
        P("resp", None),
        P("resp"),
        P("resp", None),
    )
    out_specs = P("resp", None, "mp")
    return jax.shard_map(
        on_device, mesh=mesh, in_specs=in_specs, out_specs=out_specs, check_vma=False
    )
```

```python
import functools
import math

import jax
import jax.numpy as jnp
from jax import lax
from jax.experimental import pallas as pl
from jax.experimental.pallas import tpu as pltpu
from jax.sharding import PartitionSpec as P

HQ = 32
KVH = 4
HD = 128
REACH = 3
SLOTS = 6
OFFSETS = tuple(range(1, REACH + 1)) + tuple(-hop for hop in range(1, REACH + 1))
FLIPS = (1, 2, 3, 5, 6, 7)
BLOCKS = 1 + len(OFFSETS)
LOG2E = math.log2(math.e)
VMEM_BYTES = 60 * 1024 * 1024


def flipped(value, bits):
    count = lax.axis_size("resp")
    return lax.ppermute(value, "resp", [(source, source ^ bits) for source in range(count)])


def shifted(value, axis, steps):
    count = lax.axis_size(axis)
    pairs = [(source, (source + steps) % count) for source in range(count)]
    return lax.ppermute(value, axis, pairs)


def pack_kernel(head_ref, keys_ref, values_ref, out_ref):
    del head_ref
    for tile in range(keys_ref.shape[1] // HD):
        rows = slice(tile * HD, (tile + 1) * HD)
        out_ref[0, rows, :] = keys_ref[0, rows, :].T
    out_ref[1] = values_ref[0]


def pack(kv_head, keys, values):
    seq_len = keys.shape[1]
    spec = pl.BlockSpec((1, seq_len, HD), lambda step, head: (0, 0, head[0]))
    return pl.pallas_call(
        pack_kernel,
        grid_spec=pltpu.PrefetchScalarGridSpec(
            num_scalar_prefetch=1,
            grid=(1,),
            in_specs=[spec, spec],
            out_specs=pl.BlockSpec((2, seq_len, HD), lambda step, head: (0, 0, 0)),
        ),
        out_shape=jax.ShapeDtypeStruct((2, seq_len, HD), keys.dtype),
        compiler_params=pltpu.CompilerParams(vmem_limit_bytes=VMEM_BYTES),
        cost_estimate=pl.CostEstimate(flops=0, bytes_accessed=8 * seq_len * HD, transcendentals=0),
        name="pack",
    )(kv_head, keys, values)


def gather_blocks(packed):
    if lax.axis_size("resp") != 8:
        return [packed] + [shifted(packed, "resp", -offset) for offset in OFFSETS]
    far = flipped(packed, 6)
    along_x = flipped(packed, 2)
    along_y = flipped(packed, 4)
    twin = flipped(packed, 1)
    return [
        packed, twin, along_x, flipped(along_x, 1), flipped(along_y, 1), far, flipped(far, 1)
    ]


def target_of(resp_self, resp_total, block):
    if resp_total == 8:
        return resp_self ^ FLIPS[block - 1]
    return lax.rem(resp_self + OFFSETS[block - 1] + resp_total, resp_total)


def attention_kernel(
    head_base, resp_total, where_ref, partners_ref, count_ref, order_ref, bias_ref, q_ref, *rest
):
    kv_refs = rest[:BLOCKS]
    out_ref, scores_ref, expo_ref, peak_ref, total_ref = rest[-5:]
    unit, rows = scores_ref.shape[:2]
    seq_len = kv_refs[0].shape[1]
    scale = LOG2E / math.sqrt(HD)
    first_head = where_ref[1] + head_base + pl.program_id(0) * unit

    hits = []
    for block in range(1, BLOCKS):
        target = target_of(where_ref[0], resp_total, block)
        hits.append(
            [(slot < count_ref[0]) & (partners_ref[0, slot] == target) for slot in range(SLOTS)]
        )

    def bias_of(member, block):
        if block == 0:
            return jnp.float32(0.0)
        found = jnp.float32(-jnp.inf)
        for slot in range(SLOTS):
            offset = bias_ref[order_ref[0, slot], first_head + member] * LOG2E
            found = jnp.where(hits[block - 1][slot], offset, found)
        return found

    bias = [[bias_of(member, block) for block in range(BLOCKS)] for member in range(unit)]
    ones = jnp.ones((seq_len, HD), jnp.bfloat16)

    def cols(block):
        return slice(block * seq_len, (block + 1) * seq_len)

    def score(member, block):
        keys = jnp.concatenate(
            [kv_refs[block][0, tile : tile + HD, :] for tile in range(0, seq_len, HD)], axis=1
        )
        scores = jnp.dot(
            q_ref[0, :, member * HD : (member + 1) * HD], keys, preferred_element_type=jnp.float32
        )
        if block == 0:
            row_ids = lax.broadcasted_iota(jnp.int32, scores.shape, 0)
            col_ids = lax.broadcasted_iota(jnp.int32, scores.shape, 1)
            scores = jnp.where(row_ids >= col_ids, scores, -jnp.inf)
        scores_ref[member, :, cols(block)] = scores
        part = scores[:, :HD]
        for lane in range(HD, seq_len, HD):
            part = jnp.maximum(part, scores[:, lane : lane + HD])
        part = part * scale + bias[member][block]
        peak_ref[member] = part if block == 0 else jnp.maximum(peak_ref[member], part)

    def settle(member):
        peak = jnp.max(peak_ref[member], axis=1, keepdims=True)
        peak_ref[member] = jnp.broadcast_to(peak, (rows, HD))

    def expo(member, block):
        offset = bias[member][block] - peak_ref[member]
        scores = scores_ref[member, :, cols(block)]
        shift = jnp.concatenate([offset] * (seq_len // HD), axis=1)
        expo_ref[member, :, cols(block)] = jnp.exp2(scores * scale + shift).astype(jnp.bfloat16)

    def attend(member, block):
        if block % 2 == 1 or block == BLOCKS - 1:
            low = block - block % 2
            wide = jnp.concatenate(
                [
                    jnp.concatenate([kv_refs[held][1], ones], axis=1)
                    for held in range(low, block + 1)
                ],
                axis=0,
            )
            term = jnp.dot(
                expo_ref[member, :, low * seq_len : (block + 1) * seq_len],
                wide,
                preferred_element_type=jnp.float32,
            )
            total_ref[member] = term if low == 0 else total_ref[member] + term

    def finish(member):
        total = total_ref[member]
        out_ref[:, member * HD : (member + 1) * HD] = (total[:, :HD] / total[:, HD:]).astype(
            out_ref.dtype
        )

    for stage in range(unit + 2):
        for block in range(BLOCKS):
            if 0 <= stage - 2 < unit:
                attend(stage - 2, block)
            if 0 <= stage - 1 < unit:
                expo(stage - 1, block)
            if stage < unit:
                score(stage, block)
        if stage < unit:
            settle(stage)
        if 0 <= stage - 2 < unit:
            finish(stage - 2)


def attention(where, partners, count, order, order_bias, queries, kv_blocks, head_base, heads, resp_total, after=()):
    seq_len = queries.shape[1]
    unit = 2 if heads % 2 == 0 else 1
    smem = pl.BlockSpec(memory_space=pltpu.SMEM)
    whole = pl.BlockSpec(kv_blocks[0].shape, lambda step: (0, 0, 0))
    keys_all = BLOCKS * seq_len
    return pl.pallas_call(
        functools.partial(attention_kernel, head_base, resp_total),
        grid=(heads // unit,),
        in_specs=[smem] * 5
        + [pl.BlockSpec((1, seq_len, unit * HD), lambda step: (0, 0, head_base // unit + step))]
        + [whole] * BLOCKS
        + [pl.BlockSpec(memory_space=pl.ANY)] * len(after),
        out_specs=pl.BlockSpec((seq_len, unit * HD), lambda step: (0, step)),
        out_shape=jax.ShapeDtypeStruct((seq_len, heads * HD), jnp.bfloat16),
        scratch_shapes=[
            pltpu.VMEM((unit, seq_len, keys_all), jnp.float32),
            pltpu.VMEM((unit, seq_len, keys_all), jnp.bfloat16),
            pltpu.VMEM((unit, seq_len, HD), jnp.float32),
            pltpu.VMEM((unit, seq_len, 2 * HD), jnp.float32),
        ],
        compiler_params=pltpu.CompilerParams(vmem_limit_bytes=VMEM_BYTES),
        cost_estimate=pl.CostEstimate(
            flops=heads * seq_len * keys_all * HD * 6,
            bytes_accessed=2 * seq_len * HD * (2 * heads + 2 * BLOCKS),
            transcendentals=heads * seq_len * keys_all,
        ),
        name="attend",
    )(where, partners, count, order, order_bias, queries, *kv_blocks, *after)


def project_kernel(parts, start, final, waits, place_ref, *refs):
    inputs = refs[: sum(len(kinds) + rows for kinds, rows in parts)]
    out_at = len(inputs) + waits + (0 if start else 1)
    out_ref, held_refs = refs[out_at], refs[out_at + 1 :]
    left, right = [], []
    taken = chosen = 0
    for kinds, rows in parts:
        if len(kinds) == 1:
            left.append(inputs[taken][...])
        else:
            held_ref = held_refs[chosen]
            chosen += 1
            for other, places in enumerate(kinds):
                wanted = functools.reduce(jnp.logical_or, [place_ref[0] == at for at in places])

                @pl.when((pl.program_id(0) == 0) & wanted)
                def _(source_ref=inputs[taken + other]):
                    held_ref[...] = source_ref[...]

            left.append(held_ref[...])
        taken += len(kinds)
        for _ in range(rows):
            right.append(inputs[taken][0])
            taken += 1
    total = jnp.dot(
        jnp.concatenate(left, axis=1),
        jnp.concatenate(right, axis=0),
        preferred_element_type=jnp.float32,
    )
    if not start:
        total = total + refs[len(inputs)][...]
    out_ref[...] = total.astype(out_ref.dtype)[None] if final else total


def project(place, total, parts, weight, final, after=()):
    seq_len = parts[0][0][0][0].shape[0]
    width, out_width = weight.shape[1:]
    step = min(out_width, 512)
    specs, operands, kinds, held = [], [], [], []
    depth = 0
    for buffers, rows in parts:
        kinds.append((tuple(tuple(places) for _, places in buffers), len(rows)))
        for buffer, _ in buffers:
            specs.append(pl.BlockSpec(buffer.shape, lambda col, place: (0, 0)))
            operands.append(buffer)
        if len(buffers) > 1:
            held.append(pltpu.VMEM(buffers[0][0].shape, jnp.bfloat16))
        for row in rows:
            specs.append(
                pl.BlockSpec((1, width, step), lambda col, place, row=row: (row(place[0]), 0, col))
            )
            operands.append(weight)
        depth += width * len(rows)
    tile = pl.BlockSpec((seq_len, step), lambda col, place: (0, col))
    if total is not None:
        specs.append(tile)
        operands.append(total)
    specs += [pl.BlockSpec(memory_space=pl.ANY)] * len(after)
    operands += list(after)
    if final:
        out_spec = pl.BlockSpec((1, seq_len, step), lambda col, place: (0, 0, col))
        out_shape = jax.ShapeDtypeStruct((1, seq_len, out_width), jnp.bfloat16)
    else:
        out_spec = tile
        out_shape = jax.ShapeDtypeStruct((seq_len, out_width), jnp.float32)
    return pl.pallas_call(
        functools.partial(project_kernel, tuple(kinds), total is None, final, len(after)),
        grid_spec=pltpu.PrefetchScalarGridSpec(
            num_scalar_prefetch=1,
            grid=(out_width // step,),
            in_specs=specs,
            out_specs=out_spec,
            scratch_shapes=held,
        ),
        out_shape=out_shape,
        compiler_params=pltpu.CompilerParams(vmem_limit_bytes=50 * 1024 * 1024),
        cost_estimate=pl.CostEstimate(
            flops=2 * seq_len * depth * out_width,
            bytes_accessed=2 * depth * (seq_len + out_width) + 8 * seq_len * out_width,
            transcendentals=0,
        ),
        name="project",
    )(place, *operands)


def join_kernel(left_ref, right_ref, *refs):
    out_ref = refs[-1]
    width = left_ref.shape[1]
    out_ref[:, :width] = left_ref[...]
    out_ref[:, width:] = right_ref[...]


def join(left, right, after):
    rows, width = left.shape
    spec = pl.BlockSpec((rows, width), lambda step: (0, 0))
    return pl.pallas_call(
        join_kernel,
        grid=(1,),
        in_specs=[spec, spec] + [pl.BlockSpec(memory_space=pl.ANY)] * len(after),
        out_specs=pl.BlockSpec((rows, 2 * width), lambda step: (0, 0)),
        out_shape=jax.ShapeDtypeStruct((rows, 2 * width), left.dtype),
        compiler_params=pltpu.CompilerParams(vmem_limit_bytes=8 * 1024 * 1024),
        cost_estimate=pl.CostEstimate(flops=0, bytes_accessed=8 * rows * width, transcendentals=0),
        name="join",
    )(left, right, *after)


def along_line(value, pairs):
    return lax.ppermute(value, "mp", pairs)


def on_device(queries, keys, values, out_weight, order_bias, partners, count, order):
    heads_dev = queries.shape[2] // HD
    group_size = HQ // KVH
    resp_total = lax.axis_size("resp")
    mp_total = lax.axis_size("mp")
    line = lax.axis_index("mp")
    first_head = line * heads_dev
    kv_head = (first_head // group_size).astype(jnp.int32)
    packed = pack(kv_head.reshape(1), keys, values)
    kv_blocks = gather_blocks(packed)
    where = jnp.stack([lax.axis_index("resp"), first_head]).astype(jnp.int32)
    place = line.astype(jnp.int32).reshape(1)

    def attended_of(head_base, heads, after=()):
        return attention(
            where, partners, count, order, order_bias, queries, kv_blocks, head_base, heads, resp_total, after
        )

    if mp_total != 4:
        gathered = lax.all_gather(attended_of(0, heads_dev), "mp", axis=0, tiled=False)
        weight = out_weight.reshape(mp_total, heads_dev * HD, out_weight.shape[1])
        parts = [
            ([(gathered[source], ())], [lambda at, source=source: source]) for source in range(mp_total)
        ]
        return project(place, None, parts, weight, True)

    chunks = 4
    chunk_heads = heads_dev // chunks
    weight = out_weight.reshape(mp_total * chunks, chunk_heads * HD, out_weight.shape[1])
    inner, outer = (1, 2), (0, 3)
    own, pair, joined, crossed, forwarded = [], [], [], [], []

    def cross(chunk, after):
        joined.append(join(own[chunk], pair[chunk], after))
        crossed.append(along_line(joined[chunk], [(1, 2), (2, 1)]))

    def forward(chunk, after):
        held = lax.optimization_barrier((crossed[chunk],) + after)[0]
        forwarded.append(along_line(held, [(1, 0), (2, 3)]))

    def own_part(chunk):
        return ([(own[chunk], ())], [lambda at: at * chunks + chunk])

    def pair_part(chunk):
        return ([(pair[chunk], ())], [lambda at: (at ^ 1) * chunks + chunk])

    def far_part(chunk):
        rows = [
            lambda at: jnp.where(at < 2, 2, 1) * chunks + chunk,
            lambda at: jnp.where(at < 2, 3, 0) * chunks + chunk,
        ]
        return ([(crossed[chunk], inner), (forwarded[chunk], outer)], rows)

    for chunk in range(chunks):
        after = tuple(joined[chunk - 2 : chunk - 1]) + tuple(crossed[chunk - 3 : chunk - 2])
        own.append(attended_of(chunk * chunk_heads, chunk_heads, after if chunk >= 2 else ()))
        pair.append(along_line(own[chunk], [(0, 1), (1, 0), (2, 3), (3, 2)]))
        if chunk >= 2:
            forward(chunk - 2, (own[chunk],))
        if chunk >= 1:
            cross(chunk - 1, (own[chunk],) + tuple(forwarded[chunk - 3 : chunk - 2]))
    parts = [own_part(chunk) for chunk in range(4)] + [pair_part(chunk) for chunk in range(3)]
    total = project(place, None, parts, weight, False, (joined[2], crossed[1]))
    cross(3, (total, forwarded[1]))
    forward(2, (total,))
    total = project(
        place, total, [pair_part(3), far_part(0), far_part(1)], weight, False, (joined[3], crossed[2])
    )
    forward(3, (total,))
    total = project(place, total, [far_part(2)], weight, False, (crossed[3],))
    return project(place, total, [far_part(3)], weight, True)


def solution(mesh):
    in_specs = (
        P("resp", None, "mp"),
        P("resp", None, None),
        P("resp", None, None),
        P(None, "mp"),
        P(),
        P("resp", None),
        P("resp"),
        P("resp", None),
    )
    out_specs = P("resp", None, "mp")
    return jax.shard_map(
        on_device, mesh=mesh, in_specs=in_specs, out_specs=out_specs, check_vma=False
    )
```

```python
import functools
import math

import jax
import jax.numpy as jnp
from jax import lax
from jax.experimental import pallas as pl
from jax.experimental.pallas import tpu as pltpu
from jax.sharding import PartitionSpec as P

HQ = 32
KVH = 4
HD = 128
REACH = 3
SLOTS = 6
OFFSETS = tuple(range(1, REACH + 1)) + tuple(-hop for hop in range(1, REACH + 1))
FLIPS = (1, 2, 3, 5, 6, 7)
BLOCKS = 1 + len(OFFSETS)
LOG2E = math.log2(math.e)
VMEM_BYTES = 60 * 1024 * 1024


def flipped(value, bits):
    count = lax.axis_size("resp")
    return lax.ppermute(value, "resp", [(source, source ^ bits) for source in range(count)])


def shifted(value, axis, steps):
    count = lax.axis_size(axis)
    pairs = [(source, (source + steps) % count) for source in range(count)]
    return lax.ppermute(value, axis, pairs)


def pack_kernel(head_ref, keys_ref, values_ref, out_ref):
    del head_ref
    for tile in range(keys_ref.shape[1] // HD):
        rows = slice(tile * HD, (tile + 1) * HD)
        out_ref[1, rows, :] = values_ref[0, rows, :].T
    out_ref[0] = keys_ref[0]


def pack(kv_head, keys, values):
    seq_len = keys.shape[1]
    spec = pl.BlockSpec((1, seq_len, HD), lambda step, head: (0, 0, head[0]))
    return pl.pallas_call(
        pack_kernel,
        grid_spec=pltpu.PrefetchScalarGridSpec(
            num_scalar_prefetch=1,
            grid=(1,),
            in_specs=[spec, spec],
            out_specs=pl.BlockSpec((2, seq_len, HD), lambda step, head: (0, 0, 0)),
        ),
        out_shape=jax.ShapeDtypeStruct((2, seq_len, HD), keys.dtype),
        compiler_params=pltpu.CompilerParams(vmem_limit_bytes=VMEM_BYTES),
        cost_estimate=pl.CostEstimate(flops=0, bytes_accessed=8 * seq_len * HD, transcendentals=0),
        name="pack",
    )(kv_head, keys, values)


def gather_blocks(packed):
    if lax.axis_size("resp") != 8:
        return [packed] + [shifted(packed, "resp", -offset) for offset in OFFSETS]
    far = flipped(packed, 6)
    along_x = flipped(packed, 2)
    along_y = flipped(packed, 4)
    twin = flipped(packed, 1)
    return [
        packed, twin, along_x, flipped(along_x, 1), flipped(along_y, 1), far, flipped(far, 1)
    ]


def target_of(resp_self, resp_total, block):
    if resp_total == 8:
        return resp_self ^ FLIPS[block - 1]
    return lax.rem(resp_self + OFFSETS[block - 1] + resp_total, resp_total)


def attention_kernel(
    head_base, resp_total, where_ref, partners_ref, count_ref, order_ref, bias_ref, q_ref, *rest
):
    kv_refs = rest[:BLOCKS]
    out_ref, scores_ref = rest[-2:]
    rows = scores_ref.shape[2]
    seq_len = kv_refs[0].shape[1]
    heads = q_ref.shape[2] // HD
    halves = seq_len // rows
    scale = LOG2E / math.sqrt(HD)
    first_head = where_ref[1] + head_base + pl.program_id(0) * heads

    hits = []
    for block in range(1, BLOCKS):
        target = target_of(where_ref[0], resp_total, block)
        hits.append(
            [(slot < count_ref[0]) & (partners_ref[0, slot] == target) for slot in range(SLOTS)]
        )

    def bias_of(head, block):
        if block == 0:
            return jnp.float32(0.0)
        found = jnp.float32(-jnp.inf)
        for slot in range(SLOTS):
            offset = bias_ref[order_ref[0, slot], first_head + head] * LOG2E
            found = jnp.where(hits[block - 1][slot], offset, found)
        return found

    bias = [[bias_of(head, block) for block in range(BLOCKS)] for head in range(heads)]
    units = [(head, half) for head in range(heads) for half in range(halves)]

    def segments(half):
        found = [(0, part * rows, rows, part * rows, part == half) for part in range(half + 1)]
        at = (half + 1) * rows
        for block in range(1, BLOCKS):
            found.append((block, 0, seq_len, at, False))
            at += seq_len
        return found

    def score(unit, segment):
        head, half = units[unit]
        block, first, length, at, masked = segment
        scores = lax.dot_general(
            kv_refs[block][0, first : first + length, :],
            q_ref[0, half * rows : (half + 1) * rows, head * HD : (head + 1) * HD],
            (((1,), (1,)), ((), ())),
            preferred_element_type=jnp.float32,
        )
        if masked:
            key_ids = lax.broadcasted_iota(jnp.int32, scores.shape, 0)
            query_ids = lax.broadcasted_iota(jnp.int32, scores.shape, 1)
            scores = jnp.where(query_ids >= key_ids, scores, -jnp.inf)
        scores_ref[unit % 2, at : at + length, :] = scores
        return jnp.max(scores, axis=0, keepdims=True) * scale + bias[head][block]

    def attend(unit, segment, peak):
        head, _ = units[unit]
        block, first, length, at, _ = segment
        scores = scores_ref[unit % 2, at : at + length, :]
        expo = jnp.exp2(scores * scale + (bias[head][block] - peak)).astype(jnp.bfloat16)
        turned = [kv_refs[block][1, tile : tile + HD, :] for tile in range(first, first + length, HD)]
        tall = jnp.concatenate(
            [jnp.concatenate(turned, axis=1), jnp.ones((16, length), jnp.bfloat16)], axis=0
        )
        return jnp.dot(tall, expo, preferred_element_type=jnp.float32)

    def finish(unit, total):
        head, half = units[unit]
        mean = total[:HD] / total[HD : HD + 1]
        out_ref[half * rows : (half + 1) * rows, head * HD : (head + 1) * HD] = mean.T.astype(
            out_ref.dtype
        )

    peak = None
    for stage in range(len(units) + 1):
        scoring = segments(units[stage][1]) if stage < len(units) else []
        attending = segments(units[stage - 1][1]) if stage >= 1 else []
        next_peak = total = None
        for step in range(max(len(scoring), len(attending))):
            if step < len(attending):
                term = attend(stage - 1, attending[step], peak)
                total = term if total is None else total + term
            if step < len(scoring):
                part = score(stage, scoring[step])
                next_peak = part if next_peak is None else jnp.maximum(next_peak, part)
        if stage >= 1:
            finish(stage - 1, total)
        peak = next_peak


def attention(where, partners, count, order, order_bias, queries, kv_blocks, head_base, heads, resp_total, after=()):
    seq_len = queries.shape[1]
    unit = 2 if heads % 2 == 0 else 1
    smem = pl.BlockSpec(memory_space=pltpu.SMEM)
    whole = pl.BlockSpec(kv_blocks[0].shape, lambda step: (0, 0, 0))
    keys_all = BLOCKS * seq_len
    return pl.pallas_call(
        functools.partial(attention_kernel, head_base, resp_total),
        grid=(heads // unit,),
        in_specs=[smem] * 5
        + [pl.BlockSpec((1, seq_len, unit * HD), lambda step: (0, 0, head_base // unit + step))]
        + [whole] * BLOCKS
        + [pl.BlockSpec(memory_space=pl.ANY)] * len(after),
        out_specs=pl.BlockSpec((seq_len, unit * HD), lambda step: (0, step)),
        out_shape=jax.ShapeDtypeStruct((seq_len, heads * HD), jnp.bfloat16),
        scratch_shapes=[pltpu.VMEM((2, keys_all, min(seq_len, 256)), jnp.float32)],
        compiler_params=pltpu.CompilerParams(vmem_limit_bytes=VMEM_BYTES),
        cost_estimate=pl.CostEstimate(
            flops=heads * seq_len * keys_all * HD * 6,
            bytes_accessed=2 * seq_len * HD * (2 * heads + 2 * BLOCKS),
            transcendentals=heads * seq_len * keys_all,
        ),
        name="attend",
    )(where, partners, count, order, order_bias, queries, *kv_blocks, *after)


def project_kernel(parts, start, final, waits, place_ref, *refs):
    inputs = refs[: sum(len(kinds) + rows for kinds, rows in parts)]
    out_at = len(inputs) + waits + (0 if start else 1)
    out_ref, held_refs = refs[out_at], refs[out_at + 1 :]
    left, right = [], []
    taken = chosen = 0
    for kinds, rows in parts:
        if len(kinds) == 1:
            left.append(inputs[taken][...])
        else:
            held_ref = held_refs[chosen]
            chosen += 1
            for other, places in enumerate(kinds):
                wanted = functools.reduce(jnp.logical_or, [place_ref[0] == at for at in places])

                @pl.when((pl.program_id(0) == 0) & wanted)
                def _(source_ref=inputs[taken + other]):
                    held_ref[...] = source_ref[...]

            left.append(held_ref[...])
        taken += len(kinds)
        for _ in range(rows):
            right.append(inputs[taken][0])
            taken += 1
    total = jnp.dot(
        jnp.concatenate(left, axis=1),
        jnp.concatenate(right, axis=0),
        preferred_element_type=jnp.float32,
    )
    if not start:
        total = total + refs[len(inputs)][...]
    out_ref[...] = total.astype(out_ref.dtype)[None] if final else total


def project(place, total, parts, weight, final, after=()):
    seq_len = parts[0][0][0][0].shape[0]
    width, out_width = weight.shape[1:]
    step = min(out_width, 512)
    specs, operands, kinds, held = [], [], [], []
    depth = 0
    for buffers, rows in parts:
        kinds.append((tuple(tuple(places) for _, places in buffers), len(rows)))
        for buffer, _ in buffers:
            specs.append(pl.BlockSpec(buffer.shape, lambda col, place: (0, 0)))
            operands.append(buffer)
        if len(buffers) > 1:
            held.append(pltpu.VMEM(buffers[0][0].shape, jnp.bfloat16))
        for row in rows:
            specs.append(
                pl.BlockSpec((1, width, step), lambda col, place, row=row: (row(place[0]), 0, col))
            )
            operands.append(weight)
        depth += width * len(rows)
    tile = pl.BlockSpec((seq_len, step), lambda col, place: (0, col))
    if total is not None:
        specs.append(tile)
        operands.append(total)
    specs += [pl.BlockSpec(memory_space=pl.ANY)] * len(after)
    operands += list(after)
    if final:
        out_spec = pl.BlockSpec((1, seq_len, step), lambda col, place: (0, 0, col))
        out_shape = jax.ShapeDtypeStruct((1, seq_len, out_width), jnp.bfloat16)
    else:
        out_spec = tile
        out_shape = jax.ShapeDtypeStruct((seq_len, out_width), jnp.float32)
    return pl.pallas_call(
        functools.partial(project_kernel, tuple(kinds), total is None, final, len(after)),
        grid_spec=pltpu.PrefetchScalarGridSpec(
            num_scalar_prefetch=1,
            grid=(out_width // step,),
            in_specs=specs,
            out_specs=out_spec,
            scratch_shapes=held,
        ),
        out_shape=out_shape,
        compiler_params=pltpu.CompilerParams(vmem_limit_bytes=50 * 1024 * 1024),
        cost_estimate=pl.CostEstimate(
            flops=2 * seq_len * depth * out_width,
            bytes_accessed=2 * depth * (seq_len + out_width) + 8 * seq_len * out_width,
            transcendentals=0,
        ),
        name="project",
    )(place, *operands)


def join_kernel(left_ref, right_ref, *refs):
    out_ref = refs[-1]
    width = left_ref.shape[1]
    out_ref[:, :width] = left_ref[...]
    out_ref[:, width:] = right_ref[...]


def join(left, right, after):
    rows, width = left.shape
    spec = pl.BlockSpec((rows, width), lambda step: (0, 0))
    return pl.pallas_call(
        join_kernel,
        grid=(1,),
        in_specs=[spec, spec] + [pl.BlockSpec(memory_space=pl.ANY)] * len(after),
        out_specs=pl.BlockSpec((rows, 2 * width), lambda step: (0, 0)),
        out_shape=jax.ShapeDtypeStruct((rows, 2 * width), left.dtype),
        compiler_params=pltpu.CompilerParams(vmem_limit_bytes=8 * 1024 * 1024),
        cost_estimate=pl.CostEstimate(flops=0, bytes_accessed=8 * rows * width, transcendentals=0),
        name="join",
    )(left, right, *after)


def along_line(value, pairs):
    return lax.ppermute(value, "mp", pairs)


def on_device(queries, keys, values, out_weight, order_bias, partners, count, order):
    heads_dev = queries.shape[2] // HD
    group_size = HQ // KVH
    resp_total = lax.axis_size("resp")
    mp_total = lax.axis_size("mp")
    line = lax.axis_index("mp")
    first_head = line * heads_dev
    kv_head = (first_head // group_size).astype(jnp.int32)
    packed = pack(kv_head.reshape(1), keys, values)
    kv_blocks = gather_blocks(packed)
    where = jnp.stack([lax.axis_index("resp"), first_head]).astype(jnp.int32)
    place = line.astype(jnp.int32).reshape(1)

    def attended_of(head_base, heads, after=()):
        return attention(
            where, partners, count, order, order_bias, queries, kv_blocks, head_base, heads, resp_total, after
        )

    if mp_total != 4:
        gathered = lax.all_gather(attended_of(0, heads_dev), "mp", axis=0, tiled=False)
        weight = out_weight.reshape(mp_total, heads_dev * HD, out_weight.shape[1])
        parts = [
            ([(gathered[source], ())], [lambda at, source=source: source]) for source in range(mp_total)
        ]
        return project(place, None, parts, weight, True)

    chunks = 4
    chunk_heads = heads_dev // chunks
    weight = out_weight.reshape(mp_total * chunks, chunk_heads * HD, out_weight.shape[1])
    inner, outer = (1, 2), (0, 3)
    own, pair, joined, crossed, forwarded = [], [], [], [], []

    def cross(chunk, after):
        joined.append(join(own[chunk], pair[chunk], after))
        crossed.append(along_line(joined[chunk], [(1, 2), (2, 1)]))

    def forward(chunk, after):
        held = lax.optimization_barrier((crossed[chunk],) + after)[0]
        forwarded.append(along_line(held, [(1, 0), (2, 3)]))

    def own_part(chunk):
        return ([(own[chunk], ())], [lambda at: at * chunks + chunk])

    def pair_part(chunk):
        return ([(pair[chunk], ())], [lambda at: (at ^ 1) * chunks + chunk])

    def far_part(chunk):
        rows = [
            lambda at: jnp.where(at < 2, 2, 1) * chunks + chunk,
            lambda at: jnp.where(at < 2, 3, 0) * chunks + chunk,
        ]
        return ([(crossed[chunk], inner), (forwarded[chunk], outer)], rows)

    for chunk in range(chunks):
        after = tuple(joined[chunk - 2 : chunk - 1]) + tuple(crossed[chunk - 3 : chunk - 2])
        own.append(attended_of(chunk * chunk_heads, chunk_heads, after if chunk >= 2 else ()))
        pair.append(along_line(own[chunk], [(0, 1), (1, 0), (2, 3), (3, 2)]))
        if chunk >= 2:
            forward(chunk - 2, (own[chunk],))
        if chunk >= 1:
            cross(chunk - 1, (own[chunk],) + tuple(forwarded[chunk - 3 : chunk - 2]))
    parts = [own_part(chunk) for chunk in range(4)] + [pair_part(chunk) for chunk in range(3)]
    total = project(place, None, parts, weight, False, (joined[2], crossed[1]))
    cross(3, (total, forwarded[1]))
    forward(2, (total,))
    total = project(
        place, total, [pair_part(3), far_part(0), far_part(1)], weight, False, (joined[3], crossed[2])
    )
    forward(3, (total,))
    total = project(place, total, [far_part(2)], weight, False, (crossed[3],))
    return project(place, total, [far_part(3)], weight, True)


def solution(mesh):
    in_specs = (
        P("resp", None, "mp"),
        P("resp", None, None),
        P("resp", None, None),
        P(None, "mp"),
        P(),
        P("resp", None),
        P("resp"),
        P("resp", None),
    )
    out_specs = P("resp", None, "mp")
    return jax.shard_map(
        on_device, mesh=mesh, in_specs=in_specs, out_specs=out_specs, check_vma=False
    )
```

```python
import functools
import math

import jax
import jax.numpy as jnp
from jax import lax
from jax.experimental import pallas as pl
from jax.experimental.pallas import tpu as pltpu
from jax.sharding import PartitionSpec as P

HQ = 32
KVH = 4
HD = 128
REACH = 3
SLOTS = 6
OFFSETS = tuple(range(1, REACH + 1)) + tuple(-hop for hop in range(1, REACH + 1))
FLIPS = (1, 2, 3, 5, 6, 7)
BLOCKS = 1 + len(OFFSETS)
LOG2E = math.log2(math.e)
VMEM_BYTES = 60 * 1024 * 1024


def flipped(value, bits):
    count = lax.axis_size("resp")
    return lax.ppermute(value, "resp", [(source, source ^ bits) for source in range(count)])


def shifted(value, axis, steps):
    count = lax.axis_size(axis)
    pairs = [(source, (source + steps) % count) for source in range(count)]
    return lax.ppermute(value, axis, pairs)


def pack_kernel(head_ref, keys_ref, values_ref, out_ref):
    del head_ref
    for tile in range(keys_ref.shape[1] // HD):
        rows = slice(tile * HD, (tile + 1) * HD)
        out_ref[0, rows, :] = keys_ref[0, rows, :].T
    out_ref[1] = values_ref[0]


def pack(kv_head, keys, values):
    seq_len = keys.shape[1]
    spec = pl.BlockSpec((1, seq_len, HD), lambda step, head: (0, 0, head[0]))
    return pl.pallas_call(
        pack_kernel,
        grid_spec=pltpu.PrefetchScalarGridSpec(
            num_scalar_prefetch=1,
            grid=(1,),
            in_specs=[spec, spec],
            out_specs=pl.BlockSpec((2, seq_len, HD), lambda step, head: (0, 0, 0)),
        ),
        out_shape=jax.ShapeDtypeStruct((2, seq_len, HD), keys.dtype),
        compiler_params=pltpu.CompilerParams(vmem_limit_bytes=VMEM_BYTES),
        cost_estimate=pl.CostEstimate(flops=0, bytes_accessed=8 * seq_len * HD, transcendentals=0),
        name="pack",
    )(kv_head, keys, values)


def gather_blocks(packed):
    if lax.axis_size("resp") != 8:
        return [packed] + [shifted(packed, "resp", -offset) for offset in OFFSETS]
    far = flipped(packed, 6)
    along_x = flipped(packed, 2)
    along_y = flipped(packed, 4)
    twin = flipped(packed, 1)
    return [
        packed, twin, along_x, flipped(along_x, 1), flipped(along_y, 1), far, flipped(far, 1)
    ]


def target_of(resp_self, resp_total, block):
    if resp_total == 8:
        return resp_self ^ FLIPS[block - 1]
    return lax.rem(resp_self + OFFSETS[block - 1] + resp_total, resp_total)


def attention_kernel(
    head_base, resp_total, where_ref, partners_ref, count_ref, order_ref, bias_ref, q_ref, *rest
):
    kv_refs = rest[:BLOCKS]
    out_ref, scores_ref, expo_ref, peak_ref, total_ref = rest[-5:]
    unit, rows = scores_ref.shape[:2]
    seq_len = kv_refs[0].shape[1]
    scale = LOG2E / math.sqrt(HD)
    first_head = where_ref[1] + head_base + pl.program_id(0) * unit

    hits = []
    for block in range(1, BLOCKS):
        target = target_of(where_ref[0], resp_total, block)
        hits.append(
            [(slot < count_ref[0]) & (partners_ref[0, slot] == target) for slot in range(SLOTS)]
        )

    def bias_of(member, block):
        if block == 0:
            return jnp.float32(0.0)
        found = jnp.float32(-jnp.inf)
        for slot in range(SLOTS):
            offset = bias_ref[order_ref[0, slot], first_head + member] * LOG2E
            found = jnp.where(hits[block - 1][slot], offset, found)
        return found

    bias = [[bias_of(member, block) for block in range(BLOCKS)] for member in range(unit)]
    ones = jnp.ones((seq_len, HD), jnp.bfloat16)

    def cols(block):
        return slice(block * seq_len, (block + 1) * seq_len)

    def score(member, block):
        keys = jnp.concatenate(
            [kv_refs[block][0, tile : tile + HD, :] for tile in range(0, seq_len, HD)], axis=1
        )
        scores = jnp.dot(
            q_ref[0, :, member * HD : (member + 1) * HD], keys, preferred_element_type=jnp.float32
        )
        if block == 0:
            row_ids = lax.broadcasted_iota(jnp.int32, scores.shape, 0)
            col_ids = lax.broadcasted_iota(jnp.int32, scores.shape, 1)
            scores = jnp.where(row_ids >= col_ids, scores, -jnp.inf)
        scores_ref[member, :, cols(block)] = scores
        part = scores[:, :HD]
        for lane in range(HD, seq_len, HD):
            part = jnp.maximum(part, scores[:, lane : lane + HD])
        part = part * scale + bias[member][block]
        peak_ref[member] = part if block == 0 else jnp.maximum(peak_ref[member], part)

    def settle(member):
        peak = jnp.max(peak_ref[member], axis=1, keepdims=True)
        peak_ref[member] = jnp.broadcast_to(peak, (rows, HD))

    def expo(member, block):
        offset = bias[member][block] - peak_ref[member]
        scores = scores_ref[member, :, cols(block)]
        shift = jnp.concatenate([offset] * (seq_len // HD), axis=1)
        expo_ref[member, :, cols(block)] = jnp.exp2(scores * scale + shift).astype(jnp.bfloat16)

    def attend(member, block):
        if block % 2 == 1 or block == BLOCKS - 1:
            low = block - block % 2
            wide = jnp.concatenate(
                [
                    jnp.concatenate([kv_refs[held][1], ones], axis=1)
                    for held in range(low, block + 1)
                ],
                axis=0,
            )
            term = jnp.dot(
                expo_ref[member, :, low * seq_len : (block + 1) * seq_len],
                wide,
                preferred_element_type=jnp.float32,
            )
            total_ref[member] = term if low == 0 else total_ref[member] + term

    def finish(member):
        total = total_ref[member]
        out_ref[:, member * HD : (member + 1) * HD] = (total[:, :HD] / total[:, HD:]).astype(
            out_ref.dtype
        )

    for stage in range(unit + 2):
        for block in range(BLOCKS):
            if 0 <= stage - 2 < unit:
                attend(stage - 2, block)
            if 0 <= stage - 1 < unit:
                expo(stage - 1, block)
            if stage < unit:
                score(stage, block)
        if stage < unit:
            settle(stage)
        if 0 <= stage - 2 < unit:
            finish(stage - 2)


def attention(where, partners, count, order, order_bias, queries, kv_blocks, head_base, heads, resp_total, after=()):
    seq_len = queries.shape[1]
    unit = 2 if heads % 2 == 0 else 1
    smem = pl.BlockSpec(memory_space=pltpu.SMEM)
    whole = pl.BlockSpec(kv_blocks[0].shape, lambda step: (0, 0, 0))
    keys_all = BLOCKS * seq_len
    return pl.pallas_call(
        functools.partial(attention_kernel, head_base, resp_total),
        grid=(heads // unit,),
        in_specs=[smem] * 5
        + [pl.BlockSpec((1, seq_len, unit * HD), lambda step: (0, 0, head_base // unit + step))]
        + [whole] * BLOCKS
        + [pl.BlockSpec(memory_space=pl.ANY)] * len(after),
        out_specs=pl.BlockSpec((seq_len, unit * HD), lambda step: (0, step)),
        out_shape=jax.ShapeDtypeStruct((seq_len, heads * HD), jnp.bfloat16),
        scratch_shapes=[
            pltpu.VMEM((unit, seq_len, keys_all), jnp.float32),
            pltpu.VMEM((unit, seq_len, keys_all), jnp.bfloat16),
            pltpu.VMEM((unit, seq_len, HD), jnp.float32),
            pltpu.VMEM((unit, seq_len, 2 * HD), jnp.float32),
        ],
        compiler_params=pltpu.CompilerParams(vmem_limit_bytes=VMEM_BYTES),
        cost_estimate=pl.CostEstimate(
            flops=heads * seq_len * keys_all * HD * 6,
            bytes_accessed=2 * seq_len * HD * (2 * heads + 2 * BLOCKS),
            transcendentals=heads * seq_len * keys_all,
        ),
        name="attend",
    )(where, partners, count, order, order_bias, queries, *kv_blocks, *after)


def project_kernel(parts, start, final, waits, place_ref, weight_ref, *refs):
    inputs = refs[: sum(len(kinds) for kinds, _ in parts)]
    out_at = len(inputs) + waits + (0 if start else 1)
    out_ref, held_weight, sems, *held_refs = refs[out_at:]
    steps, _, step = held_weight.shape
    col = pl.program_id(0)
    place = place_ref[0]

    def copies(at):
        found, depth = [], 0
        for _, rows in parts:
            for first, count in rows:
                found.append(
                    pltpu.make_async_copy(
                        weight_ref.at[pl.ds(pl.multiple_of(first(place), HD), count), pl.ds(at * step, step)],
                        held_weight.at[at, pl.ds(depth, count), :],
                        sems.at[at, len(found)],
                    )
                )
                depth += count
        return found

    @pl.when(col == 0)
    def _():
        for at in range(steps):
            for copy in copies(at):
                copy.start()

    left = []
    taken = chosen = 0
    for kinds, _ in parts:
        if len(kinds) == 1:
            left.append(inputs[taken][...])
        else:
            held_ref = held_refs[chosen]
            chosen += 1
            for other, places in enumerate(kinds):
                wanted = functools.reduce(jnp.logical_or, [place == at for at in places])

                @pl.when((col == 0) & wanted)
                def _(source_ref=inputs[taken + other], held_ref=held_ref):
                    held_ref[...] = source_ref[...]

            left.append(held_ref[...])
        taken += len(kinds)
    for at in range(steps):

        @pl.when(col == at)
        def _(at=at):
            for copy in copies(at):
                copy.wait()

    total = jnp.dot(
        jnp.concatenate(left, axis=1), held_weight[col], preferred_element_type=jnp.float32
    )
    if not start:
        total = total + refs[len(inputs)][...]
    out_ref[...] = total.astype(out_ref.dtype)[None] if final else total


def project(place, total, parts, weight, final, after=()):
    seq_len = parts[0][0][0][0].shape[0]
    out_width = weight.shape[1]
    step = min(out_width, 512)
    specs, operands, kinds, held = [pl.BlockSpec(memory_space=pl.ANY)], [weight], [], []
    depth = runs = 0
    for buffers, rows in parts:
        kinds.append((tuple(tuple(places) for _, places in buffers), tuple(rows)))
        for buffer, _ in buffers:
            specs.append(pl.BlockSpec(buffer.shape, lambda col, place: (0, 0)))
            operands.append(buffer)
        if len(buffers) > 1:
            held.append(pltpu.VMEM(buffers[0][0].shape, jnp.bfloat16))
        depth += sum(count for _, count in rows)
        runs += len(rows)
    tile = pl.BlockSpec((seq_len, step), lambda col, place: (0, col))
    if total is not None:
        specs.append(tile)
        operands.append(total)
    specs += [pl.BlockSpec(memory_space=pl.ANY)] * len(after)
    operands += list(after)
    if final:
        out_spec = pl.BlockSpec((1, seq_len, step), lambda col, place: (0, 0, col))
        out_shape = jax.ShapeDtypeStruct((1, seq_len, out_width), jnp.bfloat16)
    else:
        out_spec = tile
        out_shape = jax.ShapeDtypeStruct((seq_len, out_width), jnp.float32)
    steps = out_width // step
    return pl.pallas_call(
        functools.partial(project_kernel, tuple(kinds), total is None, final, len(after)),
        grid_spec=pltpu.PrefetchScalarGridSpec(
            num_scalar_prefetch=1,
            grid=(steps,),
            in_specs=specs,
            out_specs=out_spec,
            scratch_shapes=[
                pltpu.VMEM((steps, depth, step), weight.dtype),
                pltpu.SemaphoreType.DMA((steps, runs)),
            ]
            + held,
        ),
        out_shape=out_shape,
        compiler_params=pltpu.CompilerParams(vmem_limit_bytes=50 * 1024 * 1024),
        cost_estimate=pl.CostEstimate(
            flops=2 * seq_len * depth * out_width,
            bytes_accessed=2 * depth * (seq_len + out_width) + 8 * seq_len * out_width,
            transcendentals=0,
        ),
        name="project",
    )(place, *operands)


def join_kernel(left_ref, right_ref, *refs):
    out_ref = refs[-1]
    width = left_ref.shape[1]
    out_ref[:, :width] = left_ref[...]
    out_ref[:, width:] = right_ref[...]


def join(left, right, after):
    rows, width = left.shape
    spec = pl.BlockSpec((rows, width), lambda step: (0, 0))
    return pl.pallas_call(
        join_kernel,
        grid=(1,),
        in_specs=[spec, spec] + [pl.BlockSpec(memory_space=pl.ANY)] * len(after),
        out_specs=pl.BlockSpec((rows, 2 * width), lambda step: (0, 0)),
        out_shape=jax.ShapeDtypeStruct((rows, 2 * width), left.dtype),
        compiler_params=pltpu.CompilerParams(vmem_limit_bytes=8 * 1024 * 1024),
        cost_estimate=pl.CostEstimate(flops=0, bytes_accessed=8 * rows * width, transcendentals=0),
        name="join",
    )(left, right, *after)


def along_line(value, pairs):
    return lax.ppermute(value, "mp", pairs)


def on_device(queries, keys, values, out_weight, order_bias, partners, count, order):
    heads_dev = queries.shape[2] // HD
    group_size = HQ // KVH
    resp_total = lax.axis_size("resp")
    mp_total = lax.axis_size("mp")
    line = lax.axis_index("mp")
    first_head = line * heads_dev
    kv_head = (first_head // group_size).astype(jnp.int32)
    packed = pack(kv_head.reshape(1), keys, values)
    kv_blocks = gather_blocks(packed)
    where = jnp.stack([lax.axis_index("resp"), first_head]).astype(jnp.int32)
    place = line.astype(jnp.int32).reshape(1)

    def attended_of(head_base, heads, after=()):
        return attention(
            where, partners, count, order, order_bias, queries, kv_blocks, head_base, heads, resp_total, after
        )

    device_rows = heads_dev * HD
    if mp_total != 4 or heads_dev % 4:
        gathered = lax.all_gather(attended_of(0, heads_dev), "mp", axis=0, tiled=False)
        parts = [
            ([(gathered[source], ())], [(lambda at, source=source: source * device_rows, device_rows)])
            for source in range(mp_total)
        ]
        return project(place, None, parts, out_weight, True)

    chunks = 4
    chunk_heads = heads_dev // chunks
    rows = chunk_heads * HD
    inner, outer = (1, 2), (0, 3)

    def held_until(value, *after):
        return lax.optimization_barrier((value,) + after)[0]

    def exchange(value):
        return along_line(value, [(0, 1), (1, 0), (2, 3), (3, 2)])

    def cross(value):
        return along_line(value, [(1, 2), (2, 1)])

    def forward(value):
        return along_line(value, [(1, 0), (2, 3)])

    def run_of(source, chunk):
        return (lambda at: source(at) * device_rows + chunk * rows, rows)

    def own_part(chunk):
        return ([(own[chunk], ())], [run_of(lambda at: at, chunk)])

    def pair_part(chunk):
        return ([(pair[chunk], ())], [run_of(lambda at: at ^ 1, chunk)])

    near = lambda at: jnp.where(at < 2, 2, 1)
    far = lambda at: jnp.where(at < 2, 3, 0)

    def near_part(chunk):
        return ([(near_in[chunk], inner), (near_out[chunk], outer)], [run_of(near, chunk)])

    def far_part(chunk):
        return ([(far_in[chunk], inner), (far_out[chunk], outer)], [run_of(far, chunk)])

    def both_part(chunk):
        return (
            [(both_in[chunk], inner), (both_out[chunk], outer)], [run_of(near, chunk), run_of(far, chunk)]
        )

    own, pair = [None] * chunks, [None] * chunks
    near_in, near_out, far_in, far_out, both_in, both_out = ({} for _ in range(6))

    def attend_chunk(chunk, *after):
        own[chunk] = attended_of(chunk * chunk_heads, chunk_heads, after)

    attend_chunk(0)
    pair[0] = exchange(own[0])
    near_in[0] = cross(own[0])
    attend_chunk(1)
    far_in[0] = cross(held_until(pair[0], own[1]))
    near_out[0] = forward(held_until(near_in[0], own[1]))
    pair[1] = exchange(own[1])
    near_in[1] = cross(own[1])
    attend_chunk(2)
    far_out[0] = forward(held_until(far_in[0], own[2]))
    far_in[1] = cross(held_until(pair[1], own[2]))
    near_out[1] = forward(held_until(near_in[1], own[2]))
    pair[2] = exchange(own[2])
    attend_chunk(3, near_out[0])
    both_in[2] = cross(join(own[2], pair[2], (own[3],)))
    far_out[1] = forward(held_until(far_in[1], own[3]))
    pair[3] = exchange(own[3])
    total = project(
        place,
        None,
        [own_part(chunk) for chunk in range(4)]
        + [pair_part(chunk) for chunk in range(3)]
        + [near_part(0), far_part(0), near_part(1)],
        out_weight,
        False,
    )
    both_in[3] = cross(join(own[3], pair[3], (total, far_out[1])))
    both_out[2] = forward(held_until(both_in[2], total))
    total = project(
        place, total, [pair_part(3), far_part(1)], out_weight, False
    )
    both_out[3] = forward(held_until(both_in[3], total))
    total = project(place, total, [both_part(2)], out_weight, False, (both_in[3],))
    return project(place, total, [both_part(3)], out_weight, True)


def solution(mesh):
    in_specs = (
        P("resp", None, "mp"),
        P("resp", None, None),
        P("resp", None, None),
        P(None, "mp"),
        P(),
        P("resp", None),
        P("resp"),
        P("resp", None),
    )
    out_specs = P("resp", None, "mp")
    return jax.shard_map(
        on_device, mesh=mesh, in_specs=in_specs, out_specs=out_specs, check_vma=False
    )
```

```python
import functools
import math

import jax
import jax.numpy as jnp
from jax import lax
from jax.experimental import pallas as pl
from jax.experimental.pallas import tpu as pltpu
from jax.sharding import PartitionSpec as P

HQ = 32
KVH = 4
HD = 128
REACH = 3
SLOTS = 6
OFFSETS = tuple(range(1, REACH + 1)) + tuple(-hop for hop in range(1, REACH + 1))
FLIPS = (1, 2, 3, 5, 6, 7)
BLOCKS = 1 + len(OFFSETS)
LOG2E = math.log2(math.e)
VMEM_BYTES = 60 * 1024 * 1024


def flipped(value, bits):
    count = lax.axis_size("resp")
    return lax.ppermute(value, "resp", [(source, source ^ bits) for source in range(count)])


def shifted(value, axis, steps):
    count = lax.axis_size(axis)
    pairs = [(source, (source + steps) % count) for source in range(count)]
    return lax.ppermute(value, axis, pairs)


def pack_kernel(head_ref, keys_ref, values_ref, out_ref):
    del head_ref
    for tile in range(keys_ref.shape[1] // HD):
        rows = slice(tile * HD, (tile + 1) * HD)
        out_ref[0, rows, :] = keys_ref[0, rows, :].T
    out_ref[1] = values_ref[0]


def pack(kv_head, keys, values):
    seq_len = keys.shape[1]
    spec = pl.BlockSpec((1, seq_len, HD), lambda step, head: (0, 0, head[0]))
    return pl.pallas_call(
        pack_kernel,
        grid_spec=pltpu.PrefetchScalarGridSpec(
            num_scalar_prefetch=1,
            grid=(1,),
            in_specs=[spec, spec],
            out_specs=pl.BlockSpec((2, seq_len, HD), lambda step, head: (0, 0, 0)),
        ),
        out_shape=jax.ShapeDtypeStruct((2, seq_len, HD), keys.dtype),
        compiler_params=pltpu.CompilerParams(vmem_limit_bytes=VMEM_BYTES),
        cost_estimate=pl.CostEstimate(flops=0, bytes_accessed=8 * seq_len * HD, transcendentals=0),
        name="pack",
    )(kv_head, keys, values)


def gather_blocks(packed):
    if lax.axis_size("resp") != 8:
        return [packed] + [shifted(packed, "resp", -offset) for offset in OFFSETS]
    far = flipped(packed, 6)
    along_x = flipped(packed, 2)
    along_y = flipped(packed, 4)
    twin = flipped(packed, 1)
    return [
        packed, twin, along_x, flipped(along_x, 1), flipped(along_y, 1), far, flipped(far, 1)
    ]


def target_of(resp_self, resp_total, block):
    if resp_total == 8:
        return resp_self ^ FLIPS[block - 1]
    return lax.rem(resp_self + OFFSETS[block - 1] + resp_total, resp_total)


def attention_kernel(
    head_base, resp_total, where_ref, partners_ref, count_ref, order_ref, bias_ref, q_ref, *rest
):
    kv_refs = rest[:BLOCKS]
    out_ref, scores_ref, expo_ref, peak_ref, total_ref = rest[-5:]
    unit, rows = scores_ref.shape[:2]
    seq_len = kv_refs[0].shape[1]
    scale = LOG2E / math.sqrt(HD)
    first_head = where_ref[1] + head_base + pl.program_id(0) * unit

    hits = []
    for block in range(1, BLOCKS):
        target = target_of(where_ref[0], resp_total, block)
        hits.append(
            [(slot < count_ref[0]) & (partners_ref[0, slot] == target) for slot in range(SLOTS)]
        )

    def bias_of(member, block):
        if block == 0:
            return jnp.float32(0.0)
        found = jnp.float32(-jnp.inf)
        for slot in range(SLOTS):
            offset = bias_ref[order_ref[0, slot], first_head + member] * LOG2E
            found = jnp.where(hits[block - 1][slot], offset, found)
        return found

    bias = [[bias_of(member, block) for block in range(BLOCKS)] for member in range(unit)]
    ones = jnp.ones((seq_len, HD), jnp.bfloat16)

    def cols(block):
        return slice(block * seq_len, (block + 1) * seq_len)

    def score(member, block):
        keys = jnp.concatenate(
            [kv_refs[block][0, tile : tile + HD, :] for tile in range(0, seq_len, HD)], axis=1
        )
        scores = jnp.dot(
            q_ref[0, :, member * HD : (member + 1) * HD], keys, preferred_element_type=jnp.float32
        )
        if block == 0:
            row_ids = lax.broadcasted_iota(jnp.int32, scores.shape, 0)
            col_ids = lax.broadcasted_iota(jnp.int32, scores.shape, 1)
            scores = jnp.where(row_ids >= col_ids, scores, -jnp.inf)
        scores_ref[member, :, cols(block)] = scores
        part = scores[:, :HD]
        for lane in range(HD, seq_len, HD):
            part = jnp.maximum(part, scores[:, lane : lane + HD])
        part = part * scale + bias[member][block]
        peak_ref[member] = part if block == 0 else jnp.maximum(peak_ref[member], part)

    def settle(member):
        peak = jnp.max(peak_ref[member], axis=1, keepdims=True)
        peak_ref[member] = jnp.broadcast_to(peak, (rows, HD))

    def expo(member, block):
        offset = bias[member][block] - peak_ref[member]
        scores = scores_ref[member, :, cols(block)]
        shift = jnp.concatenate([offset] * (seq_len // HD), axis=1)
        expo_ref[member, :, cols(block)] = jnp.exp2(scores * scale + shift).astype(jnp.bfloat16)

    def attend(member, block):
        if block % 2 == 1 or block == BLOCKS - 1:
            low = block - block % 2
            wide = jnp.concatenate(
                [
                    jnp.concatenate([kv_refs[held][1], ones], axis=1)
                    for held in range(low, block + 1)
                ],
                axis=0,
            )
            term = jnp.dot(
                expo_ref[member, :, low * seq_len : (block + 1) * seq_len],
                wide,
                preferred_element_type=jnp.float32,
            )
            total_ref[member] = term if low == 0 else total_ref[member] + term

    def finish(member):
        total = total_ref[member]
        out_ref[:, member * HD : (member + 1) * HD] = (total[:, :HD] / total[:, HD:]).astype(
            out_ref.dtype
        )

    for stage in range(unit + 2):
        for block in range(BLOCKS):
            if 0 <= stage - 2 < unit:
                attend(stage - 2, block)
            if 0 <= stage - 1 < unit:
                expo(stage - 1, block)
            if stage < unit:
                score(stage, block)
        if stage < unit:
            settle(stage)
        if 0 <= stage - 2 < unit:
            finish(stage - 2)


def attention(where, partners, count, order, order_bias, queries, kv_blocks, head_base, heads, resp_total, after=()):
    seq_len = queries.shape[1]
    unit = 2 if heads % 2 == 0 else 1
    smem = pl.BlockSpec(memory_space=pltpu.SMEM)
    whole = pl.BlockSpec(kv_blocks[0].shape, lambda step: (0, 0, 0))
    keys_all = BLOCKS * seq_len
    return pl.pallas_call(
        functools.partial(attention_kernel, head_base, resp_total),
        grid=(heads // unit,),
        in_specs=[smem] * 5
        + [pl.BlockSpec((1, seq_len, unit * HD), lambda step: (0, 0, head_base // unit + step))]
        + [whole] * BLOCKS
        + [pl.BlockSpec(memory_space=pl.ANY)] * len(after),
        out_specs=pl.BlockSpec((seq_len, unit * HD), lambda step: (0, step)),
        out_shape=jax.ShapeDtypeStruct((seq_len, heads * HD), jnp.bfloat16),
        scratch_shapes=[
            pltpu.VMEM((unit, seq_len, keys_all), jnp.float32),
            pltpu.VMEM((unit, seq_len, keys_all), jnp.bfloat16),
            pltpu.VMEM((unit, seq_len, HD), jnp.float32),
            pltpu.VMEM((unit, seq_len, 2 * HD), jnp.float32),
        ],
        compiler_params=pltpu.CompilerParams(vmem_limit_bytes=VMEM_BYTES),
        cost_estimate=pl.CostEstimate(
            flops=heads * seq_len * keys_all * HD * 6,
            bytes_accessed=2 * seq_len * HD * (2 * heads + 2 * BLOCKS),
            transcendentals=heads * seq_len * keys_all,
        ),
        name="attend",
    )(where, partners, count, order, order_bias, queries, *kv_blocks, *after)


def project_kernel(parts, start, final, waits, place_ref, *refs):
    inputs = refs[: sum(len(kinds) + rows for kinds, rows in parts)]
    out_at = len(inputs) + waits + (0 if start else 1)
    out_ref, held_refs = refs[out_at], refs[out_at + 1 :]
    left, right = [], []
    taken = chosen = 0
    for kinds, rows in parts:
        if len(kinds) == 1:
            left.append(inputs[taken][...])
        else:
            held_ref = held_refs[chosen]
            chosen += 1
            for other, places in enumerate(kinds):
                wanted = functools.reduce(jnp.logical_or, [place_ref[0] == at for at in places])

                @pl.when((pl.program_id(0) == 0) & wanted)
                def _(source_ref=inputs[taken + other]):
                    held_ref[...] = source_ref[...]

            left.append(held_ref[...])
        taken += len(kinds)
        for _ in range(rows):
            right.append(inputs[taken][0])
            taken += 1
    total = jnp.dot(
        jnp.concatenate(left, axis=1),
        jnp.concatenate(right, axis=0),
        preferred_element_type=jnp.float32,
    )
    if not start:
        total = total + refs[len(inputs)][...]
    out_ref[...] = total.astype(out_ref.dtype)[None] if final else total


def project(place, total, parts, weight, final, after=()):
    seq_len = parts[0][0][0][0].shape[0]
    width, out_width = weight.shape[1:]
    step = min(out_width, 512)
    specs, operands, kinds, held = [], [], [], []
    depth = 0
    for buffers, rows in parts:
        kinds.append((tuple(tuple(places) for _, places in buffers), len(rows)))
        for buffer, _ in buffers:
            specs.append(pl.BlockSpec(buffer.shape, lambda col, place: (0, 0)))
            operands.append(buffer)
        if len(buffers) > 1:
            held.append(pltpu.VMEM(buffers[0][0].shape, jnp.bfloat16))
        for row in rows:
            specs.append(
                pl.BlockSpec((1, width, step), lambda col, place, row=row: (row(place[0]), 0, col))
            )
            operands.append(weight)
        depth += width * len(rows)
    tile = pl.BlockSpec((seq_len, step), lambda col, place: (0, col))
    if total is not None:
        specs.append(tile)
        operands.append(total)
    specs += [pl.BlockSpec(memory_space=pl.ANY)] * len(after)
    operands += list(after)
    if final:
        out_spec = pl.BlockSpec((1, seq_len, step), lambda col, place: (0, 0, col))
        out_shape = jax.ShapeDtypeStruct((1, seq_len, out_width), jnp.bfloat16)
    else:
        out_spec = tile
        out_shape = jax.ShapeDtypeStruct((seq_len, out_width), jnp.float32)
    return pl.pallas_call(
        functools.partial(project_kernel, tuple(kinds), total is None, final, len(after)),
        grid_spec=pltpu.PrefetchScalarGridSpec(
            num_scalar_prefetch=1,
            grid=(out_width // step,),
            in_specs=specs,
            out_specs=out_spec,
            scratch_shapes=held,
        ),
        out_shape=out_shape,
        compiler_params=pltpu.CompilerParams(vmem_limit_bytes=(50 if final else 60) * 1024 * 1024),
        cost_estimate=pl.CostEstimate(
            flops=2 * seq_len * depth * out_width,
            bytes_accessed=2 * depth * (seq_len + out_width) + 8 * seq_len * out_width,
            transcendentals=0,
        ),
        name="project",
    )(place, *operands)


def join_kernel(left_ref, right_ref, *refs):
    out_ref = refs[-1]
    width = left_ref.shape[1]
    out_ref[:, :width] = left_ref[...]
    out_ref[:, width:] = right_ref[...]


def join(left, right, after):
    rows, width = left.shape
    spec = pl.BlockSpec((rows, width), lambda step: (0, 0))
    return pl.pallas_call(
        join_kernel,
        grid=(1,),
        in_specs=[spec, spec] + [pl.BlockSpec(memory_space=pl.ANY)] * len(after),
        out_specs=pl.BlockSpec((rows, 2 * width), lambda step: (0, 0)),
        out_shape=jax.ShapeDtypeStruct((rows, 2 * width), left.dtype),
        compiler_params=pltpu.CompilerParams(vmem_limit_bytes=8 * 1024 * 1024),
        cost_estimate=pl.CostEstimate(flops=0, bytes_accessed=8 * rows * width, transcendentals=0),
        name="join",
    )(left, right, *after)


def along_line(value, pairs):
    return lax.ppermute(value, "mp", pairs)


def on_device(queries, keys, values, out_weight, order_bias, partners, count, order):
    heads_dev = queries.shape[2] // HD
    group_size = HQ // KVH
    resp_total = lax.axis_size("resp")
    mp_total = lax.axis_size("mp")
    line = lax.axis_index("mp")
    first_head = line * heads_dev
    kv_head = (first_head // group_size).astype(jnp.int32)
    packed = pack(kv_head.reshape(1), keys, values)
    kv_blocks = gather_blocks(packed)
    where = jnp.stack([lax.axis_index("resp"), first_head]).astype(jnp.int32)
    place = line.astype(jnp.int32).reshape(1)

    def attended_of(head_base, heads, after=()):
        return attention(
            where, partners, count, order, order_bias, queries, kv_blocks, head_base, heads, resp_total, after
        )

    if mp_total != 4:
        gathered = lax.all_gather(attended_of(0, heads_dev), "mp", axis=0, tiled=False)
        weight = out_weight.reshape(mp_total, heads_dev * HD, out_weight.shape[1])
        parts = [
            ([(gathered[source], ())], [lambda at, source=source: source]) for source in range(mp_total)
        ]
        return project(place, None, parts, weight, True)

    chunks = 4
    chunk_heads = heads_dev // chunks
    weight = out_weight.reshape(mp_total * chunks, chunk_heads * HD, out_weight.shape[1])
    inner, outer = (1, 2), (0, 3)
    own, pair, joined, crossed, forwarded = [], [], [], [], []

    def held_until(value, *after):
        return lax.optimization_barrier((value,) + after)[0]

    def attend_chunk(*after):
        chunk = len(own)
        own.append(attended_of(chunk * chunk_heads, chunk_heads, after))

    def exchange():
        pair.append(along_line(own[-1], [(0, 1), (1, 0), (2, 3), (3, 2)]))

    def cross(*after):
        chunk = len(joined)
        joined.append(join(own[chunk], pair[chunk], after))
        crossed.append(along_line(joined[chunk], [(1, 2), (2, 1)]))

    def forward(*after):
        held = held_until(crossed[len(forwarded)], *after)
        forwarded.append(along_line(held, [(1, 0), (2, 3)]))

    def own_part(chunk):
        return ([(own[chunk], ())], [lambda at: at * chunks + chunk])

    def pair_part(chunk):
        return ([(pair[chunk], ())], [lambda at: (at ^ 1) * chunks + chunk])

    def far_part(chunk):
        rows = [
            lambda at: jnp.where(at < 2, 2, 1) * chunks + chunk,
            lambda at: jnp.where(at < 2, 3, 0) * chunks + chunk,
        ]
        return ([(crossed[chunk], inner), (forwarded[chunk], outer)], rows)

    attend_chunk()
    exchange()
    attend_chunk()
    cross(own[1])
    exchange()
    attend_chunk(joined[0])
    cross(own[2])
    exchange()
    forward(own[2])
    attend_chunk(joined[1], crossed[0])
    exchange()
    cross(own[3])
    forward(joined[2])
    parts = [own_part(chunk) for chunk in range(4)] + [pair_part(chunk) for chunk in range(3)]
    total = project(place, None, parts + [far_part(0)], weight, False, (joined[2],))
    cross(total)
    forward(joined[3])
    total = project(place, total, [pair_part(3), far_part(1)], weight, False, (joined[3], crossed[2]))
    forward(total)
    total = project(place, total, [far_part(2)], weight, False, (crossed[3],))
    return project(place, total, [far_part(3)], weight, True)


def solution(mesh):
    in_specs = (
        P("resp", None, "mp"),
        P("resp", None, None),
        P("resp", None, None),
        P(None, "mp"),
        P(),
        P("resp", None),
        P("resp"),
        P("resp", None),
    )
    out_specs = P("resp", None, "mp")
    return jax.shard_map(
        on_device, mesh=mesh, in_specs=in_specs, out_specs=out_specs, check_vma=False
    )
```

```python
import functools
import math

import jax
import jax.numpy as jnp
from jax import lax
from jax.experimental import pallas as pl
from jax.experimental.pallas import tpu as pltpu
from jax.sharding import PartitionSpec as P

HQ = 32
KVH = 4
HD = 128
REACH = 3
SLOTS = 6
OFFSETS = tuple(range(1, REACH + 1)) + tuple(-hop for hop in range(1, REACH + 1))
FLIPS = (1, 2, 3, 5, 6, 7)
BLOCKS = 1 + len(OFFSETS)
LOG2E = math.log2(math.e)
VMEM_BYTES = 60 * 1024 * 1024


def flipped(value, bits):
    count = lax.axis_size("resp")
    return lax.ppermute(value, "resp", [(source, source ^ bits) for source in range(count)])


def shifted(value, axis, steps):
    count = lax.axis_size(axis)
    pairs = [(source, (source + steps) % count) for source in range(count)]
    return lax.ppermute(value, axis, pairs)


def pack_kernel(head_ref, keys_ref, values_ref, out_ref):
    del head_ref
    for tile in range(keys_ref.shape[1] // HD):
        rows = slice(tile * HD, (tile + 1) * HD)
        out_ref[0, rows, :] = keys_ref[0, rows, :].T
    out_ref[1] = values_ref[0]


def pack(kv_head, keys, values):
    seq_len = keys.shape[1]
    spec = pl.BlockSpec((1, seq_len, HD), lambda step, head: (0, 0, head[0]))
    return pl.pallas_call(
        pack_kernel,
        grid_spec=pltpu.PrefetchScalarGridSpec(
            num_scalar_prefetch=1,
            grid=(1,),
            in_specs=[spec, spec],
            out_specs=pl.BlockSpec((2, seq_len, HD), lambda step, head: (0, 0, 0)),
        ),
        out_shape=jax.ShapeDtypeStruct((2, seq_len, HD), keys.dtype),
        compiler_params=pltpu.CompilerParams(vmem_limit_bytes=VMEM_BYTES),
        cost_estimate=pl.CostEstimate(flops=0, bytes_accessed=8 * seq_len * HD, transcendentals=0),
        name="pack",
    )(kv_head, keys, values)


def gather_blocks(packed):
    if lax.axis_size("resp") != 8:
        return [packed] + [shifted(packed, "resp", -offset) for offset in OFFSETS]
    far = flipped(packed, 6)
    along_x = flipped(packed, 2)
    along_y = flipped(packed, 4)
    twin = flipped(packed, 1)
    return [
        packed, twin, along_x, flipped(along_x, 1), flipped(along_y, 1), far, flipped(far, 1)
    ]


def target_of(resp_self, resp_total, block):
    if resp_total == 8:
        return resp_self ^ FLIPS[block - 1]
    return lax.rem(resp_self + OFFSETS[block - 1] + resp_total, resp_total)


def attention_kernel(
    head_base, resp_total, where_ref, partners_ref, count_ref, order_ref, bias_ref, q_ref, *rest
):
    kv_in, out_ref = rest[:BLOCKS], rest[BLOCKS]
    held_q, kv_refs, scores_ref, expo_ref, peak_ref, total_ref, sems = rest[BLOCKS + 1 :]
    unit, rows = total_ref.shape[:2]
    seq_len = kv_refs.shape[2]
    scale = LOG2E / math.sqrt(HD)
    first_head = where_ref[1] + head_base
    copies = [
        pltpu.make_async_copy(
            q_ref.at[0, :, pl.ds(head_base * HD, unit * HD)], held_q, sems.at[BLOCKS]
        )
    ]
    for block in range(BLOCKS):
        copies.append(pltpu.make_async_copy(kv_in[block], kv_refs.at[block], sems.at[block]))
    for copy in copies:
        copy.start()

    hits = []
    for block in range(1, BLOCKS):
        target = target_of(where_ref[0], resp_total, block)
        hits.append(
            [(slot < count_ref[0]) & (partners_ref[0, slot] == target) for slot in range(SLOTS)]
        )

    def bias_of(member, block):
        if block == 0:
            return jnp.float32(0.0)
        found = jnp.float32(-jnp.inf)
        for slot in range(SLOTS):
            offset = bias_ref[order_ref[0, slot], first_head + member] * LOG2E
            found = jnp.where(hits[block - 1][slot], offset, found)
        return found

    bias = [[bias_of(member, block) for block in range(BLOCKS)] for member in range(unit)]
    ones = jnp.ones((seq_len, HD), jnp.bfloat16)

    def cols(block):
        return slice(block * seq_len, (block + 1) * seq_len)

    def score(member, block):
        if member == 0:
            if block == 0:
                copies[0].wait()
            copies[block + 1].wait()
        keys = jnp.concatenate(
            [kv_refs[block, 0, tile : tile + HD, :] for tile in range(0, seq_len, HD)], axis=1
        )
        scores = jnp.dot(
            held_q[:, member * HD : (member + 1) * HD], keys, preferred_element_type=jnp.float32
        )
        if block == 0:
            row_ids = lax.broadcasted_iota(jnp.int32, scores.shape, 0)
            col_ids = lax.broadcasted_iota(jnp.int32, scores.shape, 1)
            scores = jnp.where(row_ids >= col_ids, scores, -jnp.inf)
        scores_ref[member, :, cols(block)] = scores
        part = scores[:, :HD]
        for lane in range(HD, seq_len, HD):
            part = jnp.maximum(part, scores[:, lane : lane + HD])
        part = part * scale + bias[member][block]
        peak_ref[member] = part if block == 0 else jnp.maximum(peak_ref[member], part)

    def settle(member):
        peak = jnp.max(peak_ref[member], axis=1, keepdims=True)
        peak_ref[member] = jnp.broadcast_to(peak, (rows, HD))

    def expo(member, block):
        offset = bias[member][block] - peak_ref[member]
        scores = scores_ref[member, :, cols(block)]
        shift = jnp.concatenate([offset] * (seq_len // HD), axis=1)
        expo_ref[member, :, cols(block)] = jnp.exp2(scores * scale + shift).astype(jnp.bfloat16)

    def attend(member, block):
        if block % 2 == 1 or block == BLOCKS - 1:
            low = block - block % 2
            wide = jnp.concatenate(
                [
                    jnp.concatenate([kv_refs[held, 1], ones], axis=1)
                    for held in range(low, block + 1)
                ],
                axis=0,
            )
            term = jnp.dot(
                expo_ref[member, :, low * seq_len : (block + 1) * seq_len],
                wide,
                preferred_element_type=jnp.float32,
            )
            total_ref[member] = term if low == 0 else total_ref[member] + term

    def finish(member):
        total = total_ref[member]
        out_ref[:, member * HD : (member + 1) * HD] = (total[:, :HD] / total[:, HD:]).astype(
            out_ref.dtype
        )

    for stage in range(unit + 2):
        for block in range(BLOCKS):
            if 0 <= stage - 2 < unit:
                attend(stage - 2, block)
            if 0 <= stage - 1 < unit:
                expo(stage - 1, block)
            if stage < unit:
                score(stage, block)
        if stage < unit:
            settle(stage)
        if 0 <= stage - 2 < unit:
            finish(stage - 2)


def attention(where, partners, count, order, order_bias, queries, kv_blocks, head_base, heads, resp_total):
    seq_len = queries.shape[1]
    smem = pl.BlockSpec(memory_space=pltpu.SMEM)
    there = pl.BlockSpec(memory_space=pl.ANY)
    keys_all = BLOCKS * seq_len
    return pl.pallas_call(
        functools.partial(attention_kernel, head_base, resp_total),
        in_specs=[smem] * 5 + [there] * (1 + BLOCKS),
        out_specs=pl.BlockSpec(memory_space=pltpu.VMEM),
        out_shape=jax.ShapeDtypeStruct((seq_len, heads * HD), jnp.bfloat16),
        scratch_shapes=[
            pltpu.VMEM((seq_len, heads * HD), jnp.bfloat16),
            pltpu.VMEM((BLOCKS,) + kv_blocks[0].shape, jnp.bfloat16),
            pltpu.VMEM((heads, seq_len, keys_all), jnp.float32),
            pltpu.VMEM((heads, seq_len, keys_all), jnp.bfloat16),
            pltpu.VMEM((heads, seq_len, HD), jnp.float32),
            pltpu.VMEM((heads, seq_len, 2 * HD), jnp.float32),
            pltpu.SemaphoreType.DMA((BLOCKS + 1,)),
        ],
        compiler_params=pltpu.CompilerParams(vmem_limit_bytes=VMEM_BYTES),
        cost_estimate=pl.CostEstimate(
            flops=heads * seq_len * keys_all * HD * 6,
            bytes_accessed=2 * seq_len * HD * (2 * heads + 2 * BLOCKS),
            transcendentals=heads * seq_len * keys_all,
        ),
        name="attend",
    )(where, partners, count, order, order_bias, queries, *kv_blocks)


def project_kernel(parts, start, final, place_ref, *refs):
    inputs = refs[: sum(len(kinds) + rows for kinds, rows in parts)]
    out_at = len(inputs) + (0 if start else 1)
    out_ref, held_refs = refs[out_at], refs[out_at + 1 :]
    left, right = [], []
    taken = chosen = 0
    for kinds, rows in parts:
        if len(kinds) == 1:
            left.append(inputs[taken][...])
        else:
            held_ref = held_refs[chosen]
            chosen += 1
            for other, places in enumerate(kinds):
                wanted = functools.reduce(jnp.logical_or, [place_ref[0] == at for at in places])

                @pl.when((pl.program_id(0) == 0) & wanted)
                def _(source_ref=inputs[taken + other]):
                    held_ref[...] = source_ref[...]

            left.append(held_ref[...])
        taken += len(kinds)
        for _ in range(rows):
            right.append(inputs[taken][0])
            taken += 1
    total = jnp.dot(
        jnp.concatenate(left, axis=1),
        jnp.concatenate(right, axis=0),
        preferred_element_type=jnp.float32,
    )
    if not start:
        total = total + refs[len(inputs)][...]
    out_ref[...] = total.astype(out_ref.dtype)[None] if final else total


def project(place, total, parts, weight, final):
    seq_len = parts[0][0][0][0].shape[0]
    width, out_width = weight.shape[1:]
    step = min(out_width, 512)
    specs, operands, kinds, held = [], [], [], []
    depth = 0
    for buffers, rows in parts:
        kinds.append((tuple(tuple(places) for _, places in buffers), len(rows)))
        for buffer, _ in buffers:
            specs.append(pl.BlockSpec(buffer.shape, lambda col, place: (0, 0)))
            operands.append(buffer)
        if len(buffers) > 1:
            held.append(pltpu.VMEM(buffers[0][0].shape, jnp.bfloat16))
        for row in rows:
            specs.append(
                pl.BlockSpec((1, width, step), lambda col, place, row=row: (row(place[0]), 0, col))
            )
            operands.append(weight)
        depth += width * len(rows)
    tile = pl.BlockSpec((seq_len, step), lambda col, place: (0, col))
    if total is not None:
        specs.append(tile)
        operands.append(total)
    if final:
        out_spec = pl.BlockSpec((1, seq_len, step), lambda col, place: (0, 0, col))
        out_shape = jax.ShapeDtypeStruct((1, seq_len, out_width), jnp.bfloat16)
    else:
        out_spec = tile
        out_shape = jax.ShapeDtypeStruct((seq_len, out_width), jnp.float32)
    return pl.pallas_call(
        functools.partial(project_kernel, tuple(kinds), total is None, final),
        grid_spec=pltpu.PrefetchScalarGridSpec(
            num_scalar_prefetch=1,
            grid=(out_width // step,),
            in_specs=specs,
            out_specs=out_spec,
            scratch_shapes=held,
        ),
        out_shape=out_shape,
        compiler_params=pltpu.CompilerParams(vmem_limit_bytes=(50 if final else 60) * 1024 * 1024),
        cost_estimate=pl.CostEstimate(
            flops=2 * seq_len * depth * out_width,
            bytes_accessed=2 * depth * (seq_len + out_width) + 8 * seq_len * out_width,
            transcendentals=0,
        ),
        name="project",
    )(place, *operands)


def along_line(value, pairs):
    return lax.ppermute(value, "mp", pairs)


def on_device(queries, keys, values, out_weight, order_bias, partners, count, order):
    heads_dev = queries.shape[2] // HD
    group_size = HQ // KVH
    resp_total = lax.axis_size("resp")
    mp_total = lax.axis_size("mp")
    line = lax.axis_index("mp")
    first_head = line * heads_dev
    kv_head = (first_head // group_size).astype(jnp.int32)
    packed = pack(kv_head.reshape(1), keys, values)
    kv_blocks = gather_blocks(packed)
    where = jnp.stack([lax.axis_index("resp"), first_head]).astype(jnp.int32)
    place = line.astype(jnp.int32).reshape(1)

    def held_until(value, *after):
        return lax.optimization_barrier((value,) + after)[0]

    def attended_of(head_base, heads, *after):
        return attention(
            held_until(where, *after), partners, count, order, order_bias, queries, kv_blocks,
            head_base, heads, resp_total,
        )

    def add(total, parts, final, *after):
        return project(held_until(place, *after), total, parts, weight, final)

    if mp_total != 4 or heads_dev % 4:
        pieces = [attended_of(head, 1) for head in range(heads_dev)]
        gathered = lax.all_gather(jnp.concatenate(pieces, axis=1), "mp", axis=0, tiled=False)
        weight = out_weight.reshape(mp_total, heads_dev * HD, out_weight.shape[1])
        parts = [
            ([(gathered[source], ())], [lambda at, source=source: source]) for source in range(mp_total)
        ]
        return project(place, None, parts, weight, True)

    chunks = 4
    chunk_heads = heads_dev // chunks
    weight = out_weight.reshape(mp_total * chunks, chunk_heads * HD, out_weight.shape[1])
    inner, outer = (1, 2), (0, 3)
    own, pair, joined, crossed, forwarded = [], [], [], [], []

    def attend_chunk(*after):
        chunk = len(own)
        own.append(attended_of(chunk * chunk_heads, chunk_heads, *after))

    def exchange(*after):
        pair.append(along_line(held_until(own[-1], *after), [(0, 1), (1, 0), (2, 3), (3, 2)]))

    def cross(*after):
        chunk = len(joined)
        both = jnp.concatenate([own[chunk], held_until(pair[chunk], *after)], axis=1)
        joined.append(lax.optimization_barrier(both))
        crossed.append(along_line(joined[chunk], [(1, 2), (2, 1)]))

    def forward(*after):
        held = held_until(crossed[len(forwarded)], *after)
        forwarded.append(along_line(held, [(1, 0), (2, 3)]))

    def own_part(chunk):
        return ([(own[chunk], ())], [lambda at: at * chunks + chunk])

    def pair_part(chunk):
        return ([(pair[chunk], ())], [lambda at: (at ^ 1) * chunks + chunk])

    def far_part(chunk):
        rows = [
            lambda at: jnp.where(at < 2, 2, 1) * chunks + chunk,
            lambda at: jnp.where(at < 2, 3, 0) * chunks + chunk,
        ]
        return ([(crossed[chunk], inner), (forwarded[chunk], outer)], rows)

    attend_chunk()
    exchange()
    attend_chunk()
    cross(own[1])
    exchange()
    attend_chunk(joined[0])
    cross(own[2])
    exchange()
    forward(own[2])
    attend_chunk(joined[1], crossed[0])
    exchange(forwarded[0])
    cross(own[3])
    forward(joined[2])
    parts = [own_part(chunk) for chunk in range(4)] + [pair_part(chunk) for chunk in range(2)]
    total = add(None, parts, False, joined[2], crossed[1])
    cross(total)
    forward(joined[3])
    parts = [pair_part(2), pair_part(3), far_part(0), far_part(1)]
    total = add(total, parts, False, joined[3], crossed[2])
    forward(total)
    total = add(total, [far_part(2)], False, crossed[3])
    return add(total, [far_part(3)], True)


def solution(mesh):
    in_specs = (
        P("resp", None, "mp"),
        P("resp", None, None),
        P("resp", None, None),
        P(None, "mp"),
        P(),
        P("resp", None),
        P("resp"),
        P("resp", None),
    )
    out_specs = P("resp", None, "mp")
    return jax.shard_map(
        on_device, mesh=mesh, in_specs=in_specs, out_specs=out_specs, check_vma=False
    )
```

```python
import functools
import math

import jax
import jax.numpy as jnp
from jax import lax
from jax.experimental import pallas as pl
from jax.experimental.pallas import tpu as pltpu
from jax.sharding import PartitionSpec as P

HQ = 32
KVH = 4
HD = 128
REACH = 3
SLOTS = 6
OFFSETS = tuple(range(1, REACH + 1)) + tuple(-hop for hop in range(1, REACH + 1))
FLIPS = (1, 2, 3, 5, 6, 7)
BLOCKS = 1 + len(OFFSETS)
LOG2E = math.log2(math.e)
VMEM_BYTES = 60 * 1024 * 1024


def flipped(value, bits):
    count = lax.axis_size("resp")
    return lax.ppermute(value, "resp", [(source, source ^ bits) for source in range(count)])


def shifted(value, axis, steps):
    count = lax.axis_size(axis)
    pairs = [(source, (source + steps) % count) for source in range(count)]
    return lax.ppermute(value, axis, pairs)


def pack_kernel(head_ref, keys_ref, values_ref, out_ref):
    del head_ref
    for tile in range(keys_ref.shape[1] // HD):
        rows = slice(tile * HD, (tile + 1) * HD)
        out_ref[0, rows, :] = keys_ref[0, rows, :].T
    out_ref[1] = values_ref[0]


def pack(kv_head, keys, values):
    seq_len = keys.shape[1]
    spec = pl.BlockSpec((1, seq_len, HD), lambda step, head: (0, 0, head[0]))
    return pl.pallas_call(
        pack_kernel,
        grid_spec=pltpu.PrefetchScalarGridSpec(
            num_scalar_prefetch=1,
            grid=(1,),
            in_specs=[spec, spec],
            out_specs=pl.BlockSpec((2, seq_len, HD), lambda step, head: (0, 0, 0)),
        ),
        out_shape=jax.ShapeDtypeStruct((2, seq_len, HD), keys.dtype),
        compiler_params=pltpu.CompilerParams(vmem_limit_bytes=VMEM_BYTES),
        cost_estimate=pl.CostEstimate(flops=0, bytes_accessed=8 * seq_len * HD, transcendentals=0),
        name="pack",
    )(kv_head, keys, values)


def gather_blocks(packed):
    if lax.axis_size("resp") != 8:
        return [packed] + [shifted(packed, "resp", -offset) for offset in OFFSETS]
    far = flipped(packed, 6)
    along_x = flipped(packed, 2)
    along_y = flipped(packed, 4)
    twin = flipped(packed, 1)
    return [
        packed, twin, along_x, flipped(along_x, 1), flipped(along_y, 1), far, flipped(far, 1)
    ]


def target_of(resp_self, resp_total, block):
    if resp_total == 8:
        return resp_self ^ FLIPS[block - 1]
    return lax.rem(resp_self + OFFSETS[block - 1] + resp_total, resp_total)


def attention_kernel(
    head_base, resp_total, where_ref, partners_ref, count_ref, order_ref, bias_ref, q_ref, *rest
):
    kv_refs = rest[:BLOCKS]
    out_ref, scores_ref, expo_ref, peak_ref, total_ref = rest[-5:]
    unit, rows = scores_ref.shape[:2]
    seq_len = kv_refs[0].shape[1]
    scale = LOG2E / math.sqrt(HD)
    first_head = where_ref[1] + head_base + pl.program_id(0) * unit

    hits = []
    for block in range(1, BLOCKS):
        target = target_of(where_ref[0], resp_total, block)
        hits.append(
            [(slot < count_ref[0]) & (partners_ref[0, slot] == target) for slot in range(SLOTS)]
        )

    def bias_of(member, block):
        if block == 0:
            return jnp.float32(0.0)
        found = jnp.float32(-jnp.inf)
        for slot in range(SLOTS):
            offset = bias_ref[order_ref[0, slot], first_head + member] * LOG2E
            found = jnp.where(hits[block - 1][slot], offset, found)
        return found

    bias = [[bias_of(member, block) for block in range(BLOCKS)] for member in range(unit)]
    ones = jnp.ones((seq_len, HD), jnp.bfloat16)

    def cols(block):
        return slice(block * seq_len, (block + 1) * seq_len)

    def score(member, block):
        keys = jnp.concatenate(
            [kv_refs[block][0, tile : tile + HD, :] for tile in range(0, seq_len, HD)], axis=1
        )
        scores = jnp.dot(
            q_ref[0, :, member * HD : (member + 1) * HD], keys, preferred_element_type=jnp.float32
        )
        if block == 0:
            row_ids = lax.broadcasted_iota(jnp.int32, scores.shape, 0)
            col_ids = lax.broadcasted_iota(jnp.int32, scores.shape, 1)
            scores = jnp.where(row_ids >= col_ids, scores, -jnp.inf)
        scores_ref[member, :, cols(block)] = scores
        part = scores[:, :HD]
        for lane in range(HD, seq_len, HD):
            part = jnp.maximum(part, scores[:, lane : lane + HD])
        part = part * scale + bias[member][block]
        peak_ref[member] = part if block == 0 else jnp.maximum(peak_ref[member], part)

    def settle(member):
        peak = jnp.max(peak_ref[member], axis=1, keepdims=True)
        peak_ref[member] = jnp.broadcast_to(peak, (rows, HD))

    def expo(member, block):
        offset = bias[member][block] - peak_ref[member]
        scores = scores_ref[member, :, cols(block)]
        shift = jnp.concatenate([offset] * (seq_len // HD), axis=1)
        expo_ref[member, :, cols(block)] = jnp.exp2(scores * scale + shift).astype(jnp.bfloat16)

    def attend(member, block):
        if block % 2 == 1 or block == BLOCKS - 1:
            low = block - block % 2
            wide = jnp.concatenate(
                [
                    jnp.concatenate([kv_refs[held][1], ones], axis=1)
                    for held in range(low, block + 1)
                ],
                axis=0,
            )
            term = jnp.dot(
                expo_ref[member, :, low * seq_len : (block + 1) * seq_len],
                wide,
                preferred_element_type=jnp.float32,
            )
            total_ref[member] = term if low == 0 else total_ref[member] + term

    def finish(member):
        total = total_ref[member]
        out_ref[:, member * HD : (member + 1) * HD] = (total[:, :HD] / total[:, HD:]).astype(
            out_ref.dtype
        )

    for stage in range(unit + 2):
        for block in range(BLOCKS):
            if 0 <= stage - 2 < unit:
                attend(stage - 2, block)
            if 0 <= stage - 1 < unit:
                expo(stage - 1, block)
            if stage < unit:
                score(stage, block)
        if stage < unit:
            settle(stage)
        if 0 <= stage - 2 < unit:
            finish(stage - 2)


def attention(where, partners, count, order, order_bias, queries, kv_blocks, head_base, heads, resp_total):
    seq_len = queries.shape[1]
    unit = 2 if heads % 2 == 0 else 1
    smem = pl.BlockSpec(memory_space=pltpu.SMEM)
    whole = pl.BlockSpec(kv_blocks[0].shape, lambda step: (0, 0, 0))
    keys_all = BLOCKS * seq_len
    return pl.pallas_call(
        functools.partial(attention_kernel, head_base, resp_total),
        grid=(heads // unit,),
        in_specs=[smem] * 5
        + [pl.BlockSpec((1, seq_len, unit * HD), lambda step: (0, 0, head_base // unit + step))]
        + [whole] * BLOCKS,
        out_specs=pl.BlockSpec((seq_len, unit * HD), lambda step: (0, step)),
        out_shape=jax.ShapeDtypeStruct((seq_len, heads * HD), jnp.bfloat16),
        scratch_shapes=[
            pltpu.VMEM((unit, seq_len, keys_all), jnp.float32),
            pltpu.VMEM((unit, seq_len, keys_all), jnp.bfloat16),
            pltpu.VMEM((unit, seq_len, HD), jnp.float32),
            pltpu.VMEM((unit, seq_len, 2 * HD), jnp.float32),
        ],
        compiler_params=pltpu.CompilerParams(vmem_limit_bytes=VMEM_BYTES),
        cost_estimate=pl.CostEstimate(
            flops=heads * seq_len * keys_all * HD * 6,
            bytes_accessed=2 * seq_len * HD * (2 * heads + 2 * BLOCKS),
            transcendentals=heads * seq_len * keys_all,
        ),
        name="attend",
    )(where, partners, count, order, order_bias, queries, *kv_blocks)


def project_kernel(parts, start, final, place_ref, *refs):
    inputs = refs[: sum(len(kinds) + rows for kinds, rows in parts)]
    out_at = len(inputs) + (0 if start else 1)
    out_ref, held_refs = refs[out_at], refs[out_at + 1 :]
    left, right = [], []
    taken = chosen = 0
    for kinds, rows in parts:
        if len(kinds) == 1:
            left.append(inputs[taken][...])
        else:
            held_ref = held_refs[chosen]
            chosen += 1
            for other, places in enumerate(kinds):
                wanted = functools.reduce(jnp.logical_or, [place_ref[0] == at for at in places])

                @pl.when((pl.program_id(0) == 0) & wanted)
                def _(source_ref=inputs[taken + other]):
                    held_ref[...] = source_ref[...]

            left.append(held_ref[...])
        taken += len(kinds)
        for _ in range(rows):
            right.append(inputs[taken][0])
            taken += 1
    total = jnp.dot(
        jnp.concatenate(left, axis=1),
        jnp.concatenate(right, axis=0),
        preferred_element_type=jnp.float32,
    )
    if not start:
        total = total + refs[len(inputs)][...]
    out_ref[...] = total.astype(out_ref.dtype)[None] if final else total


def project(place, total, parts, weight, final):
    seq_len = parts[0][0][0][0].shape[0]
    width, out_width = weight.shape[1:]
    step = min(out_width, 512)
    specs, operands, kinds, held = [], [], [], []
    depth = 0
    for buffers, rows in parts:
        kinds.append((tuple(tuple(places) for _, places in buffers), len(rows)))
        for buffer, _ in buffers:
            specs.append(pl.BlockSpec(buffer.shape, lambda col, place: (0, 0)))
            operands.append(buffer)
        if len(buffers) > 1:
            held.append(pltpu.VMEM(buffers[0][0].shape, jnp.bfloat16))
        for row in rows:
            specs.append(
                pl.BlockSpec((1, width, step), lambda col, place, row=row: (row(place[0]), 0, col))
            )
            operands.append(weight)
        depth += width * len(rows)
    tile = pl.BlockSpec((seq_len, step), lambda col, place: (0, col))
    if total is not None:
        specs.append(tile)
        operands.append(total)
    if final:
        out_spec = pl.BlockSpec((1, seq_len, step), lambda col, place: (0, 0, col))
        out_shape = jax.ShapeDtypeStruct((1, seq_len, out_width), jnp.bfloat16)
    else:
        out_spec = tile
        out_shape = jax.ShapeDtypeStruct((seq_len, out_width), jnp.float32)
    return pl.pallas_call(
        functools.partial(project_kernel, tuple(kinds), total is None, final),
        grid_spec=pltpu.PrefetchScalarGridSpec(
            num_scalar_prefetch=1,
            grid=(out_width // step,),
            in_specs=specs,
            out_specs=out_spec,
            scratch_shapes=held,
        ),
        out_shape=out_shape,
        compiler_params=pltpu.CompilerParams(vmem_limit_bytes=(50 if final else 60) * 1024 * 1024),
        cost_estimate=pl.CostEstimate(
            flops=2 * seq_len * depth * out_width,
            bytes_accessed=2 * depth * (seq_len + out_width) + 8 * seq_len * out_width,
            transcendentals=0,
        ),
        name="project",
    )(place, *operands)


def along_line(value, pairs):
    return lax.ppermute(value, "mp", pairs)


def on_device(queries, keys, values, out_weight, order_bias, partners, count, order):
    heads_dev = queries.shape[2] // HD
    group_size = HQ // KVH
    resp_total = lax.axis_size("resp")
    mp_total = lax.axis_size("mp")
    line = lax.axis_index("mp")
    first_head = line * heads_dev
    kv_head = (first_head // group_size).astype(jnp.int32)
    packed = pack(kv_head.reshape(1), keys, values)
    kv_blocks = gather_blocks(packed)
    where = jnp.stack([lax.axis_index("resp"), first_head]).astype(jnp.int32)
    place = line.astype(jnp.int32).reshape(1)

    def held_until(value, *after):
        return lax.optimization_barrier((value,) + after)[0]

    def attended_of(head_base, heads, *after):
        return attention(
            held_until(where, *after), partners, count, order, order_bias, queries, kv_blocks,
            head_base, heads, resp_total,
        )

    def add(total, parts, final, *after):
        return project(held_until(place, *after), total, parts, weight, final)

    if mp_total != 4 or heads_dev % 4:
        pieces = [attended_of(head, 1) for head in range(heads_dev)]
        gathered = lax.all_gather(jnp.concatenate(pieces, axis=1), "mp", axis=0, tiled=False)
        weight = out_weight.reshape(mp_total, heads_dev * HD, out_weight.shape[1])
        parts = [
            ([(gathered[source], ())], [lambda at, source=source: source]) for source in range(mp_total)
        ]
        return project(place, None, parts, weight, True)

    chunks = 4
    chunk_heads = heads_dev // chunks
    weight = out_weight.reshape(mp_total * chunks, chunk_heads * HD, out_weight.shape[1])
    inner, outer = (1, 2), (0, 3)
    straight = (0, 1)
    own, pair, middle, second, near_out, far_out = [], [], [], [], [], []

    def attend_chunk(*after):
        chunk = len(own)
        own.append(attended_of(chunk * chunk_heads, chunk_heads, *after))
        pair.append(along_line(own[chunk], [(0, 1), (1, 0), (2, 3), (3, 2)]))
        middle.append(along_line(own[chunk], [(1, 2), (2, 1)]))
        if chunk in straight:
            second.append(along_line(own[chunk], [(0, 2), (2, 0), (1, 3), (3, 1)]))
            near_out.append(second[chunk])
        else:
            second.append(along_line(own[chunk], [(0, 2), (3, 1)]))

    def forward(held):
        return along_line(held, [(1, 0), (2, 3)])

    def own_part(chunk):
        return ([(own[chunk], ())], [lambda at: at * chunks + chunk])

    def pair_part(chunk):
        return ([(pair[chunk], ())], [lambda at: (at ^ 1) * chunks + chunk])

    def near_part(chunk):
        row = lambda at: jnp.where(at < 2, 2, 1) * chunks + chunk
        return ([(middle[chunk], inner), (near_out[chunk], outer)], [row])

    def far_part(chunk):
        row = lambda at: jnp.where(at < 2, 3, 0) * chunks + chunk
        return ([(second[chunk], inner), (far_out[chunk], outer)], [row])

    attend_chunk()
    attend_chunk()
    attend_chunk(middle[0], pair[0])
    far_out.append(forward(held_until(second[0], own[2])))
    attend_chunk(second[0], middle[1], pair[1])
    far_out.append(forward(held_until(second[1], own[3])))
    parts = [own_part(chunk) for chunk in range(4)] + [pair_part(chunk) for chunk in range(3)]
    total = add(None, parts + [near_part(0)], False, second[1], middle[2], far_out[0])
    near_out.append(forward(held_until(middle[2], total)))
    far_out.append(forward(held_until(second[2], total)))
    parts = [pair_part(3), near_part(1), far_part(0), far_part(1)]
    total = add(total, parts, False, middle[3], second[2])
    near_out.append(forward(held_until(middle[3], total)))
    far_out.append(forward(held_until(second[3], total)))
    total = add(total, [near_part(2), far_part(2)], False, second[3], middle[3])
    return add(total, [near_part(3), far_part(3)], True)


def solution(mesh):
    in_specs = (
        P("resp", None, "mp"),
        P("resp", None, None),
        P("resp", None, None),
        P(None, "mp"),
        P(),
        P("resp", None),
        P("resp"),
        P("resp", None),
    )
    out_specs = P("resp", None, "mp")
    return jax.shard_map(
        on_device, mesh=mesh, in_specs=in_specs, out_specs=out_specs, check_vma=False
    )
```

```python
import functools
import math

import jax
import jax.numpy as jnp
from jax import lax
from jax.experimental import pallas as pl
from jax.experimental.pallas import tpu as pltpu
from jax.sharding import PartitionSpec as P

HQ = 32
KVH = 4
HD = 128
REACH = 3
SLOTS = 6
OFFSETS = tuple(range(1, REACH + 1)) + tuple(-hop for hop in range(1, REACH + 1))
FLIPS = (1, 2, 3, 5, 6, 7)
BLOCKS = 1 + len(OFFSETS)
LOG2E = math.log2(math.e)
VMEM_BYTES = 60 * 1024 * 1024


def flipped(value, bits):
    count = lax.axis_size("resp")
    return lax.ppermute(value, "resp", [(source, source ^ bits) for source in range(count)])


def shifted(value, axis, steps):
    count = lax.axis_size(axis)
    pairs = [(source, (source + steps) % count) for source in range(count)]
    return lax.ppermute(value, axis, pairs)


def pack_kernel(head_ref, keys_ref, values_ref, out_ref):
    del head_ref
    for tile in range(keys_ref.shape[1] // HD):
        rows = slice(tile * HD, (tile + 1) * HD)
        out_ref[0, rows, :] = keys_ref[0, rows, :].T
    out_ref[1] = values_ref[0]


def pack(kv_head, keys, values):
    seq_len = keys.shape[1]
    spec = pl.BlockSpec((1, seq_len, HD), lambda step, head: (0, 0, head[0]))
    return pl.pallas_call(
        pack_kernel,
        grid_spec=pltpu.PrefetchScalarGridSpec(
            num_scalar_prefetch=1,
            grid=(1,),
            in_specs=[spec, spec],
            out_specs=pl.BlockSpec((2, seq_len, HD), lambda step, head: (0, 0, 0)),
        ),
        out_shape=jax.ShapeDtypeStruct((2, seq_len, HD), keys.dtype),
        compiler_params=pltpu.CompilerParams(vmem_limit_bytes=VMEM_BYTES),
        cost_estimate=pl.CostEstimate(flops=0, bytes_accessed=8 * seq_len * HD, transcendentals=0),
        name="pack",
    )(kv_head, keys, values)


def gather_blocks(packed):
    if lax.axis_size("resp") != 8:
        return [packed] + [shifted(packed, "resp", -offset) for offset in OFFSETS]
    far = flipped(packed, 6)
    along_x = flipped(packed, 2)
    along_y = flipped(packed, 4)
    twin = flipped(packed, 1)
    return [
        packed, twin, along_x, flipped(along_x, 1), flipped(along_y, 1), far, flipped(far, 1)
    ]


def target_of(resp_self, resp_total, block):
    if resp_total == 8:
        return resp_self ^ FLIPS[block - 1]
    return lax.rem(resp_self + OFFSETS[block - 1] + resp_total, resp_total)


def attention_kernel(
    head_base, resp_total, where_ref, partners_ref, count_ref, order_ref, bias_ref, q_ref, *rest
):
    kv_refs = rest[:BLOCKS]
    out_ref, scores_ref, expo_ref, peak_ref, total_ref = rest[-5:]
    unit, rows = scores_ref.shape[:2]
    seq_len = kv_refs[0].shape[1]
    scale = LOG2E / math.sqrt(HD)
    first_head = where_ref[1] + head_base + pl.program_id(0) * unit

    hits = []
    for block in range(1, BLOCKS):
        target = target_of(where_ref[0], resp_total, block)
        hits.append(
            [(slot < count_ref[0]) & (partners_ref[0, slot] == target) for slot in range(SLOTS)]
        )

    def bias_of(member, block):
        if block == 0:
            return jnp.float32(0.0)
        found = jnp.float32(-jnp.inf)
        for slot in range(SLOTS):
            offset = bias_ref[order_ref[0, slot], first_head + member] * LOG2E
            found = jnp.where(hits[block - 1][slot], offset, found)
        return found

    bias = [[bias_of(member, block) for block in range(BLOCKS)] for member in range(unit)]
    ones = jnp.ones((seq_len, HD), jnp.bfloat16)

    def cols(block):
        return slice(block * seq_len, (block + 1) * seq_len)

    def score(member, block):
        keys = jnp.concatenate(
            [kv_refs[block][0, tile : tile + HD, :] for tile in range(0, seq_len, HD)], axis=1
        )
        scores = jnp.dot(
            q_ref[0, :, member * HD : (member + 1) * HD], keys, preferred_element_type=jnp.float32
        )
        if block == 0:
            row_ids = lax.broadcasted_iota(jnp.int32, scores.shape, 0)
            col_ids = lax.broadcasted_iota(jnp.int32, scores.shape, 1)
            scores = jnp.where(row_ids >= col_ids, scores, -jnp.inf)
        scores_ref[member, :, cols(block)] = scores
        part = scores[:, :HD]
        for lane in range(HD, seq_len, HD):
            part = jnp.maximum(part, scores[:, lane : lane + HD])
        part = part * scale + bias[member][block]
        peak_ref[member] = part if block == 0 else jnp.maximum(peak_ref[member], part)

    def settle(member):
        peak = jnp.max(peak_ref[member], axis=1, keepdims=True)
        peak_ref[member] = jnp.broadcast_to(peak, (rows, HD))

    def expo(member, block):
        offset = bias[member][block] - peak_ref[member]
        scores = scores_ref[member, :, cols(block)]
        shift = jnp.concatenate([offset] * (seq_len // HD), axis=1)
        expo_ref[member, :, cols(block)] = jnp.exp2(scores * scale + shift).astype(jnp.bfloat16)

    def attend(member, block):
        if block % 2 == 1 or block == BLOCKS - 1:
            low = block - block % 2
            wide = jnp.concatenate(
                [
                    jnp.concatenate([kv_refs[held][1], ones], axis=1)
                    for held in range(low, block + 1)
                ],
                axis=0,
            )
            term = jnp.dot(
                expo_ref[member, :, low * seq_len : (block + 1) * seq_len],
                wide,
                preferred_element_type=jnp.float32,
            )
            total_ref[member] = term if low == 0 else total_ref[member] + term

    def finish(member):
        total = total_ref[member]
        out_ref[:, member * HD : (member + 1) * HD] = (total[:, :HD] / total[:, HD:]).astype(
            out_ref.dtype
        )

    for stage in range(unit + 2):
        for block in range(BLOCKS):
            if 0 <= stage - 2 < unit:
                attend(stage - 2, block)
            if 0 <= stage - 1 < unit:
                expo(stage - 1, block)
            if stage < unit:
                score(stage, block)
        if stage < unit:
            settle(stage)
        if 0 <= stage - 2 < unit:
            finish(stage - 2)


def attention(where, partners, count, order, order_bias, queries, kv_blocks, head_base, heads, resp_total):
    seq_len = queries.shape[1]
    unit = 2 if heads % 2 == 0 else 1
    smem = pl.BlockSpec(memory_space=pltpu.SMEM)
    whole = pl.BlockSpec(kv_blocks[0].shape, lambda step: (0, 0, 0))
    keys_all = BLOCKS * seq_len
    return pl.pallas_call(
        functools.partial(attention_kernel, head_base, resp_total),
        grid=(heads // unit,),
        in_specs=[smem] * 5
        + [pl.BlockSpec((1, seq_len, unit * HD), lambda step: (0, 0, head_base // unit + step))]
        + [whole] * BLOCKS,
        out_specs=pl.BlockSpec((seq_len, unit * HD), lambda step: (0, step)),
        out_shape=jax.ShapeDtypeStruct((seq_len, heads * HD), jnp.bfloat16),
        scratch_shapes=[
            pltpu.VMEM((unit, seq_len, keys_all), jnp.float32),
            pltpu.VMEM((unit, seq_len, keys_all), jnp.bfloat16),
            pltpu.VMEM((unit, seq_len, HD), jnp.float32),
            pltpu.VMEM((unit, seq_len, 2 * HD), jnp.float32),
        ],
        compiler_params=pltpu.CompilerParams(vmem_limit_bytes=VMEM_BYTES),
        cost_estimate=pl.CostEstimate(
            flops=heads * seq_len * keys_all * HD * 6,
            bytes_accessed=2 * seq_len * HD * (2 * heads + 2 * BLOCKS),
            transcendentals=heads * seq_len * keys_all,
        ),
        name="attend",
    )(where, partners, count, order, order_bias, queries, *kv_blocks)


def project_kernel(parts, start, final, place_ref, weight_ref, *refs):
    buffers = refs[: sum(len(kinds) for kinds, _ in parts)]
    total_ref = None if start else refs[len(buffers)]
    out_ref, left_ref, right_ref, held_ref, made_ref, left_sems, right_sems, total_sems, out_sems = refs[-9:]
    steps, _, step = right_ref.shape
    place = place_ref[0]

    def tile(ref, at):
        return ref.at[0, :, pl.ds(at * step, step)] if final else ref.at[at]

    def sources():
        taken = first = 0
        for index, (kinds, rows) in enumerate(parts):
            width = sum(count for _, count in rows)
            target = left_ref.at[:, pl.ds(first, width)]
            found = [
                (kinds[other], pltpu.make_async_copy(buffers[taken + other], target, left_sems.at[index]))
                for other in range(len(kinds))
            ]
            yield found
            taken += len(kinds)
            first += width

    def weights(at):
        found, first = [], 0
        for _, rows in parts:
            for row, count in rows:
                found.append(
                    pltpu.make_async_copy(
                        weight_ref.at[pl.ds(pl.multiple_of(row(place), HD), count), pl.ds(at * step, step)],
                        right_ref.at[at, pl.ds(first, count), :],
                        right_sems.at[at, len(found)],
                    )
                )
                first += count
        return found

    def totals(at):
        return [] if start else [pltpu.make_async_copy(total_ref.at[at], held_ref.at[at], total_sems.at[at])]

    for found in sources():
        for places, copy in found:
            if len(found) == 1:
                copy.start()
            else:
                wanted = functools.reduce(jnp.logical_or, [place == at for at in places])
                pl.when(wanted)(copy.start)
    for at in range(steps):
        for copy in weights(at) + totals(at):
            copy.start()
    for found in sources():
        found[0][1].wait()
    leaving = []
    for at in range(steps):
        for copy in weights(at) + totals(at):
            copy.wait()
        total = jnp.dot(left_ref[...], right_ref[at], preferred_element_type=jnp.float32)
        if not start:
            total = total + held_ref[at]
        made_ref[at] = total.astype(made_ref.dtype)
        leaving.append(pltpu.make_async_copy(made_ref.at[at], tile(out_ref, at), out_sems.at[at]))
        leaving[at].start()
    for copy in leaving:
        copy.wait()


def project(place, total, parts, weight, final):
    seq_len = parts[0][0][0][0].shape[0]
    out_width = weight.shape[1]
    step = min(out_width, 512)
    steps = out_width // step
    operands, kinds = [weight], []
    depth = runs = 0
    for buffers, rows in parts:
        kinds.append((tuple(tuple(places) for _, places in buffers), tuple(rows)))
        operands += [buffer for buffer, _ in buffers]
        depth += sum(count for _, count in rows)
        runs += len(rows)
    if total is not None:
        operands.append(total)
    there = pl.BlockSpec(memory_space=pl.ANY)
    if final:
        out_shape = jax.ShapeDtypeStruct((1, seq_len, out_width), jnp.bfloat16)
    else:
        out_shape = jax.ShapeDtypeStruct((steps, seq_len, step), jnp.float32)
    return pl.pallas_call(
        functools.partial(project_kernel, tuple(kinds), total is None, final),
        in_specs=[pl.BlockSpec(memory_space=pltpu.SMEM)] + [there] * len(operands),
        out_specs=there,
        out_shape=out_shape,
        scratch_shapes=[
            pltpu.VMEM((seq_len, depth), jnp.bfloat16),
            pltpu.VMEM((steps, depth, step), weight.dtype),
            pltpu.VMEM((1 if total is None else steps, seq_len, step), jnp.float32),
            pltpu.VMEM((steps, seq_len, step), out_shape.dtype),
            pltpu.SemaphoreType.DMA((len(parts),)),
            pltpu.SemaphoreType.DMA((steps, runs)),
            pltpu.SemaphoreType.DMA((steps,)),
            pltpu.SemaphoreType.DMA((steps,)),
        ],
        compiler_params=pltpu.CompilerParams(vmem_limit_bytes=52 * 1024 * 1024),
        cost_estimate=pl.CostEstimate(
            flops=2 * seq_len * depth * out_width,
            bytes_accessed=2 * depth * (seq_len + out_width) + 8 * seq_len * out_width,
            transcendentals=0,
        ),
        name="project",
    )(place, *operands)


def along_line(value, pairs):
    return lax.ppermute(value, "mp", pairs)


def on_device(queries, keys, values, out_weight, order_bias, partners, count, order):
    heads_dev = queries.shape[2] // HD
    group_size = HQ // KVH
    resp_total = lax.axis_size("resp")
    mp_total = lax.axis_size("mp")
    line = lax.axis_index("mp")
    first_head = line * heads_dev
    kv_head = (first_head // group_size).astype(jnp.int32)
    packed = pack(kv_head.reshape(1), keys, values)
    kv_blocks = gather_blocks(packed)
    where = jnp.stack([lax.axis_index("resp"), first_head]).astype(jnp.int32)
    place = line.astype(jnp.int32).reshape(1)

    def held_until(value, *after):
        return lax.optimization_barrier((value,) + after)[0]

    def attended_of(head_base, heads, *after):
        return attention(
            held_until(where, *after), partners, count, order, order_bias, queries, kv_blocks,
            head_base, heads, resp_total,
        )

    def add(total, parts, final, *after):
        return project(held_until(place, *after), total, parts, out_weight, final)

    device_rows = heads_dev * HD
    if mp_total != 4 or heads_dev % 4:
        pieces = [attended_of(head, 1) for head in range(heads_dev)]
        gathered = lax.all_gather(jnp.concatenate(pieces, axis=1), "mp", axis=0, tiled=False)
        parts = [
            ([(gathered[source], ())], [(lambda at, source=source: source * device_rows, device_rows)])
            for source in range(mp_total)
        ]
        return add(None, parts, True)

    chunks = 4
    chunk_heads = heads_dev // chunks
    rows = chunk_heads * HD
    inner, outer = (1, 2), (0, 3)
    straight = (0, 1)
    own, pair, middle, second, near_out, far_out = [], [], [], [], [], []

    def attend_chunk(*after):
        chunk = len(own)
        own.append(attended_of(chunk * chunk_heads, chunk_heads, *after))
        pair.append(along_line(own[chunk], [(0, 1), (1, 0), (2, 3), (3, 2)]))
        middle.append(along_line(own[chunk], [(1, 2), (2, 1)]))
        if chunk in straight:
            second.append(along_line(own[chunk], [(0, 2), (2, 0), (1, 3), (3, 1)]))
            near_out.append(second[chunk])
        else:
            second.append(along_line(own[chunk], [(0, 2), (3, 1)]))

    def forward(held):
        return along_line(held, [(1, 0), (2, 3)])

    def run_of(source, chunk):
        return [(lambda at: source(at) * device_rows + chunk * rows, rows)]

    def own_part(chunk):
        return ([(own[chunk], ())], run_of(lambda at: at, chunk))

    def pair_part(chunk):
        return ([(pair[chunk], ())], run_of(lambda at: at ^ 1, chunk))

    def near_part(chunk):
        row = run_of(lambda at: jnp.where(at < 2, 2, 1), chunk)
        return ([(middle[chunk], inner), (near_out[chunk], outer)], row)

    def far_part(chunk):
        row = run_of(lambda at: jnp.where(at < 2, 3, 0), chunk)
        return ([(second[chunk], inner), (far_out[chunk], outer)], row)

    attend_chunk()
    attend_chunk()
    attend_chunk(pair[0])
    far_out.append(forward(held_until(second[0], own[2])))
    attend_chunk(second[0], middle[0], pair[1])
    far_out.append(forward(held_until(second[1], own[3])))
    parts = [own_part(chunk) for chunk in range(4)] + [pair_part(chunk) for chunk in range(3)]
    total = add(None, parts, False, second[1], middle[1], middle[2], far_out[0])
    near_out.append(forward(held_until(middle[2], total)))
    far_out.append(forward(held_until(second[2], total)))
    parts = [pair_part(3), near_part(0), near_part(1), far_part(0), far_part(1)]
    total = add(total, parts, False, middle[3], second[2])
    near_out.append(forward(held_until(middle[3], total)))
    far_out.append(forward(held_until(second[3], total)))
    total = add(total, [near_part(2), far_part(2)], False, second[3], middle[3])
    return add(total, [near_part(3), far_part(3)], True)


def solution(mesh):
    in_specs = (
        P("resp", None, "mp"),
        P("resp", None, None),
        P("resp", None, None),
        P(None, "mp"),
        P(),
        P("resp", None),
        P("resp"),
        P("resp", None),
    )
    out_specs = P("resp", None, "mp")
    return jax.shard_map(
        on_device, mesh=mesh, in_specs=in_specs, out_specs=out_specs, check_vma=False
    )
```

```python
import functools
import math

import jax
import jax.numpy as jnp
from jax import lax
from jax.experimental import pallas as pl
from jax.experimental.pallas import tpu as pltpu
from jax.sharding import PartitionSpec as P

HQ = 32
KVH = 4
HD = 128
REACH = 3
SLOTS = 6
OFFSETS = tuple(range(1, REACH + 1)) + tuple(-hop for hop in range(1, REACH + 1))
FLIPS = (1, 2, 3, 5, 6, 7)
BLOCKS = 1 + len(OFFSETS)
LOG2E = math.log2(math.e)
VMEM_BYTES = 60 * 1024 * 1024


def flipped(value, bits):
    count = lax.axis_size("resp")
    return lax.ppermute(value, "resp", [(source, source ^ bits) for source in range(count)])


def shifted(value, axis, steps):
    count = lax.axis_size(axis)
    pairs = [(source, (source + steps) % count) for source in range(count)]
    return lax.ppermute(value, axis, pairs)


def pack_kernel(head_ref, keys_ref, values_ref, out_ref):
    del head_ref
    for tile in range(keys_ref.shape[1] // HD):
        rows = slice(tile * HD, (tile + 1) * HD)
        out_ref[0, rows, :] = keys_ref[0, rows, :].T
    out_ref[1] = values_ref[0]


def pack(kv_head, keys, values):
    seq_len = keys.shape[1]
    spec = pl.BlockSpec((1, seq_len, HD), lambda step, head: (0, 0, head[0]))
    return pl.pallas_call(
        pack_kernel,
        grid_spec=pltpu.PrefetchScalarGridSpec(
            num_scalar_prefetch=1,
            grid=(1,),
            in_specs=[spec, spec],
            out_specs=pl.BlockSpec((2, seq_len, HD), lambda step, head: (0, 0, 0)),
        ),
        out_shape=jax.ShapeDtypeStruct((2, seq_len, HD), keys.dtype),
        compiler_params=pltpu.CompilerParams(vmem_limit_bytes=VMEM_BYTES),
        cost_estimate=pl.CostEstimate(flops=0, bytes_accessed=8 * seq_len * HD, transcendentals=0),
        name="pack",
    )(kv_head, keys, values)


def gather_blocks(packed):
    if lax.axis_size("resp") != 8:
        return [packed] + [shifted(packed, "resp", -offset) for offset in OFFSETS]
    far = flipped(packed, 6)
    along_x = flipped(packed, 2)
    along_y = flipped(packed, 4)
    twin = flipped(packed, 1)
    return [
        packed, twin, along_x, flipped(along_x, 1), flipped(along_y, 1), far, flipped(far, 1)
    ]


def target_of(resp_self, resp_total, block):
    if resp_total == 8:
        return resp_self ^ FLIPS[block - 1]
    return lax.rem(resp_self + OFFSETS[block - 1] + resp_total, resp_total)


def attention_kernel(
    head_base, resp_total, where_ref, partners_ref, count_ref, order_ref, bias_ref, q_ref, *rest
):
    kv_refs = rest[:BLOCKS]
    out_ref, scores_ref, expo_ref, peak_ref, total_ref = rest[-5:]
    unit, rows = scores_ref.shape[:2]
    seq_len = kv_refs[0].shape[1]
    scale = LOG2E / math.sqrt(HD)
    first_head = where_ref[1] + head_base + pl.program_id(0) * unit

    hits = []
    for block in range(1, BLOCKS):
        target = target_of(where_ref[0], resp_total, block)
        hits.append(
            [(slot < count_ref[0]) & (partners_ref[0, slot] == target) for slot in range(SLOTS)]
        )

    def bias_of(member, block):
        if block == 0:
            return jnp.float32(0.0)
        found = jnp.float32(-jnp.inf)
        for slot in range(SLOTS):
            offset = bias_ref[order_ref[0, slot], first_head + member] * LOG2E
            found = jnp.where(hits[block - 1][slot], offset, found)
        return found

    bias = [[bias_of(member, block) for block in range(BLOCKS)] for member in range(unit)]
    ones = jnp.ones((seq_len, HD), jnp.bfloat16)

    def cols(block):
        return slice(block * seq_len, (block + 1) * seq_len)

    def score(member, block):
        keys = jnp.concatenate(
            [kv_refs[block][0, tile : tile + HD, :] for tile in range(0, seq_len, HD)], axis=1
        )
        scores = jnp.dot(
            q_ref[0, :, member * HD : (member + 1) * HD], keys, preferred_element_type=jnp.float32
        )
        if block == 0:
            row_ids = lax.broadcasted_iota(jnp.int32, scores.shape, 0)
            col_ids = lax.broadcasted_iota(jnp.int32, scores.shape, 1)
            scores = jnp.where(row_ids >= col_ids, scores, -jnp.inf)
        scores_ref[member, :, cols(block)] = scores
        part = scores[:, :HD]
        for lane in range(HD, seq_len, HD):
            part = jnp.maximum(part, scores[:, lane : lane + HD])
        part = part * scale + bias[member][block]
        peak_ref[member] = part if block == 0 else jnp.maximum(peak_ref[member], part)

    def settle(member):
        peak = jnp.max(peak_ref[member], axis=1, keepdims=True)
        peak_ref[member] = jnp.broadcast_to(peak, (rows, HD))

    def expo(member, block):
        offset = bias[member][block] - peak_ref[member]
        scores = scores_ref[member, :, cols(block)]
        shift = jnp.concatenate([offset] * (seq_len // HD), axis=1)
        expo_ref[member, :, cols(block)] = jnp.exp2(scores * scale + shift).astype(jnp.bfloat16)

    def attend(member, block):
        if block % 2 == 1 or block == BLOCKS - 1:
            low = block - block % 2
            wide = jnp.concatenate(
                [
                    jnp.concatenate([kv_refs[held][1], ones], axis=1)
                    for held in range(low, block + 1)
                ],
                axis=0,
            )
            term = jnp.dot(
                expo_ref[member, :, low * seq_len : (block + 1) * seq_len],
                wide,
                preferred_element_type=jnp.float32,
            )
            total_ref[member] = term if low == 0 else total_ref[member] + term

    def finish(member):
        total = total_ref[member]
        out_ref[:, member * HD : (member + 1) * HD] = (total[:, :HD] / total[:, HD:]).astype(
            out_ref.dtype
        )

    for stage in range(unit + 2):
        for block in range(BLOCKS):
            if 0 <= stage - 2 < unit:
                attend(stage - 2, block)
            if 0 <= stage - 1 < unit:
                expo(stage - 1, block)
            if stage < unit:
                score(stage, block)
        if stage < unit:
            settle(stage)
        if 0 <= stage - 2 < unit:
            finish(stage - 2)


def attention(where, partners, count, order, order_bias, queries, kv_blocks, head_base, heads, resp_total):
    seq_len = queries.shape[1]
    unit = 2 if heads % 2 == 0 else 1
    smem = pl.BlockSpec(memory_space=pltpu.SMEM)
    whole = pl.BlockSpec(kv_blocks[0].shape, lambda step: (0, 0, 0))
    keys_all = BLOCKS * seq_len
    return pl.pallas_call(
        functools.partial(attention_kernel, head_base, resp_total),
        grid=(heads // unit,),
        in_specs=[smem] * 5
        + [pl.BlockSpec((1, seq_len, unit * HD), lambda step: (0, 0, head_base // unit + step))]
        + [whole] * BLOCKS,
        out_specs=pl.BlockSpec((seq_len, unit * HD), lambda step: (0, step)),
        out_shape=jax.ShapeDtypeStruct((seq_len, heads * HD), jnp.bfloat16),
        scratch_shapes=[
            pltpu.VMEM((unit, seq_len, keys_all), jnp.float32),
            pltpu.VMEM((unit, seq_len, keys_all), jnp.bfloat16),
            pltpu.VMEM((unit, seq_len, HD), jnp.float32),
            pltpu.VMEM((unit, seq_len, 2 * HD), jnp.float32),
        ],
        compiler_params=pltpu.CompilerParams(vmem_limit_bytes=VMEM_BYTES),
        cost_estimate=pl.CostEstimate(
            flops=heads * seq_len * keys_all * HD * 6,
            bytes_accessed=2 * seq_len * HD * (2 * heads + 2 * BLOCKS),
            transcendentals=heads * seq_len * keys_all,
        ),
        name="attend",
    )(where, partners, count, order, order_bias, queries, *kv_blocks)


def project_kernel(parts, start, final, place_ref, weight_ref, *refs):
    buffers = refs[: sum(len(kinds) for kinds, _ in parts)]
    total_ref = None if start else refs[len(buffers)]
    out_ref, left_ref, right_ref, held_ref, made_ref, left_sems, right_sems, total_sems, out_sems = refs[-9:]
    steps, _, step = right_ref.shape
    place = place_ref[0]

    def tile(ref, at):
        return ref.at[0, :, pl.ds(at * step, step)] if final else ref.at[at]

    def sources():
        taken = first = 0
        for index, (kinds, rows) in enumerate(parts):
            width = sum(count for _, count in rows)
            target = left_ref.at[:, pl.ds(first, width)]
            found = [
                (kinds[other], pltpu.make_async_copy(buffers[taken + other], target, left_sems.at[index]))
                for other in range(len(kinds))
            ]
            yield found
            taken += len(kinds)
            first += width

    def weights(at):
        found, first = [], 0
        for _, rows in parts:
            for row, count in rows:
                found.append(
                    pltpu.make_async_copy(
                        weight_ref.at[pl.ds(pl.multiple_of(row(place), HD), count), pl.ds(at * step, step)],
                        right_ref.at[at, pl.ds(first, count), :],
                        right_sems.at[at, len(found)],
                    )
                )
                first += count
        return found

    def totals(at):
        return [] if start else [pltpu.make_async_copy(total_ref.at[at], held_ref.at[at], total_sems.at[at])]

    for found in sources():
        for places, copy in found:
            if len(found) == 1:
                copy.start()
            else:
                wanted = functools.reduce(jnp.logical_or, [place == at for at in places])
                pl.when(wanted)(copy.start)
    for at in range(steps):
        for copy in weights(at) + totals(at):
            copy.start()
    for found in sources():
        found[0][1].wait()
    leaving = []
    for at in range(steps):
        for copy in weights(at) + totals(at):
            copy.wait()
        total = jnp.dot(left_ref[...], right_ref[at], preferred_element_type=jnp.float32)
        if not start:
            total = total + held_ref[at]
        made_ref[at] = total.astype(made_ref.dtype)
        leaving.append(pltpu.make_async_copy(made_ref.at[at], tile(out_ref, at), out_sems.at[at]))
        leaving[at].start()
    for copy in leaving:
        copy.wait()


def project(place, total, parts, weight, final):
    seq_len = parts[0][0][0][0].shape[0]
    out_width = weight.shape[1]
    step = min(out_width, 512)
    steps = out_width // step
    operands, kinds = [weight], []
    depth = runs = 0
    for buffers, rows in parts:
        kinds.append((tuple(tuple(places) for _, places in buffers), tuple(rows)))
        operands += [buffer for buffer, _ in buffers]
        depth += sum(count for _, count in rows)
        runs += len(rows)
    if total is not None:
        operands.append(total)
    there = pl.BlockSpec(memory_space=pl.ANY)
    if final:
        out_shape = jax.ShapeDtypeStruct((1, seq_len, out_width), jnp.bfloat16)
    else:
        out_shape = jax.ShapeDtypeStruct((steps, seq_len, step), jnp.float32)
    return pl.pallas_call(
        functools.partial(project_kernel, tuple(kinds), total is None, final),
        in_specs=[pl.BlockSpec(memory_space=pltpu.SMEM)] + [there] * len(operands),
        out_specs=there,
        out_shape=out_shape,
        scratch_shapes=[
            pltpu.VMEM((seq_len, depth), jnp.bfloat16),
            pltpu.VMEM((steps, depth, step), weight.dtype),
            pltpu.VMEM((1 if total is None else steps, seq_len, step), jnp.float32),
            pltpu.VMEM((steps, seq_len, step), out_shape.dtype),
            pltpu.SemaphoreType.DMA((len(parts),)),
            pltpu.SemaphoreType.DMA((steps, runs)),
            pltpu.SemaphoreType.DMA((steps,)),
            pltpu.SemaphoreType.DMA((steps,)),
        ],
        compiler_params=pltpu.CompilerParams(vmem_limit_bytes=52 * 1024 * 1024),
        cost_estimate=pl.CostEstimate(
            flops=2 * seq_len * depth * out_width,
            bytes_accessed=2 * depth * (seq_len + out_width) + 8 * seq_len * out_width,
            transcendentals=0,
        ),
        name="project",
    )(place, *operands)


def along_line(value, pairs):
    return lax.ppermute(value, "mp", pairs)


def on_device(queries, keys, values, out_weight, order_bias, partners, count, order):
    heads_dev = queries.shape[2] // HD
    group_size = HQ // KVH
    resp_total = lax.axis_size("resp")
    mp_total = lax.axis_size("mp")
    line = lax.axis_index("mp")
    first_head = line * heads_dev
    kv_head = (first_head // group_size).astype(jnp.int32)
    packed = pack(kv_head.reshape(1), keys, values)
    kv_blocks = gather_blocks(packed)
    where = jnp.stack([lax.axis_index("resp"), first_head]).astype(jnp.int32)
    place = line.astype(jnp.int32).reshape(1)

    def held_until(value, *after):
        return lax.optimization_barrier((value,) + after)[0]

    def attended_of(head_base, heads, *after):
        return attention(
            held_until(where, *after), partners, count, order, order_bias, queries, kv_blocks,
            head_base, heads, resp_total,
        )

    def add(total, parts, final, *after):
        return project(held_until(place, *after), total, parts, out_weight, final)

    device_rows = heads_dev * HD
    if mp_total != 4 or heads_dev % 4:
        pieces = [attended_of(head, 1) for head in range(heads_dev)]
        gathered = lax.all_gather(jnp.concatenate(pieces, axis=1), "mp", axis=0, tiled=False)
        parts = [
            ([(gathered[source], ())], [(lambda at, source=source: source * device_rows, device_rows)])
            for source in range(mp_total)
        ]
        return add(None, parts, True)

    chunks = 4
    chunk_heads = heads_dev // chunks
    rows = chunk_heads * HD
    inner, outer = (1, 2), (0, 3)
    own, pair, middle, second, near_out, far_out = [], [], [], [], [], []

    def attend_chunk(*after):
        chunk = len(own)
        own.append(attended_of(chunk * chunk_heads, chunk_heads, *after))
        pair.append(along_line(own[chunk], [(0, 1), (1, 0), (2, 3), (3, 2)]))
        crossing = [(1, 2), (2, 1)] + ([(0, 3), (3, 0)] if chunk == 0 else [])
        middle.append(along_line(own[chunk], crossing))
        if chunk <= 1:
            second.append(along_line(own[chunk], [(0, 2), (2, 0), (1, 3), (3, 1)]))
            near_out.append(second[chunk])
        else:
            second.append(along_line(own[chunk], [(0, 2), (3, 1)]))
        if chunk == 0:
            far_out.append(middle[chunk])

    def forward(held):
        return along_line(held, [(1, 0), (2, 3)])

    def run_of(source, chunk):
        return [(lambda at: source(at) * device_rows + chunk * rows, rows)]

    def own_part(chunk):
        return ([(own[chunk], ())], run_of(lambda at: at, chunk))

    def pair_part(chunk):
        return ([(pair[chunk], ())], run_of(lambda at: at ^ 1, chunk))

    def near_rows(chunk):
        return run_of(lambda at: jnp.where(at < 2, 2, 1), chunk)

    def far_rows(chunk):
        return run_of(lambda at: jnp.where(at < 2, 3, 0), chunk)

    def near_part(chunk):
        return ([(middle[chunk], inner), (near_out[chunk], outer)], near_rows(chunk))

    def far_part(chunk):
        return ([(second[chunk], inner), (far_out[chunk], outer)], far_rows(chunk))

    def both_part(chunk):
        near, far = near_rows(chunk), far_rows(chunk)
        return ([(both_in[chunk], inner), (both_out[chunk], outer)], near + far)

    both_in, both_out = {}, {}

    def join(chunk, *after):
        both = jnp.concatenate([held_until(middle[chunk], *after), second[chunk]], axis=1)
        both_in[chunk] = lax.optimization_barrier(both)
        both_out[chunk] = forward(both_in[chunk])

    attend_chunk()
    attend_chunk()
    attend_chunk(pair[0], middle[0])
    attend_chunk(pair[1], second[0], middle[1])
    far_out.append(forward(held_until(second[1], own[3])))
    join(2, own[3])
    parts = [own_part(chunk) for chunk in range(4)] + [pair_part(0), pair_part(1), near_part(0), far_part(0)]
    total = add(None, parts, False, pair[2], middle[1], second[1], both_in[2])
    join(3, total)
    parts = [pair_part(2), pair_part(3), near_part(1), far_part(1), both_part(2)]
    total = add(total, parts, False, both_in[3])
    return add(total, [both_part(3)], True)


def solution(mesh):
    in_specs = (
        P("resp", None, "mp"),
        P("resp", None, None),
        P("resp", None, None),
        P(None, "mp"),
        P(),
        P("resp", None),
        P("resp"),
        P("resp", None),
    )
    out_specs = P("resp", None, "mp")
    return jax.shard_map(
        on_device, mesh=mesh, in_specs=in_specs, out_specs=out_specs, check_vma=False
    )
```

```python
import functools
import math

import jax
import jax.numpy as jnp
from jax import lax
from jax.experimental import pallas as pl
from jax.experimental.pallas import tpu as pltpu
from jax.sharding import PartitionSpec as P

HQ = 32
KVH = 4
HD = 128
REACH = 3
SLOTS = 6
OFFSETS = tuple(range(1, REACH + 1)) + tuple(-hop for hop in range(1, REACH + 1))
FLIPS = (1, 2, 3, 5, 6, 7)
BLOCKS = 1 + len(OFFSETS)
LOG2E = math.log2(math.e)
VMEM_BYTES = 60 * 1024 * 1024


def flipped(value, bits):
    count = lax.axis_size("resp")
    return lax.ppermute(value, "resp", [(source, source ^ bits) for source in range(count)])


def shifted(value, axis, steps):
    count = lax.axis_size(axis)
    pairs = [(source, (source + steps) % count) for source in range(count)]
    return lax.ppermute(value, axis, pairs)


def pack_kernel(head_ref, keys_ref, values_ref, out_ref):
    del head_ref
    for tile in range(keys_ref.shape[1] // HD):
        rows = slice(tile * HD, (tile + 1) * HD)
        out_ref[0, rows, :] = keys_ref[0, rows, :].T
    out_ref[1] = values_ref[0]


def pack(kv_head, keys, values):
    seq_len = keys.shape[1]
    spec = pl.BlockSpec((1, seq_len, HD), lambda step, head: (0, 0, head[0]))
    return pl.pallas_call(
        pack_kernel,
        grid_spec=pltpu.PrefetchScalarGridSpec(
            num_scalar_prefetch=1,
            grid=(1,),
            in_specs=[spec, spec],
            out_specs=pl.BlockSpec((2, seq_len, HD), lambda step, head: (0, 0, 0)),
        ),
        out_shape=jax.ShapeDtypeStruct((2, seq_len, HD), keys.dtype),
        compiler_params=pltpu.CompilerParams(vmem_limit_bytes=VMEM_BYTES),
        cost_estimate=pl.CostEstimate(flops=0, bytes_accessed=8 * seq_len * HD, transcendentals=0),
        name="pack",
    )(kv_head, keys, values)


def gather_blocks(packed):
    if lax.axis_size("resp") != 8:
        return [packed] + [shifted(packed, "resp", -offset) for offset in OFFSETS]
    far = flipped(packed, 6)
    along_x = flipped(packed, 2)
    along_y = flipped(packed, 4)
    twin = flipped(packed, 1)
    return [
        packed, twin, along_x, flipped(along_x, 1), flipped(along_y, 1), far, flipped(far, 1)
    ]


def target_of(resp_self, resp_total, block):
    if resp_total == 8:
        return resp_self ^ FLIPS[block - 1]
    return lax.rem(resp_self + OFFSETS[block - 1] + resp_total, resp_total)


def attention_kernel(
    head_base, resp_total, where_ref, bias_ref, q_ref, *rest
):
    kv_refs = rest[:BLOCKS]
    out_ref, scores_ref, expo_ref, peak_ref, total_ref = rest[-5:]
    unit, rows = scores_ref.shape[:2]
    seq_len = kv_refs[0].shape[1]
    scale = LOG2E / math.sqrt(HD)

    hits = []
    for block in range(1, BLOCKS):
        target = target_of(where_ref[0], resp_total, block)
        hits.append(
            [(slot < where_ref[1]) & (where_ref[2 + slot] == target) for slot in range(SLOTS)]
        )

    def bias_of(member, block):
        if block == 0:
            return jnp.float32(0.0)
        found = jnp.float32(-jnp.inf)
        for slot in range(SLOTS):
            offset = bias_ref[slot, head_base + member] * LOG2E
            found = jnp.where(hits[block - 1][slot], offset, found)
        return found

    bias = [[bias_of(member, block) for block in range(BLOCKS)] for member in range(unit)]
    ones = jnp.ones((seq_len, HD), jnp.bfloat16)

    def cols(block):
        return slice(block * seq_len, (block + 1) * seq_len)

    def score(member, block):
        keys = jnp.concatenate(
            [kv_refs[block][0, tile : tile + HD, :] for tile in range(0, seq_len, HD)], axis=1
        )
        scores = jnp.dot(
            q_ref[0, :, member * HD : (member + 1) * HD], keys, preferred_element_type=jnp.float32
        )
        if block == 0:
            row_ids = lax.broadcasted_iota(jnp.int32, scores.shape, 0)
            col_ids = lax.broadcasted_iota(jnp.int32, scores.shape, 1)
            scores = jnp.where(row_ids >= col_ids, scores, -jnp.inf)
        scores_ref[member, :, cols(block)] = scores
        part = scores[:, :HD]
        for lane in range(HD, seq_len, HD):
            part = jnp.maximum(part, scores[:, lane : lane + HD])
        part = part * scale + bias[member][block]
        peak_ref[member] = part if block == 0 else jnp.maximum(peak_ref[member], part)

    def settle(member):
        peak = jnp.max(peak_ref[member], axis=1, keepdims=True)
        peak_ref[member] = jnp.broadcast_to(peak, (rows, HD))

    def expo(member, block):
        offset = bias[member][block] - peak_ref[member]
        scores = scores_ref[member, :, cols(block)]
        shift = jnp.concatenate([offset] * (seq_len // HD), axis=1)
        expo_ref[member, :, cols(block)] = jnp.exp2(scores * scale + shift).astype(jnp.bfloat16)

    def attend(member, block):
        if block % 2 == 1 or block == BLOCKS - 1:
            low = block - block % 2
            wide = jnp.concatenate(
                [
                    jnp.concatenate([kv_refs[held][1], ones], axis=1)
                    for held in range(low, block + 1)
                ],
                axis=0,
            )
            term = jnp.dot(
                expo_ref[member, :, low * seq_len : (block + 1) * seq_len],
                wide,
                preferred_element_type=jnp.float32,
            )
            total_ref[member] = term if low == 0 else total_ref[member] + term

    def finish(member):
        total = total_ref[member]
        out_ref[:, member * HD : (member + 1) * HD] = (total[:, :HD] / total[:, HD:]).astype(
            out_ref.dtype
        )

    for stage in range(unit + 2):
        for block in range(BLOCKS):
            if 0 <= stage - 2 < unit:
                attend(stage - 2, block)
            if 0 <= stage - 1 < unit:
                expo(stage - 1, block)
            if stage < unit:
                score(stage, block)
        if stage < unit:
            settle(stage)
        if 0 <= stage - 2 < unit:
            finish(stage - 2)


def attention(where, slot_bias, queries, kv_blocks, head_base, heads, resp_total):
    seq_len = queries.shape[1]
    unit = 2 if heads % 2 == 0 else 1
    smem = pl.BlockSpec(memory_space=pltpu.SMEM)
    whole = pl.BlockSpec(kv_blocks[0].shape, lambda step: (0, 0, 0))
    keys_all = BLOCKS * seq_len
    return pl.pallas_call(
        functools.partial(attention_kernel, head_base, resp_total),
        grid=(heads // unit,),
        in_specs=[smem] * 2
        + [pl.BlockSpec((1, seq_len, unit * HD), lambda step: (0, 0, head_base // unit + step))]
        + [whole] * BLOCKS,
        out_specs=pl.BlockSpec((seq_len, unit * HD), lambda step: (0, step)),
        out_shape=jax.ShapeDtypeStruct((seq_len, heads * HD), jnp.bfloat16),
        scratch_shapes=[
            pltpu.VMEM((unit, seq_len, keys_all), jnp.float32),
            pltpu.VMEM((unit, seq_len, keys_all), jnp.bfloat16),
            pltpu.VMEM((unit, seq_len, HD), jnp.float32),
            pltpu.VMEM((unit, seq_len, 2 * HD), jnp.float32),
        ],
        compiler_params=pltpu.CompilerParams(vmem_limit_bytes=52 * 1024 * 1024),
        cost_estimate=pl.CostEstimate(
            flops=heads * seq_len * keys_all * HD * 6,
            bytes_accessed=2 * seq_len * HD * (2 * heads + 2 * BLOCKS),
            transcendentals=heads * seq_len * keys_all,
        ),
        name="attend",
    )(where, slot_bias, queries, *kv_blocks)


def project_kernel(parts, start, final, place_ref, weight_ref, *refs):
    buffers = refs[: sum(len(kinds) for kinds, _ in parts)]
    total_ref = None if start else refs[len(buffers)]
    out_ref, left_ref, right_ref, held_ref, made_ref, left_sems, right_sems, total_sems, out_sems = refs[-9:]
    steps, _, step = right_ref.shape
    place = place_ref[0]

    def tile(ref, at):
        return ref.at[0, :, pl.ds(at * step, step)] if final else ref.at[at]

    def sources():
        taken = first = 0
        for index, (kinds, rows) in enumerate(parts):
            width = sum(count for _, count in rows)
            target = left_ref.at[:, pl.ds(first, width)]
            found = [
                (kinds[other], pltpu.make_async_copy(buffers[taken + other], target, left_sems.at[index]))
                for other in range(len(kinds))
            ]
            yield found
            taken += len(kinds)
            first += width

    def weights(at):
        found, first = [], 0
        for _, rows in parts:
            for row, count in rows:
                found.append(
                    pltpu.make_async_copy(
                        weight_ref.at[pl.ds(pl.multiple_of(row(place), HD), count), pl.ds(at * step, step)],
                        right_ref.at[at, pl.ds(first, count), :],
                        right_sems.at[at, len(found)],
                    )
                )
                first += count
        return found

    def totals(at):
        return [] if start else [pltpu.make_async_copy(total_ref.at[at], held_ref.at[at], total_sems.at[at])]

    for found in sources():
        for places, copy in found:
            if len(found) == 1:
                copy.start()
            else:
                wanted = functools.reduce(jnp.logical_or, [place == at for at in places])
                pl.when(wanted)(copy.start)
    for at in range(steps):
        for copy in weights(at) + totals(at):
            copy.start()
    for found in sources():
        found[0][1].wait()
    leaving = []
    for at in range(steps):
        for copy in weights(at) + totals(at):
            copy.wait()
        total = jnp.dot(left_ref[...], right_ref[at], preferred_element_type=jnp.float32)
        if not start:
            total = total + held_ref[at]
        made_ref[at] = total.astype(made_ref.dtype)
        leaving.append(pltpu.make_async_copy(made_ref.at[at], tile(out_ref, at), out_sems.at[at]))
        leaving[at].start()
    for copy in leaving:
        copy.wait()


def project(place, total, parts, weight, final):
    seq_len = parts[0][0][0][0].shape[0]
    out_width = weight.shape[1]
    step = min(out_width, 512)
    steps = out_width // step
    operands, kinds = [weight], []
    depth = runs = 0
    for buffers, rows in parts:
        kinds.append((tuple(tuple(places) for _, places in buffers), tuple(rows)))
        operands += [buffer for buffer, _ in buffers]
        depth += sum(count for _, count in rows)
        runs += len(rows)
    if total is not None:
        operands.append(total)
    there = pl.BlockSpec(memory_space=pl.ANY)
    if final:
        out_shape = jax.ShapeDtypeStruct((1, seq_len, out_width), jnp.bfloat16)
    else:
        out_shape = jax.ShapeDtypeStruct((steps, seq_len, step), jnp.float32)
    return pl.pallas_call(
        functools.partial(project_kernel, tuple(kinds), total is None, final),
        in_specs=[pl.BlockSpec(memory_space=pltpu.SMEM)] + [there] * len(operands),
        out_specs=there,
        out_shape=out_shape,
        scratch_shapes=[
            pltpu.VMEM((seq_len, depth), jnp.bfloat16),
            pltpu.VMEM((steps, depth, step), weight.dtype),
            pltpu.VMEM((1 if total is None else steps, seq_len, step), jnp.float32),
            pltpu.VMEM((steps, seq_len, step), out_shape.dtype),
            pltpu.SemaphoreType.DMA((len(parts),)),
            pltpu.SemaphoreType.DMA((steps, runs)),
            pltpu.SemaphoreType.DMA((steps,)),
            pltpu.SemaphoreType.DMA((steps,)),
        ],
        compiler_params=pltpu.CompilerParams(vmem_limit_bytes=52 * 1024 * 1024),
        cost_estimate=pl.CostEstimate(
            flops=2 * seq_len * depth * out_width,
            bytes_accessed=2 * depth * (seq_len + out_width) + 8 * seq_len * out_width,
            transcendentals=0,
        ),
        name="project",
    )(place, *operands)


def along_line(value, pairs):
    return lax.ppermute(value, "mp", pairs)


def on_device(queries, keys, values, out_weight, order_bias, partners, count, order):
    heads_dev = queries.shape[2] // HD
    group_size = HQ // KVH
    resp_total = lax.axis_size("resp")
    mp_total = lax.axis_size("mp")
    line = lax.axis_index("mp")
    first_head = line * heads_dev
    kv_head = (first_head // group_size).astype(jnp.int32)
    packed = pack(kv_head.reshape(1), keys, values)
    kv_blocks = gather_blocks(packed)
    resp_self = lax.axis_index("resp").astype(jnp.int32).reshape(1)
    where = jnp.concatenate([resp_self, count, partners[0]])
    bias_dev = lax.dynamic_slice_in_dim(order_bias, first_head, heads_dev, 1)
    slot_bias = jnp.where(order[0][:, None] == 1, bias_dev[1][None, :], bias_dev[0][None, :])
    place = line.astype(jnp.int32).reshape(1)

    def held_until(value, *after):
        return lax.optimization_barrier((value,) + after)[0]

    def attended_of(head_base, heads, *after):
        return attention(
            held_until(where, *after), slot_bias, queries, kv_blocks, head_base, heads, resp_total
        )

    def add(total, parts, final, *after):
        return project(held_until(place, *after), total, parts, out_weight, final)

    device_rows = heads_dev * HD
    if mp_total != 4 or heads_dev % 4:
        pieces = [attended_of(head, 1) for head in range(heads_dev)]
        gathered = lax.all_gather(jnp.concatenate(pieces, axis=1), "mp", axis=0, tiled=False)
        parts = [
            ([(gathered[source], ())], [(lambda at, source=source: source * device_rows, device_rows)])
            for source in range(mp_total)
        ]
        return add(None, parts, True)

    chunks = 4
    chunk_heads = heads_dev // chunks
    rows = chunk_heads * HD
    inner, outer = (1, 2), (0, 3)
    own, pair, middle, second, near_out, far_out = [], [], [], [], [], []

    def attend_chunk(*after):
        chunk = len(own)
        own.append(attended_of(chunk * chunk_heads, chunk_heads, *after))
        pair.append(along_line(own[chunk], [(0, 1), (1, 0), (2, 3), (3, 2)]))
        middle.append(along_line(own[chunk], [(1, 2), (2, 1)]))
        if chunk <= 1:
            second.append(along_line(own[chunk], [(0, 2), (2, 0), (1, 3), (3, 1)]))
            near_out.append(second[chunk])
        else:
            second.append(along_line(own[chunk], [(0, 2), (3, 1)]))

    def forward(held):
        return along_line(held, [(1, 0), (2, 3)])

    def run_of(source, chunk):
        return [(lambda at: source(at) * device_rows + chunk * rows, rows)]

    def own_part(chunk):
        return ([(own[chunk], ())], run_of(lambda at: at, chunk))

    def pair_part(chunk):
        return ([(pair[chunk], ())], run_of(lambda at: at ^ 1, chunk))

    def near_rows(chunk):
        return run_of(lambda at: jnp.where(at < 2, 2, 1), chunk)

    def far_rows(chunk):
        return run_of(lambda at: jnp.where(at < 2, 3, 0), chunk)

    def near_part(chunk):
        return ([(middle[chunk], inner), (near_out[chunk], outer)], near_rows(chunk))

    def far_part(chunk):
        return ([(second[chunk], inner), (far_out[chunk], outer)], far_rows(chunk))

    def both_part(chunk):
        near, far = near_rows(chunk), far_rows(chunk)
        return ([(both_in[chunk], inner), (both_out[chunk], outer)], near + far)

    both_in, both_out = {}, {}

    def join(chunk, *after):
        both = jnp.concatenate([held_until(middle[chunk], *after), second[chunk]], axis=1)
        both_in[chunk] = lax.optimization_barrier(both)
        both_out[chunk] = forward(both_in[chunk])

    attend_chunk()
    attend_chunk()
    attend_chunk(pair[0])
    far_out.append(forward(held_until(second[0], own[2])))
    attend_chunk(second[0], middle[0], pair[1])
    far_out.append(forward(held_until(second[1], own[3])))
    parts = [own_part(chunk) for chunk in range(4)] + [pair_part(0), pair_part(1), near_part(0), far_part(0)]
    total = add(None, parts, False, middle[1], second[1], pair[2])
    join(2, total, far_out[1])
    join(3, both_in[2])
    parts = [pair_part(2), pair_part(3), near_part(1), far_part(1), both_part(2)]
    total = add(total, parts, False, both_in[3])
    return add(total, [both_part(3)], True)


def solution(mesh):
    in_specs = (
        P("resp", None, "mp"),
        P("resp", None, None),
        P("resp", None, None),
        P(None, "mp"),
        P(),
        P("resp", None),
        P("resp"),
        P("resp", None),
    )
    out_specs = P("resp", None, "mp")
    return jax.shard_map(
        on_device, mesh=mesh, in_specs=in_specs, out_specs=out_specs, check_vma=False
    )
```

```python
import functools
import math

import jax
import jax.numpy as jnp
from jax import lax
from jax.experimental import pallas as pl
from jax.experimental.pallas import tpu as pltpu
from jax.sharding import PartitionSpec as P

HQ = 32
KVH = 4
HD = 128
REACH = 3
SLOTS = 6
OFFSETS = tuple(range(1, REACH + 1)) + tuple(-hop for hop in range(1, REACH + 1))
FLIPS = (1, 2, 3, 5, 6, 7)
BLOCKS = 1 + len(OFFSETS)
LOG2E = math.log2(math.e)
VMEM_BYTES = 60 * 1024 * 1024


def flipped(value, bits):
    count = lax.axis_size("resp")
    return lax.ppermute(value, "resp", [(source, source ^ bits) for source in range(count)])


def shifted(value, axis, steps):
    count = lax.axis_size(axis)
    pairs = [(source, (source + steps) % count) for source in range(count)]
    return lax.ppermute(value, axis, pairs)


def pack_kernel(head_ref, keys_ref, values_ref, out_ref):
    del head_ref
    for tile in range(keys_ref.shape[1] // HD):
        rows = slice(tile * HD, (tile + 1) * HD)
        out_ref[0, rows, :] = keys_ref[0, rows, :].T
    out_ref[1] = values_ref[0]


def pack(kv_head, keys, values):
    seq_len = keys.shape[1]
    spec = pl.BlockSpec((1, seq_len, HD), lambda step, head: (0, 0, head[0]))
    return pl.pallas_call(
        pack_kernel,
        grid_spec=pltpu.PrefetchScalarGridSpec(
            num_scalar_prefetch=1,
            grid=(1,),
            in_specs=[spec, spec],
            out_specs=pl.BlockSpec((2, seq_len, HD), lambda step, head: (0, 0, 0)),
        ),
        out_shape=jax.ShapeDtypeStruct((2, seq_len, HD), keys.dtype),
        compiler_params=pltpu.CompilerParams(vmem_limit_bytes=60 * 1024 * 1024),
        cost_estimate=pl.CostEstimate(flops=0, bytes_accessed=8 * seq_len * HD, transcendentals=0),
        name="pack",
    )(kv_head, keys, values)


def gather_blocks(packed):
    if lax.axis_size("resp") != 8:
        return [packed] + [shifted(packed, "resp", -offset) for offset in OFFSETS]
    far = flipped(packed, 6)
    along_x = flipped(packed, 2)
    along_y = flipped(packed, 4)
    twin = flipped(packed, 1)
    return [
        packed, twin, along_x, flipped(along_x, 1), flipped(along_y, 1), far, flipped(far, 1)
    ]


def target_of(resp_self, resp_total, block):
    if resp_total == 8:
        return resp_self ^ FLIPS[block - 1]
    return lax.rem(resp_self + OFFSETS[block - 1] + resp_total, resp_total)


def attention_kernel(
    head_base, resp_total, where_ref, bias_ref, q_ref, *rest
):
    kv_refs = rest[:BLOCKS]
    out_ref, scores_ref, expo_ref, peak_ref, total_ref = rest[-5:]
    unit, rows = scores_ref.shape[:2]
    seq_len = kv_refs[0].shape[1]
    scale = LOG2E / math.sqrt(HD)

    hits = []
    for block in range(1, BLOCKS):
        target = target_of(where_ref[0], resp_total, block)
        hits.append(
            [(slot < where_ref[1]) & (where_ref[2 + slot] == target) for slot in range(SLOTS)]
        )

    def bias_of(member, block):
        if block == 0:
            return jnp.float32(0.0)
        found = jnp.float32(-jnp.inf)
        for slot in range(SLOTS):
            offset = bias_ref[slot, head_base + member] * LOG2E
            found = jnp.where(hits[block - 1][slot], offset, found)
        return found

    bias = [[bias_of(member, block) for block in range(BLOCKS)] for member in range(unit)]
    ones = jnp.ones((seq_len, HD), jnp.bfloat16)

    def cols(block):
        return slice(block * seq_len, (block + 1) * seq_len)

    def score(member, block):
        keys = jnp.concatenate(
            [kv_refs[block][0, tile : tile + HD, :] for tile in range(0, seq_len, HD)], axis=1
        )
        scores = jnp.dot(
            q_ref[0, :, member * HD : (member + 1) * HD], keys, preferred_element_type=jnp.float32
        )
        if block == 0:
            row_ids = lax.broadcasted_iota(jnp.int32, scores.shape, 0)
            col_ids = lax.broadcasted_iota(jnp.int32, scores.shape, 1)
            scores = jnp.where(row_ids >= col_ids, scores, -jnp.inf)
        scores_ref[member, :, cols(block)] = scores
        part = scores[:, :HD]
        for lane in range(HD, seq_len, HD):
            part = jnp.maximum(part, scores[:, lane : lane + HD])
        part = part * scale + bias[member][block]
        peak_ref[member] = part if block == 0 else jnp.maximum(peak_ref[member], part)

    def settle(member):
        peak = jnp.max(peak_ref[member], axis=1, keepdims=True)
        peak_ref[member] = jnp.broadcast_to(peak, (rows, HD))

    def expo(member, block):
        offset = bias[member][block] - peak_ref[member]
        scores = scores_ref[member, :, cols(block)]
        shift = jnp.concatenate([offset] * (seq_len // HD), axis=1)
        expo_ref[member, :, cols(block)] = jnp.exp2(scores * scale + shift).astype(jnp.bfloat16)

    def attend(member, block):
        if block % 2 == 1 or block == BLOCKS - 1:
            low = block - block % 2
            wide = jnp.concatenate(
                [
                    jnp.concatenate([kv_refs[held][1], ones], axis=1)
                    for held in range(low, block + 1)
                ],
                axis=0,
            )
            term = jnp.dot(
                expo_ref[member, :, low * seq_len : (block + 1) * seq_len],
                wide,
                preferred_element_type=jnp.float32,
            )
            total_ref[member] = term if low == 0 else total_ref[member] + term

    def finish(member):
        total = total_ref[member]
        out_ref[:, member * HD : (member + 1) * HD] = (total[:, :HD] / total[:, HD:]).astype(
            out_ref.dtype
        )

    for stage in range(unit + 2):
        for block in range(BLOCKS):
            if 0 <= stage - 2 < unit:
                attend(stage - 2, block)
            if 0 <= stage - 1 < unit:
                expo(stage - 1, block)
            if stage < unit:
                score(stage, block)
        if stage < unit:
            settle(stage)
        if 0 <= stage - 2 < unit:
            finish(stage - 2)


def attention(where, slot_bias, queries, kv_blocks, head_base, heads, resp_total):
    seq_len = queries.shape[1]
    unit = 2 if heads % 2 == 0 else 1
    smem = pl.BlockSpec(memory_space=pltpu.SMEM)
    whole = pl.BlockSpec(kv_blocks[0].shape, lambda step: (0, 0, 0))
    keys_all = BLOCKS * seq_len
    return pl.pallas_call(
        functools.partial(attention_kernel, head_base, resp_total),
        grid=(heads // unit,),
        in_specs=[smem] * 2
        + [pl.BlockSpec((1, seq_len, unit * HD), lambda step: (0, 0, head_base // unit + step))]
        + [whole] * BLOCKS,
        out_specs=pl.BlockSpec((seq_len, unit * HD), lambda step: (0, step)),
        out_shape=jax.ShapeDtypeStruct((seq_len, heads * HD), jnp.bfloat16),
        scratch_shapes=[
            pltpu.VMEM((unit, seq_len, keys_all), jnp.float32),
            pltpu.VMEM((unit, seq_len, keys_all), jnp.bfloat16),
            pltpu.VMEM((unit, seq_len, HD), jnp.float32),
            pltpu.VMEM((unit, seq_len, 2 * HD), jnp.float32),
        ],
        compiler_params=pltpu.CompilerParams(vmem_limit_bytes=51 * 1024 * 1024),
        cost_estimate=pl.CostEstimate(
            flops=heads * seq_len * keys_all * HD * 6,
            bytes_accessed=2 * seq_len * HD * (2 * heads + 2 * BLOCKS),
            transcendentals=heads * seq_len * keys_all,
        ),
        name="attend",
    )(where, slot_bias, queries, *kv_blocks)


def project_kernel(parts, start, final, place_ref, weight_ref, *refs):
    buffers = refs[: sum(len(kinds) for kinds, _ in parts)]
    total_ref = None if start else refs[len(buffers)]
    out_ref, left_ref, right_ref, held_ref, made_ref, left_sems, right_sems, total_sems, out_sems = refs[-9:]
    steps, _, step = right_ref.shape
    place = place_ref[0]

    def tile(ref, at):
        return ref.at[0, :, pl.ds(at * step, step)] if final else ref.at[at]

    def sources():
        taken = first = 0
        for index, (kinds, rows) in enumerate(parts):
            width = sum(count for _, count in rows)
            target = left_ref.at[:, pl.ds(first, width)]
            found = [
                (
                    kinds[other],
                    functools.partial(
                        pltpu.make_async_copy, buffers[taken + other], target, left_sems.at[index]
                    ),
                )
                for other in range(len(kinds))
            ]
            yield found
            taken += len(kinds)
            first += width

    def weights(at):
        found, first = [], 0
        for _, rows in parts:
            for row, count in rows:
                found.append(
                    pltpu.make_async_copy(
                        weight_ref.at[pl.ds(pl.multiple_of(row(place), HD), count), pl.ds(at * step, step)],
                        right_ref.at[at, pl.ds(first, count), :],
                        right_sems.at[at, len(found)],
                    )
                )
                first += count
        return found

    def totals(at):
        return [] if start else [pltpu.make_async_copy(total_ref.at[at], held_ref.at[at], total_sems.at[at])]

    for found in sources():
        for places, make in found:
            if len(found) == 1:
                make().start()
            else:
                wanted = functools.reduce(jnp.logical_or, [place == at for at in places])
                pl.when(wanted)(lambda make=make: make().start())
    for at in range(steps):
        for copy in weights(at) + totals(at):
            copy.start()
    for found in sources():
        found[0][1]().wait()
    leaving = []
    for at in range(steps):
        for copy in weights(at) + totals(at):
            copy.wait()
        total = jnp.dot(left_ref[...], right_ref[at], preferred_element_type=jnp.float32)
        if not start:
            total = total + held_ref[at]
        made_ref[at] = total.astype(made_ref.dtype)
        leaving.append(pltpu.make_async_copy(made_ref.at[at], tile(out_ref, at), out_sems.at[at]))
        leaving[at].start()
    for copy in leaving:
        copy.wait()


def project(place, total, parts, weight, final):
    seq_len = parts[0][0][0][0].shape[0]
    out_width = weight.shape[1]
    step = min(out_width, 512)
    steps = out_width // step
    operands, kinds = [weight], []
    depth = runs = 0
    for buffers, rows in parts:
        kinds.append((tuple(tuple(places) for _, places in buffers), tuple(rows)))
        operands += [buffer for buffer, _ in buffers]
        depth += sum(count for _, count in rows)
        runs += len(rows)
    if total is not None:
        operands.append(total)
    there = pl.BlockSpec(memory_space=pl.ANY)
    if final:
        out_shape = jax.ShapeDtypeStruct((1, seq_len, out_width), jnp.bfloat16)
    else:
        out_shape = jax.ShapeDtypeStruct((steps, seq_len, step), jnp.float32)
    return pl.pallas_call(
        functools.partial(project_kernel, tuple(kinds), total is None, final),
        in_specs=[pl.BlockSpec(memory_space=pltpu.SMEM)] + [there] * len(operands),
        out_specs=there,
        out_shape=out_shape,
        scratch_shapes=[
            pltpu.VMEM((seq_len, depth), jnp.bfloat16),
            pltpu.VMEM((steps, depth, step), weight.dtype),
            pltpu.VMEM((1 if total is None else steps, seq_len, step), jnp.float32),
            pltpu.VMEM((steps, seq_len, step), out_shape.dtype),
            pltpu.SemaphoreType.DMA((len(parts),)),
            pltpu.SemaphoreType.DMA((steps, runs)),
            pltpu.SemaphoreType.DMA((steps,)),
            pltpu.SemaphoreType.DMA((steps,)),
        ],
        compiler_params=pltpu.CompilerParams(vmem_limit_bytes=52 * 1024 * 1024),
        cost_estimate=pl.CostEstimate(
            flops=2 * seq_len * depth * out_width,
            bytes_accessed=2 * depth * (seq_len + out_width) + 8 * seq_len * out_width,
            transcendentals=0,
        ),
        name="project",
    )(place, *operands)


def along_line(value, pairs):
    return lax.ppermute(value, "mp", pairs)


def on_device(queries, keys, values, out_weight, order_bias, partners, count, order):
    heads_dev = queries.shape[2] // HD
    group_size = HQ // KVH
    resp_total = lax.axis_size("resp")
    mp_total = lax.axis_size("mp")
    line = lax.axis_index("mp")
    first_head = line * heads_dev
    kv_head = (first_head // group_size).astype(jnp.int32)
    packed = pack(kv_head.reshape(1), keys, values)
    kv_blocks = gather_blocks(packed)
    resp_self = lax.axis_index("resp").astype(jnp.int32).reshape(1)
    where = jnp.concatenate([resp_self, count, partners[0]])
    bias_dev = lax.dynamic_slice_in_dim(order_bias, first_head, heads_dev, 1)
    slot_bias = jnp.where(order[0][:, None] == 1, bias_dev[1][None, :], bias_dev[0][None, :])
    place = line.astype(jnp.int32).reshape(1)

    def held_until(value, *after):
        return lax.optimization_barrier((value,) + after)[0]

    def attended_of(head_base, heads, *after):
        return attention(
            held_until(where, *after), slot_bias, queries, kv_blocks, head_base, heads, resp_total
        )

    def add(total, parts, final, *after):
        return project(held_until(place, *after), total, parts, out_weight, final)

    device_rows = heads_dev * HD
    if mp_total != 4 or heads_dev % 4:
        pieces = [attended_of(head, 1) for head in range(heads_dev)]
        gathered = lax.all_gather(jnp.concatenate(pieces, axis=1), "mp", axis=0, tiled=False)
        parts = [
            ([(gathered[source], ())], [(lambda at, source=source: source * device_rows, device_rows)])
            for source in range(mp_total)
        ]
        return add(None, parts, True)

    chunks = 4
    chunk_heads = heads_dev // chunks
    rows = chunk_heads * HD
    inner, outer = (1, 2), (0, 3)
    straight = (0, 1)
    own, pair, middle, second, near_out, far_out = [], [], [], [], [], []

    def attend_chunk(*after):
        chunk = len(own)
        own.append(attended_of(chunk * chunk_heads, chunk_heads, *after))
        pair.append(along_line(own[chunk], [(0, 1), (1, 0), (2, 3), (3, 2)]))
        middle.append(along_line(own[chunk], [(1, 2), (2, 1)]))
        if chunk in straight:
            second.append(along_line(own[chunk], [(0, 2), (2, 0), (1, 3), (3, 1)]))
            near_out.append(second[chunk])
        else:
            second.append(along_line(own[chunk], [(0, 2), (3, 1)]))

    def forward(held):
        return along_line(held, [(1, 0), (2, 3)])

    def run_of(source, chunk):
        return [(lambda at: source(at) * device_rows + chunk * rows, rows)]

    def own_part(chunk):
        return ([(own[chunk], ())], run_of(lambda at: at, chunk))

    def pair_part(chunk):
        return ([(pair[chunk], ())], run_of(lambda at: at ^ 1, chunk))

    def near_part(chunk):
        row = run_of(lambda at: jnp.where(at < 2, 2, 1), chunk)
        return ([(middle[chunk], inner), (near_out[chunk], outer)], row)

    def far_part(chunk):
        row = run_of(lambda at: jnp.where(at < 2, 3, 0), chunk)
        return ([(second[chunk], inner), (far_out[chunk], outer)], row)

    attend_chunk()
    attend_chunk()
    attend_chunk(pair[0])
    far_out.append(forward(held_until(second[0], own[2])))
    attend_chunk(second[0], middle[0], pair[1])
    far_out.append(forward(held_until(second[1], own[3])))
    parts = [own_part(chunk) for chunk in range(4)] + [pair_part(chunk) for chunk in range(3)]
    total = add(None, parts, False, second[1], middle[1], middle[2], far_out[0])
    near_out.append(forward(held_until(middle[2], total)))
    far_out.append(forward(held_until(second[2], total)))
    parts = [pair_part(3), near_part(0), near_part(1), far_part(0), far_part(1)]
    total = add(total, parts, False, middle[3], second[2])
    near_out.append(forward(held_until(middle[3], total)))
    far_out.append(forward(held_until(second[3], total)))
    total = add(total, [near_part(2), far_part(2)], False, second[3], middle[3])
    return add(total, [near_part(3), far_part(3)], True)


def solution(mesh):
    in_specs = (
        P("resp", None, "mp"),
        P("resp", None, None),
        P("resp", None, None),
        P(None, "mp"),
        P(),
        P("resp", None),
        P("resp"),
        P("resp", None),
    )
    out_specs = P("resp", None, "mp")
    return jax.shard_map(
        on_device, mesh=mesh, in_specs=in_specs, out_specs=out_specs, check_vma=False
    )
```

```python
import functools
import math

import jax
import jax.numpy as jnp
from jax import lax
from jax.experimental import pallas as pl
from jax.experimental.pallas import tpu as pltpu
from jax.sharding import PartitionSpec as P

HQ = 32
KVH = 4
HD = 128
REACH = 3
SLOTS = 6
OFFSETS = tuple(range(1, REACH + 1)) + tuple(-hop for hop in range(1, REACH + 1))
FLIPS = (1, 2, 3, 5, 6, 7)
BLOCKS = 1 + len(OFFSETS)
LOG2E = math.log2(math.e)
VMEM_BYTES = 60 * 1024 * 1024


def flipped(value, bits):
    count = lax.axis_size("resp")
    return lax.ppermute(value, "resp", [(source, source ^ bits) for source in range(count)])


def shifted(value, axis, steps):
    count = lax.axis_size(axis)
    pairs = [(source, (source + steps) % count) for source in range(count)]
    return lax.ppermute(value, axis, pairs)


def pack_kernel(head_ref, keys_ref, values_ref, out_ref):
    del head_ref
    for tile in range(keys_ref.shape[1] // HD):
        rows = slice(tile * HD, (tile + 1) * HD)
        out_ref[0, rows, :] = keys_ref[0, rows, :].T
    out_ref[1] = values_ref[0]


def pack(kv_head, keys, values):
    seq_len = keys.shape[1]
    spec = pl.BlockSpec((1, seq_len, HD), lambda step, head: (0, 0, head[0]))
    return pl.pallas_call(
        pack_kernel,
        grid_spec=pltpu.PrefetchScalarGridSpec(
            num_scalar_prefetch=1,
            grid=(1,),
            in_specs=[spec, spec],
            out_specs=pl.BlockSpec((2, seq_len, HD), lambda step, head: (0, 0, 0)),
        ),
        out_shape=jax.ShapeDtypeStruct((2, seq_len, HD), keys.dtype),
        compiler_params=pltpu.CompilerParams(vmem_limit_bytes=60 * 1024 * 1024),
        cost_estimate=pl.CostEstimate(flops=0, bytes_accessed=8 * seq_len * HD, transcendentals=0),
        name="pack",
    )(kv_head, keys, values)


def gather_blocks(packed):
    if lax.axis_size("resp") != 8:
        return [packed] + [shifted(packed, "resp", -offset) for offset in OFFSETS]
    far = flipped(packed, 6)
    along_x = flipped(packed, 2)
    along_y = flipped(packed, 4)
    twin = flipped(packed, 1)
    return [
        packed, twin, along_x, flipped(along_x, 1), flipped(along_y, 1), far, flipped(far, 1)
    ]


def target_of(resp_self, resp_total, block):
    if resp_total == 8:
        return resp_self ^ FLIPS[block - 1]
    return lax.rem(resp_self + OFFSETS[block - 1] + resp_total, resp_total)


def attention_kernel(
    head_base, resp_total, where_ref, bias_ref, q_ref, *rest
):
    kv_refs = rest[:BLOCKS]
    out_ref, scores_ref, expo_ref, peak_ref, total_ref = rest[-5:]
    unit, rows = scores_ref.shape[:2]
    seq_len = kv_refs[0].shape[1]
    scale = LOG2E / math.sqrt(HD)

    hits = []
    for block in range(1, BLOCKS):
        target = target_of(where_ref[0], resp_total, block)
        hits.append(
            [(slot < where_ref[1]) & (where_ref[2 + slot] == target) for slot in range(SLOTS)]
        )

    def bias_of(member, block):
        if block == 0:
            return jnp.float32(0.0)
        found = jnp.float32(-jnp.inf)
        for slot in range(SLOTS):
            offset = bias_ref[slot, head_base + member] * LOG2E
            found = jnp.where(hits[block - 1][slot], offset, found)
        return found

    bias = [[bias_of(member, block) for block in range(BLOCKS)] for member in range(unit)]
    ones = jnp.ones((seq_len, HD), jnp.bfloat16)

    def cols(block):
        return slice(block * seq_len, (block + 1) * seq_len)

    def score(member, block):
        keys = jnp.concatenate(
            [kv_refs[block][0, tile : tile + HD, :] for tile in range(0, seq_len, HD)], axis=1
        )
        scores = jnp.dot(
            q_ref[0, :, member * HD : (member + 1) * HD], keys, preferred_element_type=jnp.float32
        )
        if block == 0:
            row_ids = lax.broadcasted_iota(jnp.int32, scores.shape, 0)
            col_ids = lax.broadcasted_iota(jnp.int32, scores.shape, 1)
            scores = jnp.where(row_ids >= col_ids, scores, -jnp.inf)
        scores_ref[member, :, cols(block)] = scores
        part = scores[:, :HD]
        for lane in range(HD, seq_len, HD):
            part = jnp.maximum(part, scores[:, lane : lane + HD])
        part = part * scale + bias[member][block]
        peak_ref[member] = part if block == 0 else jnp.maximum(peak_ref[member], part)

    def settle(member):
        peak = jnp.max(peak_ref[member], axis=1, keepdims=True)
        peak_ref[member] = jnp.broadcast_to(peak, (rows, HD))

    def expo(member, block):
        offset = bias[member][block] - peak_ref[member]
        scores = scores_ref[member, :, cols(block)]
        shift = jnp.concatenate([offset] * (seq_len // HD), axis=1)
        expo_ref[member, :, cols(block)] = jnp.exp2(scores * scale + shift).astype(jnp.bfloat16)

    def attend(member, block):
        if block % 2 == 1 or block == BLOCKS - 1:
            low = block - block % 2
            wide = jnp.concatenate(
                [
                    jnp.concatenate([kv_refs[held][1], ones], axis=1)
                    for held in range(low, block + 1)
                ],
                axis=0,
            )
            term = jnp.dot(
                expo_ref[member, :, low * seq_len : (block + 1) * seq_len],
                wide,
                preferred_element_type=jnp.float32,
            )
            total_ref[member] = term if low == 0 else total_ref[member] + term

    def finish(member):
        total = total_ref[member]
        out_ref[:, member * HD : (member + 1) * HD] = (total[:, :HD] / total[:, HD:]).astype(
            out_ref.dtype
        )

    for stage in range(unit + 2):
        for block in range(BLOCKS):
            if 0 <= stage - 2 < unit:
                attend(stage - 2, block)
            if 0 <= stage - 1 < unit:
                expo(stage - 1, block)
            if stage < unit:
                score(stage, block)
        if stage < unit:
            settle(stage)
        if 0 <= stage - 2 < unit:
            finish(stage - 2)


def attention(where, slot_bias, queries, kv_blocks, head_base, heads, resp_total):
    seq_len = queries.shape[1]
    unit = 2 if heads % 2 == 0 else 1
    smem = pl.BlockSpec(memory_space=pltpu.SMEM)
    whole = pl.BlockSpec(kv_blocks[0].shape, lambda step: (0, 0, 0))
    keys_all = BLOCKS * seq_len
    return pl.pallas_call(
        functools.partial(attention_kernel, head_base, resp_total),
        grid=(heads // unit,),
        in_specs=[smem] * 2
        + [pl.BlockSpec((1, seq_len, unit * HD), lambda step: (0, 0, head_base // unit + step))]
        + [whole] * BLOCKS,
        out_specs=pl.BlockSpec((seq_len, unit * HD), lambda step: (0, step)),
        out_shape=jax.ShapeDtypeStruct((seq_len, heads * HD), jnp.bfloat16),
        scratch_shapes=[
            pltpu.VMEM((unit, seq_len, keys_all), jnp.float32),
            pltpu.VMEM((unit, seq_len, keys_all), jnp.bfloat16),
            pltpu.VMEM((unit, seq_len, HD), jnp.float32),
            pltpu.VMEM((unit, seq_len, 2 * HD), jnp.float32),
        ],
        compiler_params=pltpu.CompilerParams(vmem_limit_bytes=51 * 1024 * 1024),
        cost_estimate=pl.CostEstimate(
            flops=heads * seq_len * keys_all * HD * 6,
            bytes_accessed=2 * seq_len * HD * (2 * heads + 2 * BLOCKS),
            transcendentals=heads * seq_len * keys_all,
        ),
        name="attend",
    )(where, slot_bias, queries, *kv_blocks)


def project_kernel(parts, start, final, place_ref, weight_ref, *refs):
    buffers = refs[: sum(len(kinds) for kinds, _ in parts)]
    total_ref = None if start else refs[len(buffers)]
    out_ref, left_ref, right_ref, held_ref, made_ref, left_sems, right_sems, total_sems, out_sems = refs[-9:]
    steps, _, step = right_ref.shape
    place = place_ref[0]

    def tile(ref, at):
        return ref.at[0, :, pl.ds(at * step, step)] if final else ref.at[at]

    def sources():
        taken = first = 0
        for index, (kinds, rows) in enumerate(parts):
            width = sum(count for _, count in rows)
            target = left_ref.at[:, pl.ds(first, width)]
            found = [
                (
                    kinds[other],
                    functools.partial(
                        pltpu.make_async_copy, buffers[taken + other], target, left_sems.at[index]
                    ),
                )
                for other in range(len(kinds))
            ]
            yield found
            taken += len(kinds)
            first += width

    def weights(at):
        found, first = [], 0
        for _, rows in parts:
            for row, count in rows:
                found.append(
                    pltpu.make_async_copy(
                        weight_ref.at[pl.ds(pl.multiple_of(row(place), HD), count), pl.ds(at * step, step)],
                        right_ref.at[at, pl.ds(first, count), :],
                        right_sems.at[at, len(found)],
                    )
                )
                first += count
        return found

    def totals(at):
        return [] if start else [pltpu.make_async_copy(total_ref.at[at], held_ref.at[at], total_sems.at[at])]

    for found in sources():
        for places, make in found:
            if len(found) == 1:
                make().start()
            else:
                wanted = functools.reduce(jnp.logical_or, [place == at for at in places])
                pl.when(wanted)(lambda make=make: make().start())
    for at in range(steps):
        for copy in weights(at) + totals(at):
            copy.start()
    for found in sources():
        found[0][1]().wait()
    leaving = []
    for at in range(steps):
        for copy in weights(at) + totals(at):
            copy.wait()
        total = jnp.dot(left_ref[...], right_ref[at], preferred_element_type=jnp.float32)
        if not start:
            total = total + held_ref[at]
        made_ref[at] = total.astype(made_ref.dtype)
        leaving.append(pltpu.make_async_copy(made_ref.at[at], tile(out_ref, at), out_sems.at[at]))
        leaving[at].start()
    for copy in leaving:
        copy.wait()


def project(place, total, parts, weight, final):
    seq_len = parts[0][0][0][0].shape[0]
    out_width = weight.shape[1]
    step = min(out_width, 512)
    steps = out_width // step
    operands, kinds = [weight], []
    depth = runs = 0
    for buffers, rows in parts:
        kinds.append((tuple(tuple(places) for _, places in buffers), tuple(rows)))
        operands += [buffer for buffer, _ in buffers]
        depth += sum(count for _, count in rows)
        runs += len(rows)
    if total is not None:
        operands.append(total)
    there = pl.BlockSpec(memory_space=pl.ANY)
    if final:
        out_shape = jax.ShapeDtypeStruct((1, seq_len, out_width), jnp.bfloat16)
    else:
        out_shape = jax.ShapeDtypeStruct((steps, seq_len, step), jnp.float32)
    return pl.pallas_call(
        functools.partial(project_kernel, tuple(kinds), total is None, final),
        in_specs=[pl.BlockSpec(memory_space=pltpu.SMEM)] + [there] * len(operands),
        out_specs=there,
        out_shape=out_shape,
        scratch_shapes=[
            pltpu.VMEM((seq_len, depth), jnp.bfloat16),
            pltpu.VMEM((steps, depth, step), weight.dtype),
            pltpu.VMEM((1 if total is None else steps, seq_len, step), jnp.float32),
            pltpu.VMEM((steps, seq_len, step), out_shape.dtype),
            pltpu.SemaphoreType.DMA((len(parts),)),
            pltpu.SemaphoreType.DMA((steps, runs)),
            pltpu.SemaphoreType.DMA((steps,)),
            pltpu.SemaphoreType.DMA((steps,)),
        ],
        compiler_params=pltpu.CompilerParams(vmem_limit_bytes=52 * 1024 * 1024),
        cost_estimate=pl.CostEstimate(
            flops=2 * seq_len * depth * out_width,
            bytes_accessed=2 * depth * (seq_len + out_width) + 8 * seq_len * out_width,
            transcendentals=0,
        ),
        name="project",
    )(place, *operands)


def along_line(value, pairs):
    return lax.ppermute(value, "mp", pairs)


def on_device(queries, keys, values, out_weight, order_bias, partners, count, order):
    heads_dev = queries.shape[2] // HD
    group_size = HQ // KVH
    resp_total = lax.axis_size("resp")
    mp_total = lax.axis_size("mp")
    line = lax.axis_index("mp")
    first_head = line * heads_dev
    kv_head = (first_head // group_size).astype(jnp.int32)
    packed = pack(kv_head.reshape(1), keys, values)
    kv_blocks = gather_blocks(packed)
    resp_self = lax.axis_index("resp").astype(jnp.int32).reshape(1)
    where = jnp.concatenate([resp_self, count, partners[0]])
    bias_dev = lax.dynamic_slice_in_dim(order_bias, first_head, heads_dev, 1)
    slot_bias = jnp.where(order[0][:, None] == 1, bias_dev[1][None, :], bias_dev[0][None, :])
    place = line.astype(jnp.int32).reshape(1)

    def held_until(value, *after):
        return lax.optimization_barrier((value,) + after)[0]

    def attended_of(head_base, heads, *after):
        return attention(
            held_until(where, *after), slot_bias, queries, kv_blocks, head_base, heads, resp_total
        )

    def add(total, parts, final, *after):
        return project(held_until(place, *after), total, parts, out_weight, final)

    device_rows = heads_dev * HD
    if mp_total != 4 or heads_dev % 4:
        pieces = [attended_of(head, 1) for head in range(heads_dev)]
        gathered = lax.all_gather(jnp.concatenate(pieces, axis=1), "mp", axis=0, tiled=False)
        parts = [
            ([(gathered[source], ())], [(lambda at, source=source: source * device_rows, device_rows)])
            for source in range(mp_total)
        ]
        return add(None, parts, True)

    chunks = 4
    chunk_heads = heads_dev // chunks
    rows = chunk_heads * HD
    inner, outer = (1, 2), (0, 3)
    own, pair, middle, second = [], [], [], []

    def attend_chunk(*after):
        chunk = len(own)
        own.append(attended_of(chunk * chunk_heads, chunk_heads, *after))
        pair.append(along_line(own[chunk], [(0, 1), (1, 0), (2, 3), (3, 2)]))
        if chunk == 0:
            middle.append(along_line(own[chunk], [(0, 3), (1, 2), (2, 1), (3, 0)]))
            second.append(along_line(own[chunk], [(0, 2), (2, 0), (1, 3), (3, 1)]))
        else:
            middle.append(along_line(own[chunk], [(1, 2), (2, 1)]))
            second.append(along_line(own[chunk], [(0, 2), (3, 1)]))

    def forward(held):
        return along_line(held, [(1, 0), (2, 3)])

    def run_of(source, chunk):
        return [(lambda at: source(at) * device_rows + chunk * rows, rows)]

    def own_part(chunk):
        return ([(own[chunk], ())], run_of(lambda at: at, chunk))

    def pair_part(chunk):
        return ([(pair[chunk], ())], run_of(lambda at: at ^ 1, chunk))

    def near_rows(chunk):
        return run_of(lambda at: jnp.where(at < 2, 2, 1), chunk)

    def far_rows(chunk):
        return run_of(lambda at: jnp.where(at < 2, 3, 0), chunk)

    def straight_parts(chunk):
        near = [(middle[chunk], inner), (second[chunk], outer)]
        far = [(second[chunk], inner), (middle[chunk], outer)]
        return [(near, near_rows(chunk)), (far, far_rows(chunk))]

    def both_part(chunk):
        buffers = [(both_in[chunk], inner), (both_out[chunk], outer)]
        return (buffers, near_rows(chunk) + far_rows(chunk))

    both_in, both_out = {}, {}

    def join(chunk, *after):
        both = jnp.concatenate([held_until(middle[chunk], *after), second[chunk]], axis=1)
        both_in[chunk] = lax.optimization_barrier(both)
        both_out[chunk] = forward(both_in[chunk])

    attend_chunk()
    attend_chunk()
    attend_chunk(pair[0])
    attend_chunk(second[0], middle[0], pair[1])
    join(1, own[3])
    parts = [own_part(chunk) for chunk in range(4)] + [pair_part(0), pair_part(1)] + straight_parts(0)
    total = add(None, parts, False, both_in[1], middle[2])
    join(2, total)
    total = add(total, [pair_part(2), pair_part(3), both_part(1)], False, both_in[2])
    join(3, total)
    total = add(total, [both_part(2)], False, both_in[3])
    return add(total, [both_part(3)], True)


def solution(mesh):
    in_specs = (
        P("resp", None, "mp"),
        P("resp", None, None),
        P("resp", None, None),
        P(None, "mp"),
        P(),
        P("resp", None),
        P("resp"),
        P("resp", None),
    )
    out_specs = P("resp", None, "mp")
    return jax.shard_map(
        on_device, mesh=mesh, in_specs=in_specs, out_specs=out_specs, check_vma=False
    )
```

```python
import functools
import math

import jax
import jax.numpy as jnp
from jax import lax
from jax.experimental import pallas as pl
from jax.experimental.pallas import tpu as pltpu
from jax.sharding import PartitionSpec as P

HQ = 32
KVH = 4
HD = 128
REACH = 3
SLOTS = 6
OFFSETS = tuple(range(1, REACH + 1)) + tuple(-hop for hop in range(1, REACH + 1))
FLIPS = (1, 2, 3, 5, 6, 7)
BLOCKS = 1 + len(OFFSETS)
LOG2E = math.log2(math.e)
VMEM_BYTES = 60 * 1024 * 1024


def flipped(value, bits):
    count = lax.axis_size("resp")
    return lax.ppermute(value, "resp", [(source, source ^ bits) for source in range(count)])


def shifted(value, axis, steps):
    count = lax.axis_size(axis)
    pairs = [(source, (source + steps) % count) for source in range(count)]
    return lax.ppermute(value, axis, pairs)


def pack_kernel(head_ref, keys_ref, values_ref, out_ref):
    del head_ref
    for tile in range(keys_ref.shape[1] // HD):
        rows = slice(tile * HD, (tile + 1) * HD)
        out_ref[0, rows, :] = keys_ref[0, rows, :].T
    out_ref[1] = values_ref[0]


def pack(kv_head, keys, values):
    seq_len = keys.shape[1]
    spec = pl.BlockSpec((1, seq_len, HD), lambda step, head: (0, 0, head[0]))
    return pl.pallas_call(
        pack_kernel,
        grid_spec=pltpu.PrefetchScalarGridSpec(
            num_scalar_prefetch=1,
            grid=(1,),
            in_specs=[spec, spec],
            out_specs=pl.BlockSpec((2, seq_len, HD), lambda step, head: (0, 0, 0)),
        ),
        out_shape=jax.ShapeDtypeStruct((2, seq_len, HD), keys.dtype),
        compiler_params=pltpu.CompilerParams(vmem_limit_bytes=60 * 1024 * 1024),
        cost_estimate=pl.CostEstimate(flops=0, bytes_accessed=8 * seq_len * HD, transcendentals=0),
        name="pack",
    )(kv_head, keys, values)


def gather_blocks(packed):
    if lax.axis_size("resp") != 8:
        return [packed] + [shifted(packed, "resp", -offset) for offset in OFFSETS]
    far = flipped(packed, 6)
    along_x = flipped(packed, 2)
    along_y = flipped(packed, 4)
    twin = flipped(packed, 1)
    return [
        packed, twin, along_x, flipped(along_x, 1), flipped(along_y, 1), far, flipped(far, 1)
    ]


def target_of(resp_self, resp_total, block):
    if resp_total == 8:
        return resp_self ^ FLIPS[block - 1]
    return lax.rem(resp_self + OFFSETS[block - 1] + resp_total, resp_total)


def attention_kernel(
    head_base, resp_total, where_ref, bias_ref, q_ref, *rest
):
    kv_refs = rest[:BLOCKS]
    out_ref, scores_ref, expo_ref, peak_ref, total_ref = rest[-5:]
    unit, rows = scores_ref.shape[:2]
    seq_len = kv_refs[0].shape[1]
    scale = LOG2E / math.sqrt(HD)

    hits = []
    for block in range(1, BLOCKS):
        target = target_of(where_ref[0], resp_total, block)
        hits.append(
            [(slot < where_ref[1]) & (where_ref[2 + slot] == target) for slot in range(SLOTS)]
        )

    def bias_of(member, block):
        if block == 0:
            return jnp.float32(0.0)
        found = jnp.float32(-jnp.inf)
        for slot in range(SLOTS):
            offset = bias_ref[slot, head_base + member] * LOG2E
            found = jnp.where(hits[block - 1][slot], offset, found)
        return found

    bias = [[bias_of(member, block) for block in range(BLOCKS)] for member in range(unit)]
    ones = jnp.ones((seq_len, HD), jnp.bfloat16)

    def cols(block):
        return slice(block * seq_len, (block + 1) * seq_len)

    def score(member, block):
        keys = jnp.concatenate(
            [kv_refs[block][0, tile : tile + HD, :] for tile in range(0, seq_len, HD)], axis=1
        )
        scores = jnp.dot(
            q_ref[0, :, member * HD : (member + 1) * HD], keys, preferred_element_type=jnp.float32
        )
        if block == 0:
            row_ids = lax.broadcasted_iota(jnp.int32, scores.shape, 0)
            col_ids = lax.broadcasted_iota(jnp.int32, scores.shape, 1)
            scores = jnp.where(row_ids >= col_ids, scores, -jnp.inf)
        scores_ref[member, :, cols(block)] = scores
        part = scores[:, :HD]
        for lane in range(HD, seq_len, HD):
            part = jnp.maximum(part, scores[:, lane : lane + HD])
        part = part * scale + bias[member][block]
        peak_ref[member] = part if block == 0 else jnp.maximum(peak_ref[member], part)

    def settle(member):
        peak = jnp.max(peak_ref[member], axis=1, keepdims=True)
        peak_ref[member] = jnp.broadcast_to(peak, (rows, HD))

    def expo(member, block):
        offset = bias[member][block] - peak_ref[member]
        scores = scores_ref[member, :, cols(block)]
        shift = jnp.concatenate([offset] * (seq_len // HD), axis=1)
        expo_ref[member, :, cols(block)] = jnp.exp2(scores * scale + shift).astype(jnp.bfloat16)

    def attend(member, block):
        if block % 2 == 1 or block == BLOCKS - 1:
            low = block - block % 2
            wide = jnp.concatenate(
                [
                    jnp.concatenate([kv_refs[held][1], ones], axis=1)
                    for held in range(low, block + 1)
                ],
                axis=0,
            )
            term = jnp.dot(
                expo_ref[member, :, low * seq_len : (block + 1) * seq_len],
                wide,
                preferred_element_type=jnp.float32,
            )
            total_ref[member] = term if low == 0 else total_ref[member] + term

    def finish(member):
        total = total_ref[member]
        out_ref[:, member * HD : (member + 1) * HD] = (total[:, :HD] / total[:, HD:]).astype(
            out_ref.dtype
        )

    for stage in range(unit + 2):
        for block in range(BLOCKS):
            if 0 <= stage - 2 < unit:
                attend(stage - 2, block)
            if 0 <= stage - 1 < unit:
                expo(stage - 1, block)
            if stage < unit:
                score(stage, block)
        if stage < unit:
            settle(stage)
        if 0 <= stage - 2 < unit:
            finish(stage - 2)


def attention(where, slot_bias, queries, kv_blocks, head_base, heads, resp_total):
    seq_len = queries.shape[1]
    unit = 2 if heads % 2 == 0 else 1
    smem = pl.BlockSpec(memory_space=pltpu.SMEM)
    whole = pl.BlockSpec(kv_blocks[0].shape, lambda step: (0, 0, 0))
    keys_all = BLOCKS * seq_len
    return pl.pallas_call(
        functools.partial(attention_kernel, head_base, resp_total),
        grid=(heads // unit,),
        in_specs=[smem] * 2
        + [pl.BlockSpec((1, seq_len, unit * HD), lambda step: (0, 0, head_base // unit + step))]
        + [whole] * BLOCKS,
        out_specs=pl.BlockSpec((seq_len, unit * HD), lambda step: (0, step)),
        out_shape=jax.ShapeDtypeStruct((seq_len, heads * HD), jnp.bfloat16),
        scratch_shapes=[
            pltpu.VMEM((unit, seq_len, keys_all), jnp.float32),
            pltpu.VMEM((unit, seq_len, keys_all), jnp.bfloat16),
            pltpu.VMEM((unit, seq_len, HD), jnp.float32),
            pltpu.VMEM((unit, seq_len, 2 * HD), jnp.float32),
        ],
        compiler_params=pltpu.CompilerParams(vmem_limit_bytes=51 * 1024 * 1024),
        cost_estimate=pl.CostEstimate(
            flops=heads * seq_len * keys_all * HD * 6,
            bytes_accessed=2 * seq_len * HD * (2 * heads + 2 * BLOCKS),
            transcendentals=heads * seq_len * keys_all,
        ),
        name="attend",
    )(where, slot_bias, queries, *kv_blocks)


def project_kernel(parts, start, final, place_ref, weight_ref, *refs):
    buffers = refs[: sum(len(kinds) for kinds, _ in parts)]
    total_ref = None if start else refs[len(buffers)]
    out_ref, left_ref, right_ref, held_ref, made_ref, left_sems, right_sems, total_sems, out_sems = refs[-9:]
    steps, _, step = right_ref.shape
    place = place_ref[0]

    def tile(ref, at):
        return ref.at[0, :, pl.ds(at * step, step)] if final else ref.at[at]

    def sources():
        taken = first = 0
        for index, (kinds, rows) in enumerate(parts):
            width = sum(count for _, count in rows)
            target = left_ref.at[:, pl.ds(first, width)]
            found = [
                (
                    kinds[other],
                    functools.partial(
                        pltpu.make_async_copy, buffers[taken + other], target, left_sems.at[index]
                    ),
                )
                for other in range(len(kinds))
            ]
            yield found
            taken += len(kinds)
            first += width

    def weights(at):
        found, first = [], 0
        for _, rows in parts:
            for row, count in rows:
                found.append(
                    pltpu.make_async_copy(
                        weight_ref.at[pl.ds(pl.multiple_of(row(place), HD), count), pl.ds(at * step, step)],
                        right_ref.at[at, pl.ds(first, count), :],
                        right_sems.at[at, len(found)],
                    )
                )
                first += count
        return found

    def totals(at):
        return [] if start else [pltpu.make_async_copy(total_ref.at[at], held_ref.at[at], total_sems.at[at])]

    for found in sources():
        for places, make in found:
            if len(found) == 1:
                make().start()
            else:
                wanted = functools.reduce(jnp.logical_or, [place == at for at in places])
                pl.when(wanted)(lambda make=make: make().start())
    for at in range(steps):
        for copy in weights(at) + totals(at):
            copy.start()
    for found in sources():
        found[0][1]().wait()
    leaving = []
    for at in range(steps):
        for copy in weights(at) + totals(at):
            copy.wait()
        total = jnp.dot(left_ref[...], right_ref[at], preferred_element_type=jnp.float32)
        if not start:
            total = total + held_ref[at]
        made_ref[at] = total.astype(made_ref.dtype)
        leaving.append(pltpu.make_async_copy(made_ref.at[at], tile(out_ref, at), out_sems.at[at]))
        leaving[at].start()
    for copy in leaving:
        copy.wait()


def project(place, total, parts, weight, final):
    seq_len = parts[0][0][0][0].shape[0]
    out_width = weight.shape[1]
    step = min(out_width, 512)
    steps = out_width // step
    operands, kinds = [weight], []
    depth = runs = 0
    for buffers, rows in parts:
        kinds.append((tuple(tuple(places) for _, places in buffers), tuple(rows)))
        operands += [buffer for buffer, _ in buffers]
        depth += sum(count for _, count in rows)
        runs += len(rows)
    if total is not None:
        operands.append(total)
    there = pl.BlockSpec(memory_space=pl.ANY)
    if final:
        out_shape = jax.ShapeDtypeStruct((1, seq_len, out_width), jnp.bfloat16)
    else:
        out_shape = jax.ShapeDtypeStruct((steps, seq_len, step), jnp.float32)
    return pl.pallas_call(
        functools.partial(project_kernel, tuple(kinds), total is None, final),
        in_specs=[pl.BlockSpec(memory_space=pltpu.SMEM)] + [there] * len(operands),
        out_specs=there,
        out_shape=out_shape,
        scratch_shapes=[
            pltpu.VMEM((seq_len, depth), jnp.bfloat16),
            pltpu.VMEM((steps, depth, step), weight.dtype),
            pltpu.VMEM((1 if total is None else steps, seq_len, step), jnp.float32),
            pltpu.VMEM((steps, seq_len, step), out_shape.dtype),
            pltpu.SemaphoreType.DMA((len(parts),)),
            pltpu.SemaphoreType.DMA((steps, runs)),
            pltpu.SemaphoreType.DMA((steps,)),
            pltpu.SemaphoreType.DMA((steps,)),
        ],
        compiler_params=pltpu.CompilerParams(vmem_limit_bytes=52 * 1024 * 1024),
        cost_estimate=pl.CostEstimate(
            flops=2 * seq_len * depth * out_width,
            bytes_accessed=2 * depth * (seq_len + out_width) + 8 * seq_len * out_width,
            transcendentals=0,
        ),
        name="project",
    )(place, *operands)


def along_line(value, pairs):
    return lax.ppermute(value, "mp", pairs)


def on_device(queries, keys, values, out_weight, order_bias, partners, count, order):
    heads_dev = queries.shape[2] // HD
    group_size = HQ // KVH
    resp_total = lax.axis_size("resp")
    mp_total = lax.axis_size("mp")
    line = lax.axis_index("mp")
    first_head = line * heads_dev
    kv_head = (first_head // group_size).astype(jnp.int32)
    packed = pack(kv_head.reshape(1), keys, values)
    kv_blocks = gather_blocks(packed)
    resp_self = lax.axis_index("resp").astype(jnp.int32).reshape(1)
    where = jnp.concatenate([resp_self, count, partners[0]])
    bias_dev = lax.dynamic_slice_in_dim(order_bias, first_head, heads_dev, 1)
    slot_bias = jnp.where(order[0][:, None] == 1, bias_dev[1][None, :], bias_dev[0][None, :])
    place = line.astype(jnp.int32).reshape(1)

    def held_until(value, *after):
        return lax.optimization_barrier((value,) + after)[0]

    def attended_of(head_base, heads, *after):
        return attention(
            held_until(where, *after), slot_bias, queries, kv_blocks, head_base, heads, resp_total
        )

    def add(total, parts, final, *after):
        return project(held_until(place, *after), total, parts, out_weight, final)

    device_rows = heads_dev * HD
    if mp_total != 4 or heads_dev % 4:
        pieces = [attended_of(head, 1) for head in range(heads_dev)]
        gathered = lax.all_gather(jnp.concatenate(pieces, axis=1), "mp", axis=0, tiled=False)
        parts = [
            ([(gathered[source], ())], [(lambda at, source=source: source * device_rows, device_rows)])
            for source in range(mp_total)
        ]
        return add(None, parts, True)

    chunks = 4
    chunk_heads = heads_dev // chunks
    rows = chunk_heads * HD
    inner, outer = (1, 2), (0, 3)
    own, pair, middle, second = [], [], [], []

    def attend_chunk(*after):
        chunk = len(own)
        own.append(attended_of(chunk * chunk_heads, chunk_heads, *after))
        pair.append(along_line(own[chunk], [(0, 1), (1, 0), (2, 3), (3, 2)]))
        if chunk == 0:
            middle.append(along_line(own[chunk], [(0, 3), (1, 2), (2, 1), (3, 0)]))
            second.append(along_line(own[chunk], [(0, 2), (2, 0), (1, 3), (3, 1)]))
        else:
            middle.append(along_line(own[chunk], [(1, 2), (2, 1)]))
            second.append(along_line(own[chunk], [(0, 2), (3, 1)]))

    def forward(held):
        return along_line(held, [(1, 0), (2, 3)])

    def run_of(source, chunk):
        return [(lambda at: source(at) * device_rows + chunk * rows, rows)]

    def own_part(chunk):
        return ([(own[chunk], ())], run_of(lambda at: at, chunk))

    def pair_part(chunk):
        return ([(pair[chunk], ())], run_of(lambda at: at ^ 1, chunk))

    def near_rows(chunk):
        return run_of(lambda at: jnp.where(at < 2, 2, 1), chunk)

    def far_rows(chunk):
        return run_of(lambda at: jnp.where(at < 2, 3, 0), chunk)

    def straight_parts(chunk):
        near = [(middle[chunk], inner), (second[chunk], outer)]
        far = [(second[chunk], inner), (middle[chunk], outer)]
        return [(near, near_rows(chunk)), (far, far_rows(chunk))]

    def both_part(chunk):
        buffers = [(both_in[chunk], inner), (both_out[chunk], outer)]
        return (buffers, near_rows(chunk) + far_rows(chunk))

    both_in, both_out = {}, {}

    def join(chunk, *after):
        both = jnp.concatenate([held_until(middle[chunk], *after), second[chunk]], axis=1)
        both_in[chunk] = lax.optimization_barrier(both)
        both_out[chunk] = forward(both_in[chunk])

    attend_chunk()
    attend_chunk()
    attend_chunk()
    attend_chunk(pair[0], second[0], middle[0])
    join(1, own[3])
    parts = [own_part(chunk) for chunk in range(4)] + [pair_part(0), pair_part(1)] + straight_parts(0)
    total = add(None, parts, False, both_in[1], middle[2])
    join(2, total)
    total = add(total, [pair_part(2), pair_part(3), both_part(1)], False, both_in[2])
    join(3, total)
    total = add(total, [both_part(2)], False, both_in[3])
    return add(total, [both_part(3)], True)


def solution(mesh):
    in_specs = (
        P("resp", None, "mp"),
        P("resp", None, None),
        P("resp", None, None),
        P(None, "mp"),
        P(),
        P("resp", None),
        P("resp"),
        P("resp", None),
    )
    out_specs = P("resp", None, "mp")
    return jax.shard_map(
        on_device, mesh=mesh, in_specs=in_specs, out_specs=out_specs, check_vma=False
    )
```

```python
import functools
import math

import jax
import jax.numpy as jnp
from jax import lax
from jax.experimental import pallas as pl
from jax.experimental.pallas import tpu as pltpu
from jax.sharding import PartitionSpec as P

HQ = 32
KVH = 4
HD = 128
REACH = 3
SLOTS = 6
OFFSETS = tuple(range(1, REACH + 1)) + tuple(-hop for hop in range(1, REACH + 1))
FLIPS = (1, 2, 3, 5, 6, 7)
BLOCKS = 1 + len(OFFSETS)
LOG2E = math.log2(math.e)
VMEM_BYTES = 60 * 1024 * 1024


def flipped(value, bits):
    count = lax.axis_size("resp")
    return lax.ppermute(value, "resp", [(source, source ^ bits) for source in range(count)])


def shifted(value, axis, steps):
    count = lax.axis_size(axis)
    pairs = [(source, (source + steps) % count) for source in range(count)]
    return lax.ppermute(value, axis, pairs)


def pack_kernel(head_ref, keys_ref, values_ref, out_ref):
    del head_ref
    for tile in range(keys_ref.shape[1] // HD):
        rows = slice(tile * HD, (tile + 1) * HD)
        out_ref[0, rows, :] = keys_ref[0, rows, :].T
    out_ref[1] = values_ref[0]


def pack(kv_head, keys, values):
    seq_len = keys.shape[1]
    spec = pl.BlockSpec((1, seq_len, HD), lambda step, head: (0, 0, head[0]))
    return pl.pallas_call(
        pack_kernel,
        grid_spec=pltpu.PrefetchScalarGridSpec(
            num_scalar_prefetch=1,
            grid=(1,),
            in_specs=[spec, spec],
            out_specs=pl.BlockSpec((2, seq_len, HD), lambda step, head: (0, 0, 0)),
        ),
        out_shape=jax.ShapeDtypeStruct((2, seq_len, HD), keys.dtype),
        compiler_params=pltpu.CompilerParams(vmem_limit_bytes=60 * 1024 * 1024),
        cost_estimate=pl.CostEstimate(flops=0, bytes_accessed=8 * seq_len * HD, transcendentals=0),
        name="pack",
    )(kv_head, keys, values)


def gather_blocks(packed):
    if lax.axis_size("resp") != 8:
        return [packed] + [shifted(packed, "resp", -offset) for offset in OFFSETS]
    far = flipped(packed, 6)
    along_x = flipped(packed, 2)
    along_y = flipped(packed, 4)
    twin = flipped(packed, 1)
    return [
        packed, twin, along_x, flipped(along_x, 1), flipped(along_y, 1), far, flipped(far, 1)
    ]


def target_of(resp_self, resp_total, block):
    if resp_total == 8:
        return resp_self ^ FLIPS[block - 1]
    return lax.rem(resp_self + OFFSETS[block - 1] + resp_total, resp_total)


def attention_kernel(
    head_base, resp_total, where_ref, bias_ref, q_ref, *rest
):
    kv_refs = rest[:BLOCKS]
    out_ref, scores_ref, expo_ref, peak_ref, total_ref = rest[-5:]
    unit, rows = scores_ref.shape[:2]
    seq_len = kv_refs[0].shape[1]
    scale = LOG2E / math.sqrt(HD)

    hits = []
    for block in range(1, BLOCKS):
        target = target_of(where_ref[0], resp_total, block)
        hits.append(
            [(slot < where_ref[1]) & (where_ref[2 + slot] == target) for slot in range(SLOTS)]
        )

    def bias_of(member, block):
        if block == 0:
            return jnp.float32(0.0)
        found = jnp.float32(-jnp.inf)
        for slot in range(SLOTS):
            offset = bias_ref[slot, head_base + member] * LOG2E
            found = jnp.where(hits[block - 1][slot], offset, found)
        return found

    bias = [[bias_of(member, block) for block in range(BLOCKS)] for member in range(unit)]
    ones = jnp.ones((seq_len, HD), jnp.bfloat16)

    def cols(block):
        return slice(block * seq_len, (block + 1) * seq_len)

    def score(member, block):
        keys = jnp.concatenate(
            [kv_refs[block][0, tile : tile + HD, :] for tile in range(0, seq_len, HD)], axis=1
        )
        scores = jnp.dot(
            q_ref[0, :, member * HD : (member + 1) * HD], keys, preferred_element_type=jnp.float32
        )
        if block == 0:
            row_ids = lax.broadcasted_iota(jnp.int32, scores.shape, 0)
            col_ids = lax.broadcasted_iota(jnp.int32, scores.shape, 1)
            scores = jnp.where(row_ids >= col_ids, scores, -jnp.inf)
        scores_ref[member, :, cols(block)] = scores
        part = scores[:, :HD]
        for lane in range(HD, seq_len, HD):
            part = jnp.maximum(part, scores[:, lane : lane + HD])
        part = part * scale + bias[member][block]
        peak_ref[member] = part if block == 0 else jnp.maximum(peak_ref[member], part)

    def settle(member):
        peak = jnp.max(peak_ref[member], axis=1, keepdims=True)
        peak_ref[member] = jnp.broadcast_to(peak, (rows, HD))

    def expo(member, block):
        offset = bias[member][block] - peak_ref[member]
        scores = scores_ref[member, :, cols(block)]
        shift = jnp.concatenate([offset] * (seq_len // HD), axis=1)
        expo_ref[member, :, cols(block)] = jnp.exp2(scores * scale + shift).astype(jnp.bfloat16)

    def attend(member, block):
        if block % 2 == 1 or block == BLOCKS - 1:
            low = block - block % 2
            wide = jnp.concatenate(
                [
                    jnp.concatenate([kv_refs[held][1], ones], axis=1)
                    for held in range(low, block + 1)
                ],
                axis=0,
            )
            term = jnp.dot(
                expo_ref[member, :, low * seq_len : (block + 1) * seq_len],
                wide,
                preferred_element_type=jnp.float32,
            )
            total_ref[member] = term if low == 0 else total_ref[member] + term

    def finish(member):
        total = total_ref[member]
        out_ref[:, member * HD : (member + 1) * HD] = (total[:, :HD] / total[:, HD:]).astype(
            out_ref.dtype
        )

    for stage in range(unit + 2):
        for block in range(BLOCKS):
            if 0 <= stage - 2 < unit:
                attend(stage - 2, block)
            if 0 <= stage - 1 < unit:
                expo(stage - 1, block)
            if stage < unit:
                score(stage, block)
        if stage < unit:
            settle(stage)
        if 0 <= stage - 2 < unit:
            finish(stage - 2)


def attention(where, slot_bias, queries, kv_blocks, head_base, heads, resp_total):
    seq_len = queries.shape[1]
    unit = 2 if heads % 2 == 0 else 1
    smem = pl.BlockSpec(memory_space=pltpu.SMEM)
    whole = pl.BlockSpec(kv_blocks[0].shape, lambda step: (0, 0, 0))
    keys_all = BLOCKS * seq_len
    return pl.pallas_call(
        functools.partial(attention_kernel, head_base, resp_total),
        grid=(heads // unit,),
        in_specs=[smem] * 2
        + [pl.BlockSpec((1, seq_len, unit * HD), lambda step: (0, 0, head_base // unit + step))]
        + [whole] * BLOCKS,
        out_specs=pl.BlockSpec((seq_len, unit * HD), lambda step: (0, step)),
        out_shape=jax.ShapeDtypeStruct((seq_len, heads * HD), jnp.bfloat16),
        scratch_shapes=[
            pltpu.VMEM((unit, seq_len, keys_all), jnp.float32),
            pltpu.VMEM((unit, seq_len, keys_all), jnp.bfloat16),
            pltpu.VMEM((unit, seq_len, HD), jnp.float32),
            pltpu.VMEM((unit, seq_len, 2 * HD), jnp.float32),
        ],
        compiler_params=pltpu.CompilerParams(vmem_limit_bytes=51 * 1024 * 1024),
        cost_estimate=pl.CostEstimate(
            flops=heads * seq_len * keys_all * HD * 6,
            bytes_accessed=2 * seq_len * HD * (2 * heads + 2 * BLOCKS),
            transcendentals=heads * seq_len * keys_all,
        ),
        name="attend",
    )(where, slot_bias, queries, *kv_blocks)


def project_kernel(parts, start, final, place_ref, weight_ref, *refs):
    buffers = refs[: sum(len(kinds) for kinds, _ in parts)]
    total_ref = None if start else refs[len(buffers)]
    out_ref, left_ref, right_ref, held_ref, made_ref, left_sems, right_sems, total_sems, out_sems = refs[-9:]
    steps, _, step = right_ref.shape
    place = place_ref[0]

    def tile(ref, at):
        return ref.at[0, :, pl.ds(at * step, step)] if final else ref.at[at]

    def sources():
        taken = first = 0
        for index, (kinds, rows) in enumerate(parts):
            width = sum(count for _, count in rows)
            target = left_ref.at[:, pl.ds(first, width)]
            found = [
                (
                    kinds[other],
                    functools.partial(
                        pltpu.make_async_copy, buffers[taken + other], target, left_sems.at[index]
                    ),
                )
                for other in range(len(kinds))
            ]
            yield found
            taken += len(kinds)
            first += width

    def weights(at):
        found, first = [], 0
        for _, rows in parts:
            for row, count in rows:
                found.append(
                    pltpu.make_async_copy(
                        weight_ref.at[pl.ds(pl.multiple_of(row(place), HD), count), pl.ds(at * step, step)],
                        right_ref.at[at, pl.ds(first, count), :],
                        right_sems.at[at, len(found)],
                    )
                )
                first += count
        return found

    def totals(at):
        return [] if start else [pltpu.make_async_copy(total_ref.at[at], held_ref.at[at], total_sems.at[at])]

    for found in sources():
        for places, make in found:
            if len(found) == 1:
                make().start()
            else:
                wanted = functools.reduce(jnp.logical_or, [place == at for at in places])
                pl.when(wanted)(lambda make=make: make().start())
    for at in range(steps):
        for copy in weights(at) + totals(at):
            copy.start()
    for found in sources():
        found[0][1]().wait()
    leaving = []
    for at in range(steps):
        for copy in weights(at) + totals(at):
            copy.wait()
        total = jnp.dot(left_ref[...], right_ref[at], preferred_element_type=jnp.float32)
        if not start:
            total = total + held_ref[at]
        made_ref[at] = total.astype(made_ref.dtype)
        leaving.append(pltpu.make_async_copy(made_ref.at[at], tile(out_ref, at), out_sems.at[at]))
        leaving[at].start()
    for copy in leaving:
        copy.wait()


def project(place, total, parts, weight, final):
    seq_len = parts[0][0][0][0].shape[0]
    out_width = weight.shape[1]
    step = min(out_width, 512)
    steps = out_width // step
    operands, kinds = [weight], []
    depth = runs = 0
    for buffers, rows in parts:
        kinds.append((tuple(tuple(places) for _, places in buffers), tuple(rows)))
        operands += [buffer for buffer, _ in buffers]
        depth += sum(count for _, count in rows)
        runs += len(rows)
    if total is not None:
        operands.append(total)
    there = pl.BlockSpec(memory_space=pl.ANY)
    if final:
        out_shape = jax.ShapeDtypeStruct((1, seq_len, out_width), jnp.bfloat16)
    else:
        out_shape = jax.ShapeDtypeStruct((steps, seq_len, step), jnp.float32)
    return pl.pallas_call(
        functools.partial(project_kernel, tuple(kinds), total is None, final),
        in_specs=[pl.BlockSpec(memory_space=pltpu.SMEM)] + [there] * len(operands),
        out_specs=there,
        out_shape=out_shape,
        scratch_shapes=[
            pltpu.VMEM((seq_len, depth), jnp.bfloat16),
            pltpu.VMEM((steps, depth, step), weight.dtype),
            pltpu.VMEM((1 if total is None else steps, seq_len, step), jnp.float32),
            pltpu.VMEM((steps, seq_len, step), out_shape.dtype),
            pltpu.SemaphoreType.DMA((len(parts),)),
            pltpu.SemaphoreType.DMA((steps, runs)),
            pltpu.SemaphoreType.DMA((steps,)),
            pltpu.SemaphoreType.DMA((steps,)),
        ],
        compiler_params=pltpu.CompilerParams(vmem_limit_bytes=52 * 1024 * 1024),
        cost_estimate=pl.CostEstimate(
            flops=2 * seq_len * depth * out_width,
            bytes_accessed=2 * depth * (seq_len + out_width) + 8 * seq_len * out_width,
            transcendentals=0,
        ),
        name="project",
    )(place, *operands)


def along_line(value, pairs):
    return lax.ppermute(value, "mp", pairs)


def on_device(queries, keys, values, out_weight, order_bias, partners, count, order):
    heads_dev = queries.shape[2] // HD
    group_size = HQ // KVH
    resp_total = lax.axis_size("resp")
    mp_total = lax.axis_size("mp")
    line = lax.axis_index("mp")
    first_head = line * heads_dev
    kv_head = (first_head // group_size).astype(jnp.int32)
    packed = pack(kv_head.reshape(1), keys, values)
    kv_blocks = gather_blocks(packed)
    resp_self = lax.axis_index("resp").astype(jnp.int32).reshape(1)
    where = jnp.concatenate([resp_self, count, partners[0]])
    bias_dev = lax.dynamic_slice_in_dim(order_bias, first_head, heads_dev, 1)
    slot_bias = jnp.where(order[0][:, None] == 1, bias_dev[1][None, :], bias_dev[0][None, :])
    place = line.astype(jnp.int32).reshape(1)

    def held_until(value, *after):
        return lax.optimization_barrier((value,) + after)[0]

    def attended_of(head_base, heads, *after):
        return attention(
            held_until(where, *after), slot_bias, queries, kv_blocks, head_base, heads, resp_total
        )

    def add(total, parts, final, *after):
        return project(held_until(place, *after), total, parts, out_weight, final)

    device_rows = heads_dev * HD
    if mp_total != 4 or heads_dev % 4:
        pieces = [attended_of(head, 1) for head in range(heads_dev)]
        gathered = lax.all_gather(jnp.concatenate(pieces, axis=1), "mp", axis=0, tiled=False)
        parts = [
            ([(gathered[source], ())], [(lambda at, source=source: source * device_rows, device_rows)])
            for source in range(mp_total)
        ]
        return add(None, parts, True)

    chunks = 4
    chunk_heads = heads_dev // chunks
    rows = chunk_heads * HD
    inner, outer = (1, 2), (0, 3)
    straight = (0, 1)
    own, pair, middle, second, near_out, far_out = [], [], [], [], [], []

    def attend_chunk(*after):
        chunk = len(own)
        own.append(attended_of(chunk * chunk_heads, chunk_heads, *after))
        pair.append(along_line(own[chunk], [(0, 1), (1, 0), (2, 3), (3, 2)]))
        middle.append(along_line(own[chunk], [(1, 2), (2, 1)]))
        if chunk in straight:
            second.append(along_line(own[chunk], [(0, 2), (2, 0), (1, 3), (3, 1)]))
            near_out.append(second[chunk])
        else:
            second.append(along_line(own[chunk], [(0, 2), (3, 1)]))

    def forward(held):
        return along_line(held, [(1, 0), (2, 3)])

    def run_of(source, chunk):
        return [(lambda at: source(at) * device_rows + chunk * rows, rows)]

    def own_part(chunk):
        return ([(own[chunk], ())], run_of(lambda at: at, chunk))

    def pair_part(chunk):
        return ([(pair[chunk], ())], run_of(lambda at: at ^ 1, chunk))

    def near_part(chunk):
        row = run_of(lambda at: jnp.where(at < 2, 2, 1), chunk)
        return ([(middle[chunk], inner), (near_out[chunk], outer)], row)

    def far_part(chunk):
        row = run_of(lambda at: jnp.where(at < 2, 3, 0), chunk)
        return ([(second[chunk], inner), (far_out[chunk], outer)], row)

    attend_chunk()
    attend_chunk()
    attend_chunk(pair[0])
    far_out.append(forward(held_until(second[0], own[2])))
    attend_chunk(second[0], middle[0], pair[1])
    far_out.append(forward(held_until(second[1], own[3])))
    parts = [own_part(chunk) for chunk in range(4)] + [pair_part(chunk) for chunk in range(3)]
    total = add(None, parts, False, second[1], middle[1], middle[2], far_out[0])
    near_out.append(forward(held_until(middle[2], total)))
    far_out.append(forward(held_until(second[2], total)))
    near_out.append(forward(held_until(middle[3], total)))
    far_out.append(forward(held_until(second[3], total)))
    parts = [pair_part(3), near_part(0), near_part(1), far_part(0), far_part(1)]
    total = add(total, parts, False, middle[3], second[3], second[2])
    total = add(total, [near_part(2), far_part(2)], False, near_out[3])
    return add(total, [near_part(3), far_part(3)], True)


def solution(mesh):
    in_specs = (
        P("resp", None, "mp"),
        P("resp", None, None),
        P("resp", None, None),
        P(None, "mp"),
        P(),
        P("resp", None),
        P("resp"),
        P("resp", None),
    )
    out_specs = P("resp", None, "mp")
    return jax.shard_map(
        on_device, mesh=mesh, in_specs=in_specs, out_specs=out_specs, check_vma=False
    )
```

```python
import functools
import math

import jax
import jax.numpy as jnp
from jax import lax
from jax.experimental import pallas as pl
from jax.experimental.pallas import tpu as pltpu
from jax.sharding import PartitionSpec as P

HQ = 32
KVH = 4
HD = 128
REACH = 3
SLOTS = 6
OFFSETS = tuple(range(1, REACH + 1)) + tuple(-hop for hop in range(1, REACH + 1))
FLIPS = (1, 2, 3, 5, 6, 7)
BLOCKS = 1 + len(OFFSETS)
LOG2E = math.log2(math.e)
VMEM_BYTES = 60 * 1024 * 1024


def flipped(value, bits):
    count = lax.axis_size("resp")
    return lax.ppermute(value, "resp", [(source, source ^ bits) for source in range(count)])


def shifted(value, axis, steps):
    count = lax.axis_size(axis)
    pairs = [(source, (source + steps) % count) for source in range(count)]
    return lax.ppermute(value, axis, pairs)


def pack_kernel(head_ref, keys_ref, values_ref, out_ref):
    del head_ref
    for tile in range(keys_ref.shape[1] // HD):
        rows = slice(tile * HD, (tile + 1) * HD)
        out_ref[0, rows, :] = keys_ref[0, rows, :].T
    out_ref[1] = values_ref[0]


def pack(kv_head, keys, values):
    seq_len = keys.shape[1]
    spec = pl.BlockSpec((1, seq_len, HD), lambda step, head: (0, 0, head[0]))
    return pl.pallas_call(
        pack_kernel,
        grid_spec=pltpu.PrefetchScalarGridSpec(
            num_scalar_prefetch=1,
            grid=(1,),
            in_specs=[spec, spec],
            out_specs=pl.BlockSpec((2, seq_len, HD), lambda step, head: (0, 0, 0)),
        ),
        out_shape=jax.ShapeDtypeStruct((2, seq_len, HD), keys.dtype),
        compiler_params=pltpu.CompilerParams(vmem_limit_bytes=60 * 1024 * 1024),
        cost_estimate=pl.CostEstimate(flops=0, bytes_accessed=8 * seq_len * HD, transcendentals=0),
        name="pack",
    )(kv_head, keys, values)


def gather_blocks(packed):
    if lax.axis_size("resp") != 8:
        return [packed] + [shifted(packed, "resp", -offset) for offset in OFFSETS]
    far = flipped(packed, 6)
    along_x = flipped(packed, 2)
    along_y = flipped(packed, 4)
    twin = flipped(packed, 1)
    return [
        packed, twin, along_x, flipped(along_x, 1), flipped(along_y, 1), far, flipped(far, 1)
    ]


def target_of(resp_self, resp_total, block):
    if resp_total == 8:
        return resp_self ^ FLIPS[block - 1]
    return lax.rem(resp_self + OFFSETS[block - 1] + resp_total, resp_total)


def attention_kernel(
    head_base, resp_total, where_ref, bias_ref, q_ref, *rest
):
    kv_refs = rest[:BLOCKS]
    out_ref, scores_ref, expo_ref, peak_ref, total_ref = rest[-5:]
    unit, rows = scores_ref.shape[:2]
    seq_len = kv_refs[0].shape[1]
    scale = LOG2E / math.sqrt(HD)

    hits = []
    for block in range(1, BLOCKS):
        target = target_of(where_ref[0], resp_total, block)
        hits.append(
            [(slot < where_ref[1]) & (where_ref[2 + slot] == target) for slot in range(SLOTS)]
        )

    def bias_of(member, block):
        if block == 0:
            return jnp.float32(0.0)
        found = jnp.float32(-jnp.inf)
        for slot in range(SLOTS):
            offset = bias_ref[slot, head_base + member] * LOG2E
            found = jnp.where(hits[block - 1][slot], offset, found)
        return found

    bias = [[bias_of(member, block) for block in range(BLOCKS)] for member in range(unit)]
    ones = jnp.ones((seq_len, HD), jnp.bfloat16)

    def cols(block):
        return slice(block * seq_len, (block + 1) * seq_len)

    def score(member, block):
        keys = jnp.concatenate(
            [kv_refs[block][0, tile : tile + HD, :] for tile in range(0, seq_len, HD)], axis=1
        )
        scores = jnp.dot(
            q_ref[0, :, member * HD : (member + 1) * HD], keys, preferred_element_type=jnp.float32
        )
        if block == 0:
            row_ids = lax.broadcasted_iota(jnp.int32, scores.shape, 0)
            col_ids = lax.broadcasted_iota(jnp.int32, scores.shape, 1)
            scores = jnp.where(row_ids >= col_ids, scores, -jnp.inf)
        scores_ref[member, :, cols(block)] = scores
        part = scores[:, :HD]
        for lane in range(HD, seq_len, HD):
            part = jnp.maximum(part, scores[:, lane : lane + HD])
        part = part * scale + bias[member][block]
        peak_ref[member] = part if block == 0 else jnp.maximum(peak_ref[member], part)

    def settle(member):
        peak = jnp.max(peak_ref[member], axis=1, keepdims=True)
        peak_ref[member] = jnp.broadcast_to(peak, (rows, HD))

    def expo(member, block):
        offset = bias[member][block] - peak_ref[member]
        scores = scores_ref[member, :, cols(block)]
        shift = jnp.concatenate([offset] * (seq_len // HD), axis=1)
        expo_ref[member, :, cols(block)] = jnp.exp2(scores * scale + shift).astype(jnp.bfloat16)

    def attend(member, block):
        if block % 2 == 1 or block == BLOCKS - 1:
            low = block - block % 2
            wide = jnp.concatenate(
                [
                    jnp.concatenate([kv_refs[held][1], ones], axis=1)
                    for held in range(low, block + 1)
                ],
                axis=0,
            )
            term = jnp.dot(
                expo_ref[member, :, low * seq_len : (block + 1) * seq_len],
                wide,
                preferred_element_type=jnp.float32,
            )
            total_ref[member] = term if low == 0 else total_ref[member] + term

    def finish(member):
        total = total_ref[member]
        out_ref[:, member * HD : (member + 1) * HD] = (total[:, :HD] / total[:, HD:]).astype(
            out_ref.dtype
        )

    for stage in range(unit + 2):
        for block in range(BLOCKS):
            if 0 <= stage - 2 < unit:
                attend(stage - 2, block)
            if 0 <= stage - 1 < unit:
                expo(stage - 1, block)
            if stage < unit:
                score(stage, block)
        if stage < unit:
            settle(stage)
        if 0 <= stage - 2 < unit:
            finish(stage - 2)


def attention(where, slot_bias, queries, kv_blocks, head_base, heads, resp_total):
    seq_len = queries.shape[1]
    unit = 2 if heads % 2 == 0 else 1
    smem = pl.BlockSpec(memory_space=pltpu.SMEM)
    whole = pl.BlockSpec(kv_blocks[0].shape, lambda step: (0, 0, 0))
    keys_all = BLOCKS * seq_len
    return pl.pallas_call(
        functools.partial(attention_kernel, head_base, resp_total),
        grid=(heads // unit,),
        in_specs=[smem] * 2
        + [pl.BlockSpec((1, seq_len, unit * HD), lambda step: (0, 0, head_base // unit + step))]
        + [whole] * BLOCKS,
        out_specs=pl.BlockSpec((seq_len, unit * HD), lambda step: (0, step)),
        out_shape=jax.ShapeDtypeStruct((seq_len, heads * HD), jnp.bfloat16),
        scratch_shapes=[
            pltpu.VMEM((unit, seq_len, keys_all), jnp.float32),
            pltpu.VMEM((unit, seq_len, keys_all), jnp.bfloat16),
            pltpu.VMEM((unit, seq_len, HD), jnp.float32),
            pltpu.VMEM((unit, seq_len, 2 * HD), jnp.float32),
        ],
        compiler_params=pltpu.CompilerParams(vmem_limit_bytes=51 * 1024 * 1024),
        cost_estimate=pl.CostEstimate(
            flops=heads * seq_len * keys_all * HD * 6,
            bytes_accessed=2 * seq_len * HD * (2 * heads + 2 * BLOCKS),
            transcendentals=heads * seq_len * keys_all,
        ),
        name="attend",
    )(where, slot_bias, queries, *kv_blocks)


def project_kernel(parts, start, final, place_ref, weight_ref, *refs):
    buffers = refs[: sum(len(kinds) for kinds, _ in parts)]
    total_ref = None if start else refs[len(buffers)]
    out_ref, left_ref, right_ref, held_ref, made_ref, left_sems, right_sems, total_sems, out_sems = refs[-9:]
    steps, _, step = right_ref.shape
    place = place_ref[0]

    def tile(ref, at):
        return ref.at[0, :, pl.ds(at * step, step)] if final else ref.at[at]

    def sources():
        taken = first = 0
        for index, (kinds, rows) in enumerate(parts):
            width = sum(count for _, count in rows)
            target = left_ref.at[:, pl.ds(first, width)]
            found = [
                (
                    kinds[other],
                    functools.partial(
                        pltpu.make_async_copy, buffers[taken + other], target, left_sems.at[index]
                    ),
                )
                for other in range(len(kinds))
            ]
            yield found
            taken += len(kinds)
            first += width

    def weights(at):
        found, first = [], 0
        for _, rows in parts:
            for row, count in rows:
                found.append(
                    pltpu.make_async_copy(
                        weight_ref.at[pl.ds(pl.multiple_of(row(place), HD), count), pl.ds(at * step, step)],
                        right_ref.at[at, pl.ds(first, count), :],
                        right_sems.at[at, len(found)],
                    )
                )
                first += count
        return found

    def totals(at):
        return [] if start else [pltpu.make_async_copy(total_ref.at[at], held_ref.at[at], total_sems.at[at])]

    for found in sources():
        for places, make in found:
            if len(found) == 1:
                make().start()
            else:
                wanted = functools.reduce(jnp.logical_or, [place == at for at in places])
                pl.when(wanted)(lambda make=make: make().start())
    for at in range(steps):
        for copy in weights(at) + totals(at):
            copy.start()
    for found in sources():
        found[0][1]().wait()
    leaving = []
    for at in range(steps):
        for copy in weights(at) + totals(at):
            copy.wait()
        total = jnp.dot(left_ref[...], right_ref[at], preferred_element_type=jnp.float32)
        if not start:
            total = total + held_ref[at]
        made_ref[at] = total.astype(made_ref.dtype)
        leaving.append(pltpu.make_async_copy(made_ref.at[at], tile(out_ref, at), out_sems.at[at]))
        leaving[at].start()
    for copy in leaving:
        copy.wait()


def project(place, total, parts, weight, final):
    seq_len = parts[0][0][0][0].shape[0]
    out_width = weight.shape[1]
    step = min(out_width, 512)
    steps = out_width // step
    operands, kinds = [weight], []
    depth = runs = 0
    for buffers, rows in parts:
        kinds.append((tuple(tuple(places) for _, places in buffers), tuple(rows)))
        operands += [buffer for buffer, _ in buffers]
        depth += sum(count for _, count in rows)
        runs += len(rows)
    if total is not None:
        operands.append(total)
    there = pl.BlockSpec(memory_space=pl.ANY)
    if final:
        out_shape = jax.ShapeDtypeStruct((1, seq_len, out_width), jnp.bfloat16)
    else:
        out_shape = jax.ShapeDtypeStruct((steps, seq_len, step), jnp.float32)
    return pl.pallas_call(
        functools.partial(project_kernel, tuple(kinds), total is None, final),
        in_specs=[pl.BlockSpec(memory_space=pltpu.SMEM)] + [there] * len(operands),
        out_specs=there,
        out_shape=out_shape,
        scratch_shapes=[
            pltpu.VMEM((seq_len, depth), jnp.bfloat16),
            pltpu.VMEM((steps, depth, step), weight.dtype),
            pltpu.VMEM((1 if total is None else steps, seq_len, step), jnp.float32),
            pltpu.VMEM((steps, seq_len, step), out_shape.dtype),
            pltpu.SemaphoreType.DMA((len(parts),)),
            pltpu.SemaphoreType.DMA((steps, runs)),
            pltpu.SemaphoreType.DMA((steps,)),
            pltpu.SemaphoreType.DMA((steps,)),
        ],
        compiler_params=pltpu.CompilerParams(vmem_limit_bytes=(46 if depth <= 4 * HD else 52) * 1024 * 1024),
        cost_estimate=pl.CostEstimate(
            flops=2 * seq_len * depth * out_width,
            bytes_accessed=2 * depth * (seq_len + out_width) + 8 * seq_len * out_width,
            transcendentals=0,
        ),
        name="project",
    )(place, *operands)


def along_line(value, pairs):
    return lax.ppermute(value, "mp", pairs)


def on_device(queries, keys, values, out_weight, order_bias, partners, count, order):
    heads_dev = queries.shape[2] // HD
    group_size = HQ // KVH
    resp_total = lax.axis_size("resp")
    mp_total = lax.axis_size("mp")
    line = lax.axis_index("mp")
    first_head = line * heads_dev
    kv_head = (first_head // group_size).astype(jnp.int32)
    packed = pack(kv_head.reshape(1), keys, values)
    kv_blocks = gather_blocks(packed)
    resp_self = lax.axis_index("resp").astype(jnp.int32).reshape(1)
    where = jnp.concatenate([resp_self, count, partners[0]])
    bias_dev = lax.dynamic_slice_in_dim(order_bias, first_head, heads_dev, 1)
    slot_bias = jnp.where(order[0][:, None] == 1, bias_dev[1][None, :], bias_dev[0][None, :])
    place = line.astype(jnp.int32).reshape(1)

    def held_until(value, *after):
        return lax.optimization_barrier((value,) + after)[0]

    def attended_of(head_base, heads, *after):
        return attention(
            held_until(where, *after), slot_bias, queries, kv_blocks, head_base, heads, resp_total
        )

    def add(total, parts, final, *after):
        return project(held_until(place, *after), total, parts, out_weight, final)

    device_rows = heads_dev * HD
    if mp_total != 4 or heads_dev % 4:
        pieces = [attended_of(head, 1) for head in range(heads_dev)]
        gathered = lax.all_gather(jnp.concatenate(pieces, axis=1), "mp", axis=0, tiled=False)
        parts = [
            ([(gathered[source], ())], [(lambda at, source=source: source * device_rows, device_rows)])
            for source in range(mp_total)
        ]
        return add(None, parts, True)

    chunks = 4
    chunk_heads = heads_dev // chunks
    rows = chunk_heads * HD
    inner, outer = (1, 2), (0, 3)
    straight = (0, 1)
    own, pair, middle, second, near_out, far_out = [], [], [], [], [], []

    def attend_chunk(*after):
        chunk = len(own)
        own.append(attended_of(chunk * chunk_heads, chunk_heads, *after))
        pair.append(along_line(own[chunk], [(0, 1), (1, 0), (2, 3), (3, 2)]))
        middle.append(along_line(own[chunk], [(1, 2), (2, 1)]))
        if chunk in straight:
            second.append(along_line(own[chunk], [(0, 2), (2, 0), (1, 3), (3, 1)]))
            near_out.append(second[chunk])
        else:
            second.append(along_line(own[chunk], [(0, 2), (3, 1)]))

    def forward(held):
        return along_line(held, [(1, 0), (2, 3)])

    def run_of(source, chunk):
        return [(lambda at: source(at) * device_rows + chunk * rows, rows)]

    def own_part(chunk):
        return ([(own[chunk], ())], run_of(lambda at: at, chunk))

    def pair_part(chunk):
        return ([(pair[chunk], ())], run_of(lambda at: at ^ 1, chunk))

    def near_part(chunk):
        row = run_of(lambda at: jnp.where(at < 2, 2, 1), chunk)
        return ([(middle[chunk], inner), (near_out[chunk], outer)], row)

    def far_part(chunk):
        row = run_of(lambda at: jnp.where(at < 2, 3, 0), chunk)
        return ([(second[chunk], inner), (far_out[chunk], outer)], row)

    attend_chunk()
    attend_chunk()
    attend_chunk(pair[0])
    far_out.append(forward(held_until(second[0], own[2])))
    attend_chunk(second[0], middle[0], pair[1])
    far_out.append(forward(held_until(second[1], own[3])))
    parts = [own_part(chunk) for chunk in range(4)] + [pair_part(chunk) for chunk in range(3)]
    total = add(None, parts, False, second[1], middle[1], middle[2], far_out[0])
    near_out.append(forward(held_until(middle[2], total)))
    far_out.append(forward(held_until(second[2], total)))
    parts = [pair_part(3), near_part(0), near_part(1), far_part(0), far_part(1)]
    total = add(total, parts, False, middle[3], second[2])
    near_out.append(forward(held_until(middle[3], total)))
    far_out.append(forward(held_until(second[3], total)))
    total = add(total, [near_part(2), far_part(2)], False, second[3], middle[3])
    return add(total, [near_part(3), far_part(3)], True)


def solution(mesh):
    in_specs = (
        P("resp", None, "mp"),
        P("resp", None, None),
        P("resp", None, None),
        P(None, "mp"),
        P(),
        P("resp", None),
        P("resp"),
        P("resp", None),
    )
    out_specs = P("resp", None, "mp")
    return jax.shard_map(
        on_device, mesh=mesh, in_specs=in_specs, out_specs=out_specs, check_vma=False
    )
```
